256 devices in a mesh: kgrp: 8 (over x, y_hi), atom: 32 (over y_lo, z, core).
Axes of the slice: x: 4, y: 4 (y_hi: 2, y_lo: 2; y = y_hi * 2 + y_lo), z: 8, core: 2. Of those that a mesh axis runs over, the one named last changes fastest.
Arguments:
- atomic_descriptors: bfloat16 [65536, 128], P('atom'), may hold values from -6 to 6
- unit_cell_coordinates: float32 [3, 65536], P(None, 'atom'), may hold values from 0 to 1
- element_labels: int32 [65536], P('atom'), may hold values from 0 to 5
- lattice_momenta: int32 [3, 4096], P(None, 'kgrp'), may hold values from -8 to 8
- feature_to_latent_matrix: bfloat16 [2, 128, 128], replicated, may hold values from -0.5 to 0.5
- latent_to_feature_matrix: bfloat16 [2, 128, 128], replicated, may hold values from -0.5 to 0.5
- element_latent_multiplier: float32 [2, 6, 128], replicated, may hold values from 0.5 to 2
- upstream_gradient: bfloat16 [65536, 128], P('atom'), may hold values from -6 to 6
Outputs:
- grad_features: bfloat16 [65536, 128], P(('atom', 'kgrp'))
- grad_positions: float32 [3, 65536], P(None, ('atom', 'kgrp'))
The draws below stay inside these ranges and needn't reach their ends.
All inputs are finite; a program needn't handle non-finite values.
Results may differ from the reference program's by a relative error of at most 0.014.
Values may be sent and summed in bfloat16 or wider, within the bound.
No kernel may reach another device: no remote copies, remote signals or barrier semaphores. Data moves between devices by JAX's collectives and lax.ppermute only.
A program may use at most 128 MiB of HBM per device.

```python
import math
import jax
import jax.numpy as jnp
from jax import lax

D = 128
C = 128
NSPEC = 6
GROUP_KSPACE_SUM = 512
TOTAL_KSPACE_NUM = 4096
ATOMS = 65536


def set_ends(drawn, key, smallest, largest):
    index_at = [jax.random.randint(jax.random.fold_in(key, axis), (), 0, length) for axis, length in enumerate(drawn.shape)]
    main_axis = drawn.shape.index(max(drawn.shape))
    neighbour = index_at[:main_axis] + [(index_at[main_axis] + 1) % drawn.shape[main_axis]] + index_at[main_axis + 1:]
    return drawn.at[tuple(index_at)].set(smallest).at[tuple(neighbour)].set(largest)


def shard_levels(own_key, shape, pieces, low, top_value):
    def one(position, blocks):
        steps = jax.random.uniform(jax.random.fold_in(jax.random.fold_in(own_key, 6), position), (blocks,), jnp.float32, low / len(pieces), top_value / len(pieces))
        return jnp.repeat(jnp.exp(steps), shape[position] // blocks).reshape((-1,) + (1,) * (len(shape) - position - 1))

    level = one(*pieces[0])
    for cut in pieces[1:]:
        level = level * one(*cut)
    return level


def gaussian(rng, extent, width, reach, shards=(), kind=jnp.bfloat16):
    values = width * jax.random.normal(rng, extent, jnp.float32)
    if shards:
        values = values * shard_levels(rng, extent, shards, -0.22, 0.18)
    return jnp.clip(values, -reach, reach).astype(kind)


def setup_inputs(seed: int = 0) -> dict:
    seeds = jax.random.split(jax.random.key(seed), 9)
    atomic_descriptors = gaussian(seeds[0], (ATOMS, D), 1.0, 6.0, ((0, 32),))
    unit_cell_coordinates = jnp.clip(1.0 * jax.random.uniform(seeds[1], (3, ATOMS), jnp.float32) ** shard_levels(seeds[1], (3, ATOMS), ((1, 32),), -0.2, 0.2), 0.0, 1.0)
    element_labels = set_ends(jax.random.randint(seeds[2], (ATOMS,), 0, NSPEC), jax.random.fold_in(seeds[2], 1), 0, NSPEC - 1).astype(jnp.int32)
    lattice_momenta = set_ends(jax.random.randint(seeds[3], (3, TOTAL_KSPACE_NUM), -8, 9), jax.random.fold_in(seeds[3], 1), -8, 8).astype(jnp.int32)
    feature_to_latent_matrix = gaussian(seeds[4], (2, D, C), D ** -0.5, 0.5)
    latent_to_feature_matrix = gaussian(seeds[5], (2, C, D), C ** -0.5, 0.5)
    element_latent_multiplier = jnp.clip(jnp.exp(jax.random.uniform(seeds[6], (2, NSPEC, C), jnp.float32, math.log(0.5), math.log(2.0))), 0.5, 2.0)
    upstream_gradient = gaussian(seeds[7], (ATOMS, D), 1.0, 6.0, ((0, 32),))
    return dict(atomic_descriptors=atomic_descriptors, unit_cell_coordinates=unit_cell_coordinates, element_labels=element_labels, lattice_momenta=lattice_momenta, feature_to_latent_matrix=feature_to_latent_matrix, latent_to_feature_matrix=latent_to_feature_matrix, element_latent_multiplier=element_latent_multiplier, upstream_gradient=upstream_gradient)


TWO_PI = 2.0 * math.pi
BOX_LENGTH = 100.0
GAUSSIAN_SIGMAS = (200.0, 100.0)

def trigonometric_lookup(unit_cell_coordinates, kblock):
    kfloat = kblock.astype(jnp.float32)
    theta = TWO_PI * (unit_cell_coordinates[0][:, None] * kfloat[0][None, :] + unit_cell_coordinates[1][:, None] * kfloat[1][None, :] + unit_cell_coordinates[2][:, None] * kfloat[2][None, :])
    return (jnp.cos(theta), jnp.sin(theta))

def green_function_coefficients(kblock, spread, green_function_prefactor):
    kfloat = kblock.astype(jnp.float32)
    return green_function_prefactor * jnp.exp(-lax.optimization_barrier(jnp.sum(kfloat * kfloat, axis=0)) / spread)

def contract_rows(table, values):
    return lax.dot_general(table, values, (((0,), (0,)), ((), ())), preferred_element_type=jnp.float32)

def contract_cols(left, right, precision=None):
    return lax.dot_general(left, right, (((1,), (1,)), ((), ())), preferred_element_type=jnp.float32, precision=precision)

def make_charges(feats, weight_in, gain_rows):
    return (jnp.dot(feats, weight_in, preferred_element_type=jnp.float32) * gain_rows).astype(jnp.bfloat16)

def theta_grad(structure_factor_real, structure_factor_imaginary, grad_pot, charges, field_re, field_im, grad_re, grad_im, kblock):
    along_re = contract_cols(grad_pot, field_re) + contract_cols(charges, grad_re)
    along_im = contract_cols(grad_pot, field_im) + contract_cols(charges, grad_im)
    gtheta = structure_factor_real * along_im - structure_factor_imaginary * along_re
    kfloat = kblock.astype(jnp.float32)
    return TWO_PI / BOX_LENGTH * contract_cols(kfloat, gtheta, lax.Precision.HIGHEST)

def reference(atomic_descriptors, unit_cell_coordinates, element_labels, lattice_momenta, feature_to_latent_matrix, latent_to_feature_matrix, element_latent_multiplier, upstream_gradient):
    number_of_layers = TOTAL_KSPACE_NUM // GROUP_KSPACE_SUM
    longrange_layers = lattice_momenta.reshape(3, number_of_layers, GROUP_KSPACE_SUM).transpose(1, 0, 2)
    green_function_prefactor = 1.0 / math.sqrt(ATOMS * TOTAL_KSPACE_NUM)
    onehot = (element_labels[:, None] == jnp.arange(NSPEC, dtype=jnp.int32)[None, :]).astype(jnp.float32)
    gains_one = jnp.dot(onehot, element_latent_multiplier[0], precision=lax.Precision.HIGHEST)
    gains_two = jnp.dot(onehot, element_latent_multiplier[1], precision=lax.Precision.HIGHEST)

    def fields(values, spread):

        def per_block(kblock):
            structure_factor_real, structure_factor_imaginary = trigonometric_lookup(unit_cell_coordinates, kblock)
            weights = green_function_coefficients(kblock, spread, green_function_prefactor)
            real_part = contract_rows(structure_factor_real.astype(jnp.bfloat16), values)
            imag_part = contract_rows(structure_factor_imaginary.astype(jnp.bfloat16), values)
            return ((weights[:, None] * real_part).astype(jnp.bfloat16), (weights[:, None] * imag_part).astype(jnp.bfloat16))
        return lax.map(per_block, longrange_layers)

    def potential(field_re, field_im):

        def advance(running, entry):
            kblock, part_re, part_im = entry
            structure_factor_real, structure_factor_imaginary = trigonometric_lookup(unit_cell_coordinates, kblock)
            running = running + jnp.dot(structure_factor_real.astype(jnp.bfloat16), part_re, preferred_element_type=jnp.float32)
            running = running + jnp.dot(structure_factor_imaginary.astype(jnp.bfloat16), part_im, preferred_element_type=jnp.float32)
            return (running, None)
        running, _ = lax.scan(advance, jnp.zeros((ATOMS, C), jnp.float32), (longrange_layers, field_re, field_im))
        return running

    def backward(grad_pot, charges, field_re, field_im, spread):
        grad_re, grad_im = fields(grad_pot, spread)

        def advance(carried, entry):
            grad_charge, grad_pos = carried
            kblock, part_re, part_im, gpart_re, gpart_im = entry
            structure_factor_real, structure_factor_imaginary = trigonometric_lookup(unit_cell_coordinates, kblock)
            grad_charge = grad_charge + jnp.dot(structure_factor_real.astype(jnp.bfloat16), gpart_re, preferred_element_type=jnp.float32)
            grad_charge = grad_charge + jnp.dot(structure_factor_imaginary.astype(jnp.bfloat16), gpart_im, preferred_element_type=jnp.float32)
            grad_pos = grad_pos + theta_grad(structure_factor_real, structure_factor_imaginary, grad_pot, charges, part_re, part_im, gpart_re, gpart_im, kblock)
            return ((grad_charge, grad_pos), None)
        start = (jnp.zeros((ATOMS, C), jnp.float32), jnp.zeros((3, ATOMS), jnp.float32))
        (grad_charge, grad_pos), _ = lax.scan(advance, start, (longrange_layers, field_re, field_im, grad_re, grad_im))
        return (grad_charge, grad_pos)
    charges_one = make_charges(atomic_descriptors, feature_to_latent_matrix[0], gains_one)
    field_one_re, field_one_im = fields(charges_one, GAUSSIAN_SIGMAS[0])
    potential_one = potential(field_one_re, field_one_im).astype(jnp.bfloat16)
    hidden = (atomic_descriptors.astype(jnp.float32) + jnp.dot(potential_one, latent_to_feature_matrix[0], preferred_element_type=jnp.float32)).astype(jnp.bfloat16)
    charges_two = make_charges(hidden, feature_to_latent_matrix[1], gains_two)
    field_two_re, field_two_im = fields(charges_two, GAUSSIAN_SIGMAS[1])
    grad_pot_two = jnp.dot(upstream_gradient, latent_to_feature_matrix[1].T, preferred_element_type=jnp.float32).astype(jnp.bfloat16)
    grad_charge_two, pos_two = backward(grad_pot_two, charges_two, field_two_re, field_two_im, GAUSSIAN_SIGMAS[1])
    scaled_two = (grad_charge_two * gains_two).astype(jnp.bfloat16)
    grad_hidden = (upstream_gradient.astype(jnp.float32) + jnp.dot(scaled_two, feature_to_latent_matrix[1].T, preferred_element_type=jnp.float32)).astype(jnp.bfloat16)
    grad_pot_one = jnp.dot(grad_hidden, latent_to_feature_matrix[0].T, preferred_element_type=jnp.float32).astype(jnp.bfloat16)
    grad_charge_one, pos_one = backward(grad_pot_one, charges_one, field_one_re, field_one_im, GAUSSIAN_SIGMAS[0])
    scaled_one = (grad_charge_one * gains_one).astype(jnp.bfloat16)
    grad_features = (grad_hidden.astype(jnp.float32) + jnp.dot(scaled_one, feature_to_latent_matrix[0].T, preferred_element_type=jnp.float32)).astype(jnp.bfloat16)
    return (grad_features, pos_one + pos_two)
```

```python
import functools
import math

import jax
import jax.numpy as jnp
import numpy as np
from jax import lax
from jax.experimental import pallas as pl
from jax.experimental.pallas import tpu as pltpu
from jax.sharding import Mesh
from jax.sharding import PartitionSpec as P

BOX_LENGTH = 100.0
GAUSSIAN_SIGMAS = (200.0, 100.0)
REACH = 8
SPAN = 2 * REACH + 1
CLASSES = (SPAN**3 + 1) // 2
SLABS = 4
SLAB = 640
TABLE = 2 * SLAB
BLOCK = 256
CHANNELS = 128
ROWS = 40
PIECES = 32
VMEM_LIMIT = 48 * 1024 * 1024
BF16 = jnp.bfloat16
F32 = jnp.float32

COS_SERIES = (
    0.999999995487496,
    -19.739205575083908,
    64.93915835436466,
    -85.45075924609554,
    60.172044623035546,
    -25.982406908145567,
    6.5475440523380986,
)
SIN_SERIES = (
    6.283185281044049,
    -41.34169782356279,
    81.60504596930859,
    -76.70182055142223,
    42.01785583003898,
    -14.873772878742722,
    3.2058159421849517,
)


def class_vectors():
    label = np.arange(SLABS * SLAB)
    label = np.where(label < CLASSES, label, 0)
    first = (label + (SPAN * SPAN) // 2) // (SPAN * SPAN)
    rest = label - SPAN * SPAN * first + (SPAN * SPAN) // 2
    second = rest // SPAN - REACH
    third = rest % SPAN - REACH
    table = np.zeros((SLABS * SLAB, CHANNELS), np.float32)
    table[:, 0], table[:, 1], table[:, 2] = first, second, third
    return table


def matmul(left, right, left_dim, right_dim):
    return lax.dot_general(
        left, right, (((left_dim,), (right_dim,)), ((), ())), preferred_element_type=F32
    )


def flip(matrix):
    return jnp.transpose(matrix.astype(F32)).astype(BF16)


def gain_columns(multiplier, labels):
    result = jnp.zeros((multiplier.shape[0], labels.shape[1]), F32)
    for species in range(multiplier.shape[1]):
        result = jnp.where(labels == species, multiplier[:, species : species + 1], result)
    return result


def series(coefficients, square):
    result = coefficients[-1] * square + coefficients[-2]
    for coefficient in coefficients[-3::-1]:
        result = result * square + coefficient
    return result


def write_pieces(place, total_ref, keep_ref, send_ref):
    core = place[2]
    for target, half in ((keep_ref, core), (send_ref, 1 - core)):
        for index in range(PIECES):
            row, side = index // 2, index % 2
            start = pl.multiple_of(half * SLAB + row * ROWS, 8)
            target[index] = total_ref[
                pl.ds(start, ROWS), side * CHANNELS : (side + 1) * CHANNELS
            ].astype(BF16)


def read_pieces(place, mine_ref, other_ref, total_ref):
    core = place[2]
    for source, half in ((mine_ref, core), (other_ref, 1 - core)):
        for index in range(PIECES):
            row, side = index // 2, index % 2
            start = pl.multiple_of(half * SLAB + row * ROWS, 8)
            total_ref[pl.ds(start, ROWS), side * CHANNELS : (side + 1) * CHANNELS] = source[
                index
            ].astype(F32)


def tables_kernel(
    place,
    vectors_ref,
    coordinates_ref,
    labels_ref,
    features_ref,
    upstream_ref,
    inward_ref,
    outward_ref,
    multiplier_ref,
    table_ref,
    values_ref,
    keep_ref,
    send_ref,
    total_ref,
):
    step = pl.program_id(0)
    along = [coordinates_ref[axis : axis + 1, :] for axis in range(3)]
    chunk = 64
    for start in range(0, SLAB, chunk):
        rows = pl.ds(start, chunk)
        turns = vectors_ref[rows, 0:1] * along[0]
        turns += vectors_ref[rows, 1:2] * along[1]
        turns += vectors_ref[rows, 2:3] * along[2]
        turns -= jnp.floor(turns + 0.5)
        square = turns * turns
        table_ref[0, rows, :] = series(COS_SERIES, square).astype(BF16)
        table_ref[0, pl.ds(SLAB + start, chunk), :] = (
            turns * series(SIN_SERIES, square)
        ).astype(BF16)
    gains = gain_columns(multiplier_ref[0], labels_ref[...])
    charges = matmul(flip(inward_ref[0]), features_ref[...], 1, 1) * gains
    grad_pot = matmul(outward_ref[1], upstream_ref[...], 1, 1)
    values = jnp.concatenate([charges, grad_pot], axis=0).astype(BF16)
    values_ref[0] = values
    part = matmul(table_ref[0], values, 1, 1)

    @pl.when(step == 0)
    def _():
        total_ref[...] = part

    @pl.when(step != 0)
    def _():
        total_ref[...] += part

    @pl.when(step == pl.num_programs(0) - 1)
    def _():
        write_pieces(place, total_ref, keep_ref, send_ref)


def weights_kernel(prefactor, place, vectors_ref, classes_ref, weights_ref):
    chunk = 128
    for start in range(0, SLAB, chunk):
        rows = pl.ds(start, chunk)
        own = lax.broadcasted_iota(jnp.int32, (chunk, CHANNELS), 0) + (place[0] * SLAB + start)
        count = jnp.zeros((chunk, CHANNELS), F32)
        for group in range(classes_ref.shape[0]):
            for offset in range(0, classes_ref.shape[1], CHANNELS):
                classes = classes_ref[group : group + 1, offset : offset + CHANNELS]
                count += jnp.where(classes == own, 1.0, 0.0)
        count = jnp.sum(count, axis=1, keepdims=True)
        vectors = vectors_ref[rows, :]
        norm = jnp.sum(vectors * vectors, axis=1, keepdims=True)
        for block, spread in enumerate(GAUSSIAN_SIGMAS):
            weight = count * (prefactor * jnp.exp(norm * (-1.0 / spread)))
            weights_ref[block, rows, :] = jnp.broadcast_to(weight, (chunk, CHANNELS))


def potential_kernel(
    place, weights_ref, mine_ref, other_ref, table_ref, fields_ref, p0, p1, p2, p3, total_ref, flipped_ref
):
    step = pl.program_id(0)

    @pl.when(step == 0)
    def _():
        read_pieces(place, mine_ref, other_ref, total_ref)
        for half in range(2):
            rows = pl.ds(half * SLAB, SLAB)
            for side in range(2):
                columns = pl.ds(side * CHANNELS, CHANNELS)
                total_ref[rows, columns] = total_ref[rows, columns] * weights_ref[side]
        fields_ref[...] = total_ref[...].astype(BF16)
        flipped_ref[...] = jnp.transpose(total_ref[...]).astype(BF16)

    product = matmul(flipped_ref[...], table_ref[0], 1, 0).astype(BF16)
    for index, target in enumerate((p0, p1, p2, p3)):

        @pl.when(step == index)
        def _():
            target[...] = product


def middle_kernel(
    place,
    q0,
    q1,
    q2,
    q3,
    labels_ref,
    features_ref,
    upstream_ref,
    inward_ref,
    outward_ref,
    multiplier_ref,
    values_ref,
    hidden_grad_ref,
):
    total = (q0[...].astype(F32) + q1[...].astype(F32)) + (q2[...].astype(F32) + q3[...].astype(F32))
    potential = total[:CHANNELS].astype(BF16)
    grad_charge = total[CHANNELS:]
    gains = gain_columns(multiplier_ref[1], labels_ref[...])
    hidden = (
        features_ref[...].astype(F32)
        + matmul(jnp.transpose(potential.astype(F32)).astype(BF16), outward_ref[0], 1, 0)
    ).astype(BF16)
    inward_flipped = flip(inward_ref[1])
    charges = matmul(inward_flipped, hidden, 1, 1) * gains
    scaled = jnp.transpose(grad_charge * gains).astype(BF16)
    hidden_grad = (
        upstream_ref[...].astype(F32) + matmul(scaled, inward_flipped, 1, 0)
    ).astype(BF16)
    hidden_grad_ref[...] = hidden_grad
    grad_pot = matmul(outward_ref[0], hidden_grad, 1, 1)
    values_ref[...] = jnp.concatenate([charges, grad_pot], axis=0).astype(BF16)


def second_kernel(place, table_ref, v0, v1, v2, v3, keep_ref, send_ref, total_ref):
    step = pl.program_id(0)
    for index, source in enumerate((v0, v1, v2, v3)):

        @pl.when(step == index)
        def _():
            part = matmul(table_ref[0], source[...], 1, 1)
            if index == 0:
                total_ref[...] = part
            else:
                total_ref[...] += part

    @pl.when(step == pl.num_programs(0) - 1)
    def _():
        write_pieces(place, total_ref, keep_ref, send_ref)


def gradient_kernel(
    place,
    weights_ref,
    mine_ref,
    other_ref,
    fields_ref,
    vectors_ref,
    table_ref,
    first_ref,
    v0,
    v1,
    v2,
    v3,
    o0,
    o1,
    o2,
    o3,
    total_ref,
    pairs_ref,
    flipped_ref,
    directions_ref,
    theta_ref,
    second_ref,
):
    step = pl.program_id(0)

    @pl.when(step == 0)
    def _():
        read_pieces(place, mine_ref, other_ref, total_ref)
        for half in range(2):
            rows = pl.ds(half * SLAB, SLAB)
            for side in range(2):
                columns = pl.ds(side * CHANNELS, CHANNELS)
                total_ref[rows, columns] = total_ref[rows, columns] * weights_ref[1 - side]
        field_two = total_ref[:, :CHANNELS].astype(BF16)
        grad_one = total_ref[:, CHANNELS:]
        pairs_ref[:, 0:CHANNELS] = grad_one.astype(BF16)
        pairs_ref[:, CHANNELS : 2 * CHANNELS] = field_two
        pairs_ref[:, 2 * CHANNELS : 3 * CHANNELS] = fields_ref[:, CHANNELS:]
        pairs_ref[:, 3 * CHANNELS :] = fields_ref[:, :CHANNELS]
        flipped_ref[...] = jnp.transpose(grad_one).astype(BF16)
        directions_ref[...] = jnp.transpose(vectors_ref[...])[:16].astype(BF16)

    for index, source in enumerate((v0, v1, v2, v3)):

        @pl.when(step == index)
        def _():
            second_ref[...] = source[...]

    values = jnp.concatenate([first_ref[0], second_ref[...]], axis=0)
    chunk = 128
    for start in range(0, SLAB, chunk):
        real = pl.ds(start, chunk)
        imag = pl.ds(SLAB + start, chunk)
        along_real = matmul(pairs_ref[real, :], values, 1, 0)
        along_imag = matmul(pairs_ref[imag, :], values, 1, 0)
        theta_ref[real, :] = (
            table_ref[0, real, :].astype(F32) * along_imag
            - table_ref[0, imag, :].astype(F32) * along_real
        ).astype(BF16)
    charge = matmul(flipped_ref[...], table_ref[0], 1, 0)
    position = matmul(directions_ref[...], theta_ref[...], 1, 0)
    result = jnp.concatenate([charge, position * (2.0 * math.pi / BOX_LENGTH)], axis=0).astype(BF16)
    for index, target in enumerate((o0, o1, o2, o3)):

        @pl.when(step == index)
        def _():
            target[...] = result


def final_kernel(
    place, q0, q1, q2, q3, labels_ref, hidden_grad_ref, inward_ref, multiplier_ref, features_ref, positions_ref
):
    total = (q0[...].astype(F32) + q1[...].astype(F32)) + (q2[...].astype(F32) + q3[...].astype(F32))
    gains = gain_columns(multiplier_ref[0], labels_ref[...])
    scaled = jnp.transpose(total[:CHANNELS] * gains).astype(BF16)
    features_ref[...] = (
        hidden_grad_ref[...].astype(F32) + matmul(scaled, flip(inward_ref[0]), 1, 0)
    ).astype(BF16)
    positions_ref[...] = total[CHANNELS : CHANNELS + 3]


def shape_of(shape, dtype):
    return jax.ShapeDtypeStruct(shape, dtype)


def whole(shape):
    return pl.BlockSpec(shape, lambda step, place: (0,) * len(shape))


def call(kernel, steps, in_specs, outs, out_specs, scratch, operands):
    return pl.pallas_call(
        kernel,
        grid_spec=pltpu.PrefetchScalarGridSpec(
            num_scalar_prefetch=1,
            grid=(steps,),
            in_specs=in_specs,
            out_specs=out_specs,
            scratch_shapes=scratch,
        ),
        out_shape=outs,
        compiler_params=pltpu.CompilerParams(
            dimension_semantics=("arbitrary",), vmem_limit_bytes=VMEM_LIMIT
        ),
    )(*operands)


ATOM_REST = ("yh", "yl", "z")


def shifted(value, shift):
    return lax.ppermute(value, "x", [(i, (i + shift) % SLABS) for i in range(SLABS)])


def swapped(value):
    return lax.ppermute(value, "core", [(0, 1), (1, 0)])


def sum_fields(keep, send):
    part = (keep.astype(F32) + swapped(send).astype(F32)).astype(BF16)
    parts = lax.all_to_all(part, ATOM_REST, 0, 0, tiled=True)
    total = jnp.sum(parts.astype(F32), axis=0).astype(BF16)
    spread = jnp.broadcast_to(total[None], (PIECES,) + total.shape)
    mine = lax.all_to_all(spread, ATOM_REST, 0, 0, tiled=True)
    return mine, swapped(mine)


def per_device(
    atomic_descriptors,
    unit_cell_coordinates,
    element_labels,
    lattice_momenta,
    feature_to_latent_matrix,
    latent_to_feature_matrix,
    element_latent_multiplier,
    upstream_gradient,
):
    place = jnp.stack(
        [lax.axis_index("x"), lax.axis_index("yh"), lax.axis_index("core")]
    ).astype(jnp.int32)
    prefactor = 1.0 / math.sqrt(
        atomic_descriptors.shape[0]
        * lattice_momenta.shape[1]
        * lax.axis_size(("x", "yh", "yl", "z", "core"))
    )
    labels = element_labels[None, :]
    multiplier = jnp.swapaxes(element_latent_multiplier, 1, 2)
    species = multiplier.shape[2]
    vectors = jnp.asarray(class_vectors())
    signed = (
        lattice_momenta[0] * (SPAN * SPAN) + lattice_momenta[1] * SPAN + lattice_momenta[2]
    )
    classes = lax.all_gather(jnp.abs(signed)[None], ("x", "yh"), axis=0, tiled=True)

    slab = pl.BlockSpec((SLAB, CHANNELS), lambda step, place: (place[0], 0))
    own_slab = slab
    matrices = whole((2, CHANNELS, CHANNELS))
    gains_spec = whole((2, CHANNELS, species))
    pieces_spec = whole((PIECES, ROWS, CHANNELS))
    pieces_shape = shape_of((PIECES, ROWS, CHANNELS), BF16)
    values_block = whole((BLOCK, BLOCK))
    values_shape = shape_of((BLOCK, BLOCK), BF16)
    table_shape = shape_of((SLABS, TABLE, BLOCK), BF16)

    def rotated(shape, sign):
        return pl.BlockSpec(
            (1,) + shape, lambda step, place: ((place[0] + sign * step + SLABS) % SLABS, 0, 0)
        )

    table, values_one, keep, send = call(
        tables_kernel,
        SLABS,
        [
            slab,
            pl.BlockSpec((3, BLOCK), lambda step, place: (0, 2 * step + place[1])),
            pl.BlockSpec((1, BLOCK), lambda step, place: (0, 2 * step + place[1])),
            pl.BlockSpec((BLOCK, CHANNELS), lambda step, place: (2 * step + place[1], 0)),
            pl.BlockSpec((BLOCK, CHANNELS), lambda step, place: (2 * step + place[1], 0)),
            matrices,
            matrices,
            gains_spec,
        ],
        (table_shape, shape_of((SLABS, BLOCK, BLOCK), BF16), pieces_shape, pieces_shape),
        (
            pl.BlockSpec((1, TABLE, BLOCK), lambda step, place: (step, 0, 0)),
            pl.BlockSpec((1, BLOCK, BLOCK), lambda step, place: (step, 0, 0)),
            pieces_spec,
            pieces_spec,
        ),
        [pltpu.VMEM((TABLE, BLOCK), F32)],
        (
            place,
            vectors,
            unit_cell_coordinates,
            labels,
            atomic_descriptors,
            upstream_gradient,
            feature_to_latent_matrix,
            latent_to_feature_matrix,
            multiplier,
        ),
    )
    weights = call(
        functools.partial(weights_kernel, prefactor),
        1,
        [own_slab, whole(classes.shape)],
        shape_of((2, SLAB, CHANNELS), F32),
        whole((2, SLAB, CHANNELS)),
        [],
        (place, vectors, classes),
    )
    mine, other = sum_fields(keep, send)
    fields, *products = call(
        potential_kernel,
        SLABS,
        [whole((2, SLAB, CHANNELS)), pieces_spec, pieces_spec, rotated((TABLE, BLOCK), 1)],
        (shape_of((TABLE, BLOCK), BF16),) + (values_shape,) * SLABS,
        (whole((TABLE, BLOCK)),) + (values_block,) * SLABS,
        [pltpu.VMEM((TABLE, BLOCK), F32), pltpu.VMEM((BLOCK, TABLE), BF16)],
        (place, weights, mine, other, table),
    )
    arrived = [products[0]] + [shifted(products[shift], shift) for shift in range(1, SLABS)]
    own_atoms = pl.BlockSpec((BLOCK, CHANNELS), lambda step, place: (2 * place[0] + place[1], 0))
    own_labels = pl.BlockSpec((1, BLOCK), lambda step, place: (0, 2 * place[0] + place[1]))
    values_two, hidden_grad = call(
        middle_kernel,
        1,
        [values_block] * SLABS
        + [own_labels, own_atoms, own_atoms, matrices, matrices, gains_spec],
        (values_shape, shape_of((BLOCK, CHANNELS), BF16)),
        (values_block, whole((BLOCK, CHANNELS))),
        [],
        (
            place,
            *arrived,
            labels,
            atomic_descriptors,
            upstream_gradient,
            feature_to_latent_matrix,
            latent_to_feature_matrix,
            multiplier,
        ),
    )
    seconds = [values_two] + [shifted(values_two, SLABS - slot) for slot in range(1, SLABS)]
    keep, send = call(
        second_kernel,
        SLABS,
        [rotated((TABLE, BLOCK), 1)] + [values_block] * SLABS,
        (pieces_shape, pieces_shape),
        (pieces_spec, pieces_spec),
        [pltpu.VMEM((TABLE, BLOCK), F32)],
        (place, table, *seconds),
    )
    mine, other = sum_fields(keep, send)
    result_shape = shape_of((CHANNELS + 16, BLOCK), BF16)
    result_spec = whole((CHANNELS + 16, BLOCK))
    results = call(
        gradient_kernel,
        SLABS,
        [
            whole((2, SLAB, CHANNELS)),
            pieces_spec,
            pieces_spec,
            whole((TABLE, BLOCK)),
            own_slab,
            rotated((TABLE, BLOCK), 1),
            rotated((BLOCK, BLOCK), 1),
        ]
        + [values_block] * SLABS,
        (result_shape,) * SLABS,
        (result_spec,) * SLABS,
        [
            pltpu.VMEM((TABLE, BLOCK), F32),
            pltpu.VMEM((TABLE, 2 * BLOCK), BF16),
            pltpu.VMEM((CHANNELS, TABLE), BF16),
            pltpu.VMEM((16, SLAB), BF16),
            pltpu.VMEM((SLAB, BLOCK), BF16),
            pltpu.VMEM((BLOCK, BLOCK), BF16),
        ],
        (place, weights, mine, other, fields, vectors, table, values_one, *seconds),
    )
    arrived = [results[0]] + [shifted(results[shift], shift) for shift in range(1, SLABS)]
    return call(
        final_kernel,
        1,
        [result_spec] * SLABS
        + [own_labels, whole((BLOCK, CHANNELS)), matrices, gains_spec],
        (shape_of((BLOCK, CHANNELS), BF16), shape_of((3, BLOCK), F32)),
        (whole((BLOCK, CHANNELS)), whole((3, BLOCK))),
        [],
        (place, *arrived, labels, hidden_grad, feature_to_latent_matrix, multiplier),
    )


def solution(mesh):
    fine = Mesh(mesh.devices.reshape(SLABS, 2, 2, -1, 2), ("x", "yh", "yl", "z", "core"))
    atom, group = ("yl", "z", "core"), ("x", "yh")
    in_specs = (
        P(atom, None),
        P(None, atom),
        P(atom),
        P(None, group),
        P(),
        P(),
        P(),
        P(atom, None),
    )
    out_specs = (P(atom + group, None), P(None, atom + group))
    return jax.shard_map(
        per_device, mesh=fine, in_specs=in_specs, out_specs=out_specs, check_vma=False
    )
```

```python
import functools
import math

import jax
import jax.numpy as jnp
from jax import lax
from jax.experimental import pallas as pl
from jax.experimental.pallas import tpu as pltpu
from jax.sharding import Mesh
from jax.sharding import PartitionSpec as P

BOX_LENGTH = 100.0
GAUSSIAN_SIGMAS = (200.0, 100.0)
REACH = 8
SPAN = 2 * REACH + 1
CLASSES = (SPAN**3 + 1) // 2
SLABS = 4
SLAB = 640
TABLE = 2 * SLAB
BLOCK = 256
CHANNELS = 128
ROWS = 40
PIECES = 32
VMEM_SHARED = 24 * 1024 * 1024
VMEM_ALL = 62 * 1024 * 1024
BF16 = jnp.bfloat16
F32 = jnp.float32

COS_SERIES = (
    0.999999660315462,
    -19.739032161520388,
    64.93001235415629,
    -85.28515888817482,
    58.84788533073816,
    -21.15810679384873,
)
SIN_SERIES = (
    6.283183359037432,
    -41.341456424111435,
    81.59687947501621,
    -76.58597187733577,
    41.22756686823296,
    -12.302134397179453,
)


def class_vectors(first_class, shape, axis):
    label = (lax.broadcasted_iota(jnp.int32, shape, axis) + first_class).astype(F32)
    square = SPAN * SPAN
    first = jnp.floor((label + (square // 2 + 0.5)) * (1.0 / square))
    rest = label - square * first
    second = jnp.floor((rest + (REACH + 0.5)) * (1.0 / SPAN))
    return first, second, rest - SPAN * second


def matmul(left, right, left_dim, right_dim):
    return lax.dot_general(
        left, right, (((left_dim,), (right_dim,)), ((), ())), preferred_element_type=F32
    )


def flip(matrix):
    return jnp.transpose(matrix.astype(F32)).astype(BF16)


def gain_columns(multiplier, labels):
    species_count, channels = multiplier.shape
    padding = jnp.zeros((8 - species_count, channels), F32)
    columns = jnp.transpose(jnp.concatenate([multiplier, padding], axis=0))
    result = jnp.zeros((channels, labels.shape[1]), F32)
    for species in range(species_count):
        result = jnp.where(labels == species, columns[:, species : species + 1], result)
    return result


def series(coefficients, square):
    result = coefficients[-1] * square + coefficients[-2]
    for coefficient in coefficients[-3::-1]:
        result = result * square + coefficient
    return result


def write_pieces(place, total_ref, keep_ref, send_ref):
    core = place[2]
    for target, half in ((keep_ref, core), (send_ref, 1 - core)):
        for index in range(PIECES):
            row, side = index // 2, index % 2
            start = pl.multiple_of(half * SLAB + row * ROWS, 8)
            target[index] = total_ref[
                pl.ds(start, ROWS), side * CHANNELS : (side + 1) * CHANNELS
            ].astype(BF16)


def read_pieces(place, mine_ref, other_ref, total_ref):
    core = place[2]
    for source, half in ((mine_ref, core), (other_ref, 1 - core)):
        for index in range(PIECES):
            row, side = index // 2, index % 2
            start = pl.multiple_of(half * SLAB + row * ROWS, 8)
            total_ref[pl.ds(start, ROWS), side * CHANNELS : (side + 1) * CHANNELS] = source[
                index
            ].astype(F32)


def tables_kernel(
    place,
    coordinates_ref,
    labels_ref,
    features_ref,
    upstream_ref,
    inward_ref,
    outward_ref,
    multiplier_ref,
    table_ref,
    values_ref,
    keep_ref,
    send_ref,
    total_ref,
):
    step = pl.program_id(0)
    chunk = 64
    for start in range(0, SLAB, chunk):
        rows = pl.ds(start, chunk)
        vectors = class_vectors(place[0] * SLAB + start, (chunk, CHANNELS), 0)
        for side in range(BLOCK // CHANNELS):
            columns = pl.ds(side * CHANNELS, CHANNELS)
            turns = vectors[0] * coordinates_ref[0:1, columns]
            turns += vectors[1] * coordinates_ref[1:2, columns]
            turns += vectors[2] * coordinates_ref[2:3, columns]
            turns -= jnp.floor(turns + 0.5)
            square = turns * turns
            table_ref[0, rows, columns] = series(COS_SERIES, square).astype(BF16)
            table_ref[0, pl.ds(SLAB + start, chunk), columns] = (
                turns * series(SIN_SERIES, square)
            ).astype(BF16)
    gains = gain_columns(multiplier_ref[:, 0, :], labels_ref[...])
    charges = matmul(flip(inward_ref[0]), features_ref[...], 1, 1) * gains
    grad_pot = matmul(outward_ref[1], upstream_ref[...], 1, 1)
    values = jnp.concatenate([charges, grad_pot], axis=0).astype(BF16)
    values_ref[0] = values
    part = matmul(table_ref[0], values, 1, 1)

    @pl.when(step == 0)
    def _():
        total_ref[...] = part

    @pl.when(step != 0)
    def _():
        total_ref[...] += part

    @pl.when(step == pl.num_programs(0) - 1)
    def _():
        write_pieces(place, total_ref, keep_ref, send_ref)


def weights_kernel(prefactor, place, classes_ref, weights_ref):
    chunk = 128
    for start in range(0, SLAB, chunk):
        rows = pl.ds(start, chunk)
        own = lax.broadcasted_iota(jnp.int32, (chunk, CHANNELS), 0) + (place[0] * SLAB + start)
        count = jnp.zeros((chunk, CHANNELS), F32)
        for group in range(classes_ref.shape[0]):
            for offset in range(0, classes_ref.shape[1], CHANNELS):
                classes = classes_ref[group : group + 1, offset : offset + CHANNELS]
                count += jnp.where(classes == own, 1.0, 0.0)
        count = jnp.sum(count, axis=1, keepdims=True)
        vectors = class_vectors(place[0] * SLAB + start, (chunk, CHANNELS), 0)
        norm = vectors[0] * vectors[0] + vectors[1] * vectors[1] + vectors[2] * vectors[2]
        for block, spread in enumerate(GAUSSIAN_SIGMAS):
            weights_ref[block, rows, :] = count * (prefactor * jnp.exp(norm * (-1.0 / spread)))


def potential_kernel(
    place, weights_ref, mine_ref, other_ref, table_ref, fields_ref, p0, p1, p2, p3, total_ref, flipped_ref
):
    step = pl.program_id(0)

    @pl.when(step == 0)
    def _():
        read_pieces(place, mine_ref, other_ref, total_ref)
        for half in range(2):
            rows = pl.ds(half * SLAB, SLAB)
            for side in range(2):
                columns = pl.ds(side * CHANNELS, CHANNELS)
                total_ref[rows, columns] = total_ref[rows, columns] * weights_ref[side]
        fields_ref[...] = total_ref[...].astype(BF16)
        flipped_ref[...] = jnp.transpose(total_ref[...]).astype(BF16)

    product = matmul(flipped_ref[...], table_ref[0], 1, 0).astype(BF16)
    for index, target in enumerate((p0, p1, p2, p3)):

        @pl.when(step == index)
        def _():
            target[...] = product


def middle_kernel(
    place,
    q0,
    q1,
    q2,
    q3,
    labels_ref,
    features_ref,
    upstream_ref,
    inward_ref,
    outward_ref,
    multiplier_ref,
    values_ref,
    hidden_grad_ref,
):
    total = (q0[...].astype(F32) + q1[...].astype(F32)) + (q2[...].astype(F32) + q3[...].astype(F32))
    potential = total[:CHANNELS].astype(BF16)
    grad_charge = total[CHANNELS:]
    gains = gain_columns(multiplier_ref[:, 1, :], labels_ref[...])
    hidden = (
        features_ref[...].astype(F32)
        + matmul(jnp.transpose(potential.astype(F32)).astype(BF16), outward_ref[0], 1, 0)
    ).astype(BF16)
    inward_flipped = flip(inward_ref[1])
    charges = matmul(inward_flipped, hidden, 1, 1) * gains
    scaled = jnp.transpose(grad_charge * gains).astype(BF16)
    hidden_grad = (
        upstream_ref[...].astype(F32) + matmul(scaled, inward_flipped, 1, 0)
    ).astype(BF16)
    hidden_grad_ref[...] = hidden_grad
    grad_pot = matmul(outward_ref[0], hidden_grad, 1, 1)
    values_ref[...] = jnp.concatenate([charges, grad_pot], axis=0).astype(BF16)


def second_kernel(place, table_ref, v0, v1, v2, v3, keep_ref, send_ref, total_ref):
    step = pl.program_id(0)
    for index, source in enumerate((v0, v1, v2, v3)):

        @pl.when(step == index)
        def _():
            part = matmul(table_ref[0], source[...], 1, 1)
            if index == 0:
                total_ref[...] = part
            else:
                total_ref[...] += part

    @pl.when(step == pl.num_programs(0) - 1)
    def _():
        write_pieces(place, total_ref, keep_ref, send_ref)


def gradient_kernel(
    place,
    weights_ref,
    mine_ref,
    other_ref,
    fields_ref,
    table_ref,
    first_ref,
    v0,
    v1,
    v2,
    v3,
    o0,
    o1,
    o2,
    o3,
    total_ref,
    pairs_ref,
    flipped_ref,
    directions_ref,
    theta_ref,
    second_ref,
):
    step = pl.program_id(0)

    @pl.when(step == 0)
    def _():
        read_pieces(place, mine_ref, other_ref, total_ref)
        for half in range(2):
            rows = pl.ds(half * SLAB, SLAB)
            for side in range(2):
                columns = pl.ds(side * CHANNELS, CHANNELS)
                total_ref[rows, columns] = total_ref[rows, columns] * weights_ref[1 - side]
        field_two = total_ref[:, :CHANNELS].astype(BF16)
        grad_one = total_ref[:, CHANNELS:]
        pairs_ref[:, 0:CHANNELS] = grad_one.astype(BF16)
        pairs_ref[:, CHANNELS : 2 * CHANNELS] = field_two
        pairs_ref[:, 2 * CHANNELS : 3 * CHANNELS] = fields_ref[:, CHANNELS:]
        pairs_ref[:, 3 * CHANNELS :] = fields_ref[:, :CHANNELS]
        flipped_ref[...] = jnp.transpose(grad_one).astype(BF16)
        vectors = class_vectors(place[0] * SLAB, (16, SLAB), 1)
        row = lax.broadcasted_iota(jnp.int32, (16, SLAB), 0)
        directions = jnp.where(row == 0, vectors[0], jnp.where(row == 1, vectors[1], vectors[2]))
        directions_ref[...] = jnp.where(row < 3, directions, 0.0).astype(BF16)

    for index, source in enumerate((v0, v1, v2, v3)):

        @pl.when(step == index)
        def _():
            second_ref[...] = source[...]

    values = jnp.concatenate([first_ref[0], second_ref[...]], axis=0)
    chunk = 128
    for start in range(0, SLAB, chunk):
        real = pl.ds(start, chunk)
        imag = pl.ds(SLAB + start, chunk)
        along_real = matmul(pairs_ref[real, :], values, 1, 0)
        along_imag = matmul(pairs_ref[imag, :], values, 1, 0)
        theta_ref[real, :] = (
            table_ref[0, real, :].astype(F32) * along_imag
            - table_ref[0, imag, :].astype(F32) * along_real
        ).astype(BF16)
    charge = matmul(flipped_ref[...], table_ref[0], 1, 0)
    position = matmul(directions_ref[...], theta_ref[...], 1, 0)
    result = jnp.concatenate([charge, position * (2.0 * math.pi / BOX_LENGTH)], axis=0).astype(BF16)
    for index, target in enumerate((o0, o1, o2, o3)):

        @pl.when(step == index)
        def _():
            target[...] = result


def final_kernel(
    place, q0, q1, q2, q3, labels_ref, hidden_grad_ref, inward_ref, multiplier_ref, features_ref, positions_ref
):
    total = (q0[...].astype(F32) + q1[...].astype(F32)) + (q2[...].astype(F32) + q3[...].astype(F32))
    gains = gain_columns(multiplier_ref[:, 0, :], labels_ref[...])
    scaled = jnp.transpose(total[:CHANNELS] * gains).astype(BF16)
    features_ref[...] = (
        hidden_grad_ref[...].astype(F32) + matmul(scaled, flip(inward_ref[0]), 1, 0)
    ).astype(BF16)
    positions_ref[...] = total[CHANNELS : CHANNELS + 3]


def shape_of(shape, dtype):
    return jax.ShapeDtypeStruct(shape, dtype)


def whole(shape):
    return pl.BlockSpec(shape, lambda step, place: (0,) * len(shape))


def call(
    kernel, steps, in_specs, outs, out_specs, scratch, operands, limit=VMEM_SHARED, micros=2
):
    return pl.pallas_call(
        kernel,
        grid_spec=pltpu.PrefetchScalarGridSpec(
            num_scalar_prefetch=1,
            grid=(steps,),
            in_specs=in_specs,
            out_specs=out_specs,
            scratch_shapes=scratch,
        ),
        out_shape=outs,
        compiler_params=pltpu.CompilerParams(
            dimension_semantics=("arbitrary",), vmem_limit_bytes=limit
        ),
        cost_estimate=pl.CostEstimate(
            flops=micros * 10**9, bytes_accessed=micros * 10**6, transcendentals=0
        ),
    )(*operands)


ATOM_REST = ("yh", "yl", "z")


def shifted(value, shift):
    return lax.ppermute(value, "x", [(i, (i + shift) % SLABS) for i in range(SLABS)])


def swapped(value):
    return lax.ppermute(value, "core", [(0, 1), (1, 0)])


def add_halves(keep, send):
    return (keep.astype(F32) + swapped(send).astype(F32)).astype(BF16)


def sum_fields(part):
    parts = lax.all_to_all(part, ATOM_REST, 0, 0, tiled=True)
    total = jnp.sum(parts.astype(F32), axis=0).astype(BF16)
    spread = jnp.broadcast_to(total[None], (PIECES,) + total.shape)
    mine = lax.all_to_all(spread, ATOM_REST, 0, 0, tiled=True)
    return mine, swapped(mine)


def per_device(
    atomic_descriptors,
    unit_cell_coordinates,
    element_labels,
    lattice_momenta,
    feature_to_latent_matrix,
    latent_to_feature_matrix,
    element_latent_multiplier,
    upstream_gradient,
):
    place = jnp.stack(
        [lax.axis_index("x"), lax.axis_index("yh"), lax.axis_index("core")]
    ).astype(jnp.int32)
    prefactor = 1.0 / math.sqrt(
        atomic_descriptors.shape[0]
        * lattice_momenta.shape[1]
        * lax.axis_size(("x", "yh", "yl", "z", "core"))
    )
    labels = element_labels[None, :]
    multiplier = jnp.swapaxes(element_latent_multiplier, 0, 1)
    signed = (
        lattice_momenta[0] * (SPAN * SPAN) + lattice_momenta[1] * SPAN + lattice_momenta[2]
    )
    own = jnp.abs(signed)[None]
    row = jnp.concatenate([own] + [shifted(own, shift) for shift in range(1, SLABS)], axis=0)

    matrices = whole((2, CHANNELS, CHANNELS))
    gains_spec = whole(multiplier.shape)
    pieces_spec = whole((PIECES, ROWS, CHANNELS))
    pieces_shape = shape_of((PIECES, ROWS, CHANNELS), BF16)
    values_block = whole((BLOCK, BLOCK))
    values_shape = shape_of((BLOCK, BLOCK), BF16)
    table_shape = shape_of((SLABS, TABLE, BLOCK), BF16)

    def rotated(shape, sign):
        return pl.BlockSpec(
            (1,) + shape, lambda step, place: ((place[0] + sign * step + SLABS) % SLABS, 0, 0)
        )

    table, values_one, keep, send = call(
        tables_kernel,
        SLABS,
        [
            pl.BlockSpec((3, BLOCK), lambda step, place: (0, 2 * step + place[1])),
            pl.BlockSpec((1, BLOCK), lambda step, place: (0, 2 * step + place[1])),
            pl.BlockSpec((BLOCK, CHANNELS), lambda step, place: (2 * step + place[1], 0)),
            pl.BlockSpec((BLOCK, CHANNELS), lambda step, place: (2 * step + place[1], 0)),
            matrices,
            matrices,
            gains_spec,
        ],
        (table_shape, shape_of((SLABS, BLOCK, BLOCK), BF16), pieces_shape, pieces_shape),
        (
            pl.BlockSpec((1, TABLE, BLOCK), lambda step, place: (step, 0, 0)),
            pl.BlockSpec((1, BLOCK, BLOCK), lambda step, place: (step, 0, 0)),
            pieces_spec,
            pieces_spec,
        ),
        [pltpu.VMEM((TABLE, BLOCK), F32)],
        (
            place,
            unit_cell_coordinates,
            labels,
            atomic_descriptors,
            upstream_gradient,
            feature_to_latent_matrix,
            latent_to_feature_matrix,
            multiplier,
        ),
        limit=VMEM_ALL,
        micros=9,
    )
    keep, send, row = lax.optimization_barrier((keep, send, row))
    part = add_halves(keep, send)
    other_row = lax.ppermute(row, "yh", [(0, 1), (1, 0)])
    part, other_row = lax.optimization_barrier((part, other_row))
    classes = jnp.concatenate([row, other_row], axis=0)
    weights = call(
        functools.partial(weights_kernel, prefactor),
        1,
        [whole(classes.shape)],
        shape_of((2, SLAB, CHANNELS), F32),
        whole((2, SLAB, CHANNELS)),
        [],
        (place, classes),
    )
    mine, other = sum_fields(part)
    fields, *products = call(
        potential_kernel,
        SLABS,
        [whole((2, SLAB, CHANNELS)), pieces_spec, pieces_spec, rotated((TABLE, BLOCK), 1)],
        (shape_of((TABLE, BLOCK), BF16),) + (values_shape,) * SLABS,
        (whole((TABLE, BLOCK)),) + (values_block,) * SLABS,
        [pltpu.VMEM((TABLE, BLOCK), F32), pltpu.VMEM((BLOCK, TABLE), BF16)],
        (place, weights, mine, other, table),
    )
    arrived = [products[0]] + [shifted(products[shift], shift) for shift in range(1, SLABS)]
    own_atoms = pl.BlockSpec((BLOCK, CHANNELS), lambda step, place: (2 * place[0] + place[1], 0))
    own_labels = pl.BlockSpec((1, BLOCK), lambda step, place: (0, 2 * place[0] + place[1]))
    values_two, hidden_grad = call(
        middle_kernel,
        1,
        [values_block] * SLABS
        + [own_labels, own_atoms, own_atoms, matrices, matrices, gains_spec],
        (values_shape, shape_of((BLOCK, CHANNELS), BF16)),
        (values_block, whole((BLOCK, CHANNELS))),
        [],
        (
            place,
            *arrived,
            labels,
            atomic_descriptors,
            upstream_gradient,
            feature_to_latent_matrix,
            latent_to_feature_matrix,
            multiplier,
        ),
    )
    seconds = [values_two] + [shifted(values_two, SLABS - slot) for slot in range(1, SLABS)]
    keep, send = call(
        second_kernel,
        SLABS,
        [rotated((TABLE, BLOCK), 1)] + [values_block] * SLABS,
        (pieces_shape, pieces_shape),
        (pieces_spec, pieces_spec),
        [pltpu.VMEM((TABLE, BLOCK), F32)],
        (place, table, *seconds),
    )
    mine, other = sum_fields(add_halves(keep, send))
    result_shape = shape_of((CHANNELS + 16, BLOCK), BF16)
    result_spec = whole((CHANNELS + 16, BLOCK))
    results = call(
        gradient_kernel,
        SLABS,
        [
            whole((2, SLAB, CHANNELS)),
            pieces_spec,
            pieces_spec,
            whole((TABLE, BLOCK)),
            rotated((TABLE, BLOCK), 1),
            rotated((BLOCK, BLOCK), 1),
        ]
        + [values_block] * SLABS,
        (result_shape,) * SLABS,
        (result_spec,) * SLABS,
        [
            pltpu.VMEM((TABLE, BLOCK), F32),
            pltpu.VMEM((TABLE, 2 * BLOCK), BF16),
            pltpu.VMEM((CHANNELS, TABLE), BF16),
            pltpu.VMEM((16, SLAB), BF16),
            pltpu.VMEM((SLAB, BLOCK), BF16),
            pltpu.VMEM((BLOCK, BLOCK), BF16),
        ],
        (place, weights, mine, other, fields, table, values_one, *seconds),
        limit=VMEM_ALL,
        micros=6,
    )
    arrived = [results[0]] + [shifted(results[shift], shift) for shift in range(1, SLABS)]
    return call(
        final_kernel,
        1,
        [result_spec] * SLABS
        + [own_labels, whole((BLOCK, CHANNELS)), matrices, gains_spec],
        (shape_of((BLOCK, CHANNELS), BF16), shape_of((3, BLOCK), F32)),
        (whole((BLOCK, CHANNELS)), whole((3, BLOCK))),
        [],
        (place, *arrived, labels, hidden_grad, feature_to_latent_matrix, multiplier),
    )


def solution(mesh):
    fine = Mesh(mesh.devices.reshape(SLABS, 2, 2, -1, 2), ("x", "yh", "yl", "z", "core"))
    atom, group = ("yl", "z", "core"), ("x", "yh")
    in_specs = (
        P(atom, None),
        P(None, atom),
        P(atom),
        P(None, group),
        P(),
        P(),
        P(),
        P(atom, None),
    )
    out_specs = (P(atom + group, None), P(None, atom + group))
    return jax.shard_map(
        per_device, mesh=fine, in_specs=in_specs, out_specs=out_specs, check_vma=False
    )
```

```python
import functools
import math

import jax
import jax.numpy as jnp
from jax import lax
from jax.experimental import pallas as pl
from jax.experimental.pallas import tpu as pltpu
from jax.sharding import Mesh
from jax.sharding import PartitionSpec as P

BOX_LENGTH = 100.0
GAUSSIAN_SIGMAS = (200.0, 100.0)
REACH = 8
SPAN = 2 * REACH + 1
CLASSES = (SPAN**3 + 1) // 2
SLABS = 4
SLAB = 640
TABLE = 2 * SLAB
BLOCK = 256
CHANNELS = 128
ROWS = 40
PIECES = 32
VMEM_LIMIT = 24 * 1024 * 1024
BF16 = jnp.bfloat16
F32 = jnp.float32

COS_SERIES = (
    0.999999660315462,
    -19.739032161520388,
    64.93001235415629,
    -85.28515888817482,
    58.84788533073816,
    -21.15810679384873,
)
SIN_SERIES = (
    6.283183359037432,
    -41.341456424111435,
    81.59687947501621,
    -76.58597187733577,
    41.22756686823296,
    -12.302134397179453,
)


def class_vectors(first_class, shape, axis):
    label = (lax.broadcasted_iota(jnp.int32, shape, axis) + first_class).astype(F32)
    square = SPAN * SPAN
    first = jnp.floor((label + (square // 2 + 0.5)) * (1.0 / square))
    rest = label - square * first
    second = jnp.floor((rest + (REACH + 0.5)) * (1.0 / SPAN))
    return first, second, rest - SPAN * second


def matmul(left, right, left_dim, right_dim):
    return lax.dot_general(
        left, right, (((left_dim,), (right_dim,)), ((), ())), preferred_element_type=F32
    )


def flip(matrix):
    return jnp.transpose(matrix.astype(F32)).astype(BF16)


def gain_columns(multiplier, labels):
    species_count, channels = multiplier.shape
    padding = jnp.zeros((8 - species_count, channels), F32)
    columns = jnp.transpose(jnp.concatenate([multiplier, padding], axis=0))
    result = jnp.zeros((channels, labels.shape[1]), F32)
    for species in range(species_count):
        result = jnp.where(labels == species, columns[:, species : species + 1], result)
    return result


def series(coefficients, square):
    result = coefficients[-1] * square + coefficients[-2]
    for coefficient in coefficients[-3::-1]:
        result = result * square + coefficient
    return result


def write_pieces(place, total_ref, keep_ref, send_ref):
    core = place[2]
    for target, half in ((keep_ref, core), (send_ref, 1 - core)):
        for index in range(PIECES):
            row, side = index // 2, index % 2
            start = pl.multiple_of(half * SLAB + row * ROWS, 8)
            target[index] = total_ref[
                pl.ds(start, ROWS), side * CHANNELS : (side + 1) * CHANNELS
            ].astype(BF16)


def read_pieces(place, mine_ref, other_ref, total_ref):
    core = place[2]
    for source, half in ((mine_ref, core), (other_ref, 1 - core)):
        for index in range(PIECES):
            row, side = index // 2, index % 2
            start = pl.multiple_of(half * SLAB + row * ROWS, 8)
            total_ref[pl.ds(start, ROWS), side * CHANNELS : (side + 1) * CHANNELS] = source[
                index
            ].astype(F32)


def slot(index):
    return slice(index * BLOCK, (index + 1) * BLOCK)


def tables_kernel(
    place,
    coordinates_hbm,
    labels_hbm,
    features_hbm,
    upstream_hbm,
    inward_hbm,
    outward_hbm,
    multiplier_hbm,
    table_ref,
    values_ref,
    keep_ref,
    send_ref,
    coordinates_ref,
    labels_ref,
    features_ref,
    upstream_ref,
    inward_ref,
    outward_ref,
    multiplier_ref,
    total_ref,
    arrivals,
):
    copies = [
        pltpu.make_async_copy(source, target, arrivals.at[index])
        for index, (source, target) in enumerate(
            (
                (coordinates_hbm, coordinates_ref),
                (labels_hbm, labels_ref),
                (features_hbm.at[:, place[1]], features_ref),
                (upstream_hbm.at[:, place[1]], upstream_ref),
                (inward_hbm, inward_ref),
                (outward_hbm, outward_ref),
                (multiplier_hbm, multiplier_ref),
            )
        )
    ]
    for copy in copies:
        copy.start()
    copies[0].wait()
    blocks = [lax.rem(place[0] + index, SLABS) for index in range(SLABS)]
    sides = [
        pl.ds(pl.multiple_of((2 * block + place[1]) * BLOCK + side * CHANNELS, CHANNELS), CHANNELS)
        for block in blocks
        for side in range(BLOCK // CHANNELS)
    ]
    chunk = 64
    for start in range(0, SLAB, chunk):
        vectors = class_vectors(place[0] * SLAB + start, (chunk, CHANNELS), 0)
        for index, side in enumerate(sides):
            columns = slice(index * CHANNELS, (index + 1) * CHANNELS)
            turns = vectors[0] * coordinates_ref[0:1, side]
            turns += vectors[1] * coordinates_ref[1:2, side]
            turns += vectors[2] * coordinates_ref[2:3, side]
            turns -= jnp.floor(turns + 0.5)
            square = turns * turns
            table_ref[start : start + chunk, columns] = series(COS_SERIES, square).astype(BF16)
            table_ref[SLAB + start : SLAB + start + chunk, columns] = (
                turns * series(SIN_SERIES, square)
            ).astype(BF16)
    for copy in copies[1:]:
        copy.wait()
    inward = flip(inward_ref[0])
    for index, block in enumerate(blocks):
        labels = labels_ref[:, pl.ds(pl.multiple_of((2 * block + place[1]) * BLOCK, BLOCK), BLOCK)]
        gains = gain_columns(multiplier_ref[:, 0, :], labels)
        charges = matmul(inward, features_ref[block], 1, 1) * gains
        grad_pot = matmul(outward_ref[1], upstream_ref[block], 1, 1)
        values_ref[:CHANNELS, slot(index)] = charges.astype(BF16)
        values_ref[CHANNELS:, slot(index)] = grad_pot.astype(BF16)
    total_ref[...] = matmul(table_ref[...], values_ref[...], 1, 1)
    write_pieces(place, total_ref, keep_ref, send_ref)


def weights_kernel(prefactor, place, classes_ref, weights_ref):
    chunk = 128
    for start in range(0, SLAB, chunk):
        rows = pl.ds(start, chunk)
        own = lax.broadcasted_iota(jnp.int32, (chunk, CHANNELS), 0) + (place[0] * SLAB + start)
        count = jnp.zeros((chunk, CHANNELS), F32)
        for group in range(classes_ref.shape[0]):
            for offset in range(0, classes_ref.shape[1], CHANNELS):
                classes = classes_ref[group : group + 1, offset : offset + CHANNELS]
                count += jnp.where(classes == own, 1.0, 0.0)
        count = jnp.sum(count, axis=1, keepdims=True)
        vectors = class_vectors(place[0] * SLAB + start, (chunk, CHANNELS), 0)
        norm = vectors[0] * vectors[0] + vectors[1] * vectors[1] + vectors[2] * vectors[2]
        for block, spread in enumerate(GAUSSIAN_SIGMAS):
            weights_ref[block, rows, :] = count * (prefactor * jnp.exp(norm * (-1.0 / spread)))


def weigh(total_ref, weights_ref, first):
    for half in range(2):
        rows = pl.ds(half * SLAB, SLAB)
        for side in range(2):
            columns = pl.ds(side * CHANNELS, CHANNELS)
            total_ref[rows, columns] = total_ref[rows, columns] * weights_ref[(first + side) % 2]


def potential_kernel(
    place, weights_ref, mine_ref, other_ref, table_ref, fields_ref, p0, p1, p2, p3, total_ref
):
    read_pieces(place, mine_ref, other_ref, total_ref)
    weigh(total_ref, weights_ref, 0)
    fields_ref[...] = total_ref[...].astype(BF16)
    flipped = jnp.transpose(total_ref[...]).astype(BF16)
    for index, target in enumerate((p0, p1, p2, p3)):
        target[...] = matmul(flipped, table_ref[:, slot(index)], 1, 0).astype(BF16)


def middle_kernel(
    place,
    q0,
    q1,
    q2,
    q3,
    labels_ref,
    features_ref,
    upstream_ref,
    inward_ref,
    outward_ref,
    multiplier_ref,
    values_ref,
    hidden_grad_ref,
):
    total = (q0[...].astype(F32) + q1[...].astype(F32)) + (q2[...].astype(F32) + q3[...].astype(F32))
    potential = total[:CHANNELS].astype(BF16)
    grad_charge = total[CHANNELS:]
    gains = gain_columns(multiplier_ref[:, 1, :], labels_ref[...])
    hidden = (
        features_ref[...].astype(F32)
        + matmul(jnp.transpose(potential.astype(F32)).astype(BF16), outward_ref[0], 1, 0)
    ).astype(BF16)
    inward_flipped = flip(inward_ref[1])
    charges = matmul(inward_flipped, hidden, 1, 1) * gains
    scaled = jnp.transpose(grad_charge * gains).astype(BF16)
    hidden_grad = (
        upstream_ref[...].astype(F32) + matmul(scaled, inward_flipped, 1, 0)
    ).astype(BF16)
    hidden_grad_ref[...] = hidden_grad
    grad_pot = matmul(outward_ref[0], hidden_grad, 1, 1)
    values_ref[...] = jnp.concatenate([charges, grad_pot], axis=0).astype(BF16)


def second_kernel(place, table_ref, v0, v1, v2, v3, values_ref, keep_ref, send_ref, total_ref):
    for index, source in enumerate((v0, v1, v2, v3)):
        values_ref[:, slot(index)] = source[...]
    total_ref[...] = matmul(table_ref[...], values_ref[...], 1, 1)
    write_pieces(place, total_ref, keep_ref, send_ref)


def gradient_kernel(
    place,
    weights_ref,
    mine_ref,
    other_ref,
    table_ref,
    fields_hbm,
    first_hbm,
    second_hbm,
    o0,
    o1,
    o2,
    o3,
    total_ref,
    pairs_ref,
    values_ref,
    theta_ref,
    fields_ref,
    arrivals,
):
    copies = [
        pltpu.make_async_copy(source, target, arrivals.at[index])
        for index, (source, target) in enumerate(
            (
                (fields_hbm, fields_ref),
                (first_hbm, values_ref.at[:BLOCK]),
                (second_hbm, values_ref.at[BLOCK:]),
            )
        )
    ]
    for copy in copies:
        copy.start()
    read_pieces(place, mine_ref, other_ref, total_ref)
    weigh(total_ref, weights_ref, 1)
    grad_one = total_ref[:, CHANNELS:]
    pairs_ref[:, 0:CHANNELS] = grad_one.astype(BF16)
    pairs_ref[:, CHANNELS : 2 * CHANNELS] = total_ref[:, :CHANNELS].astype(BF16)
    flipped = jnp.transpose(grad_one).astype(BF16)
    vectors = class_vectors(place[0] * SLAB, (16, SLAB), 1)
    row = lax.broadcasted_iota(jnp.int32, (16, SLAB), 0)
    directions = jnp.where(row == 0, vectors[0], jnp.where(row == 1, vectors[1], vectors[2]))
    directions = jnp.where(row < 3, directions, 0.0).astype(BF16)
    for copy in copies:
        copy.wait()
    pairs_ref[:, 2 * CHANNELS : 3 * CHANNELS] = fields_ref[:, CHANNELS:]
    pairs_ref[:, 3 * CHANNELS :] = fields_ref[:, :CHANNELS]
    for index, target in enumerate((o0, o1, o2, o3)):
        columns = slot(index)
        along_real = matmul(pairs_ref[:SLAB], values_ref[:, columns], 1, 0)
        along_imag = matmul(pairs_ref[SLAB:], values_ref[:, columns], 1, 0)
        theta_ref[:, columns] = (
            table_ref[:SLAB, columns].astype(F32) * along_imag
            - table_ref[SLAB:, columns].astype(F32) * along_real
        ).astype(BF16)
        charge = matmul(flipped, table_ref[:, columns], 1, 0)
        position = matmul(directions, theta_ref[:, columns], 1, 0)
        target[:CHANNELS] = charge.astype(BF16)
        target[CHANNELS:] = (position * (2.0 * math.pi / BOX_LENGTH)).astype(BF16)


def final_kernel(
    place, q0, q1, q2, q3, labels_ref, hidden_grad_ref, inward_ref, multiplier_ref, features_ref, positions_ref
):
    total = (q0[...].astype(F32) + q1[...].astype(F32)) + (q2[...].astype(F32) + q3[...].astype(F32))
    gains = gain_columns(multiplier_ref[:, 0, :], labels_ref[...])
    scaled = jnp.transpose(total[:CHANNELS] * gains).astype(BF16)
    features_ref[...] = (
        hidden_grad_ref[...].astype(F32) + matmul(scaled, flip(inward_ref[0]), 1, 0)
    ).astype(BF16)
    positions_ref[...] = total[CHANNELS : CHANNELS + 3]


def shape_of(shape, dtype):
    return jax.ShapeDtypeStruct(shape, dtype)


def far(value):
    return pltpu.with_memory_space_constraint(value, pltpu.HBM)


def near(value):
    return pltpu.with_memory_space_constraint(value, pltpu.VMEM)


def whole(shape):
    return pl.BlockSpec(shape, lambda step, place: (0,) * len(shape))


def compiler(micros):
    return dict(
        compiler_params=pltpu.CompilerParams(vmem_limit_bytes=VMEM_LIMIT),
        cost_estimate=pl.CostEstimate(
            flops=micros * 10**9, bytes_accessed=micros * 10**6, transcendentals=0
        ),
    )


def call(kernel, in_specs, outs, out_specs, operands, micros=2):
    return pl.pallas_call(
        kernel,
        grid_spec=pltpu.PrefetchScalarGridSpec(
            num_scalar_prefetch=1, grid=(1,), in_specs=in_specs, out_specs=out_specs
        ),
        out_shape=outs,
        **compiler(micros),
    )(*operands)


def call_whole(kernel, outs, scratch, place, operands, spaces=None, micros=2):
    spaces = spaces or [pltpu.VMEM] * len(operands)
    return pl.pallas_call(
        kernel,
        in_specs=[pl.BlockSpec(memory_space=pltpu.SMEM)]
        + [pl.BlockSpec(memory_space=space) for space in spaces],
        out_specs=[pl.BlockSpec(memory_space=pltpu.VMEM)] * len(outs),
        out_shape=outs,
        scratch_shapes=scratch,
        **compiler(micros),
    )(place, *operands)


ATOM_REST = ("yh", "yl", "z")


def shifted(value, shift):
    return lax.ppermute(value, "x", [(i, (i + shift) % SLABS) for i in range(SLABS)])


def swapped(value):
    return lax.ppermute(value, "core", [(0, 1), (1, 0)])


def add_halves(keep, send):
    return (keep.astype(F32) + swapped(send).astype(F32)).astype(BF16)


def sum_fields(part):
    parts = lax.all_to_all(part, ATOM_REST, 0, 0, tiled=True)
    total = jnp.sum(parts.astype(F32), axis=0).astype(BF16)
    spread = jnp.broadcast_to(total[None], (PIECES,) + total.shape)
    mine = lax.all_to_all(spread, ATOM_REST, 0, 0, tiled=True)
    return mine, swapped(mine)


def per_device(
    atomic_descriptors,
    unit_cell_coordinates,
    element_labels,
    lattice_momenta,
    feature_to_latent_matrix,
    latent_to_feature_matrix,
    element_latent_multiplier,
    upstream_gradient,
):
    place = jnp.stack(
        [lax.axis_index("x"), lax.axis_index("yh"), lax.axis_index("core")]
    ).astype(jnp.int32)
    prefactor = 1.0 / math.sqrt(
        atomic_descriptors.shape[0]
        * lattice_momenta.shape[1]
        * lax.axis_size(("x", "yh", "yl", "z", "core"))
    )
    labels = element_labels[None, :]
    multiplier = jnp.swapaxes(element_latent_multiplier, 0, 1)
    signed = (
        lattice_momenta[0] * (SPAN * SPAN) + lattice_momenta[1] * SPAN + lattice_momenta[2]
    )
    own = jnp.abs(signed)[None]
    row = jnp.concatenate([own] + [shifted(own, shift) for shift in range(1, SLABS)], axis=0)

    matrices = whole((2, CHANNELS, CHANNELS))
    gains_spec = whole(multiplier.shape)
    pieces_shape = shape_of((PIECES, ROWS, CHANNELS), BF16)
    values_block = whole((BLOCK, BLOCK))
    values_shape = shape_of((BLOCK, BLOCK), BF16)
    atoms_here = SLABS * BLOCK

    blocked = (SLABS, 2, BLOCK, CHANNELS)
    operands = [
        unit_cell_coordinates,
        labels,
        atomic_descriptors.reshape(blocked),
        upstream_gradient.reshape(blocked),
        feature_to_latent_matrix,
        latent_to_feature_matrix,
        multiplier,
    ]
    local = [shape_of(value.shape, value.dtype) for value in operands]
    local[2] = local[3] = shape_of((SLABS, BLOCK, CHANNELS), BF16)
    table, values_one, keep, send = call_whole(
        tables_kernel,
        (
            pltpu.VMEM((TABLE, atoms_here), BF16),
            shape_of((BLOCK, atoms_here), BF16),
            pieces_shape,
            pieces_shape,
        ),
        [pltpu.VMEM(value.shape, value.dtype) for value in local]
        + [pltpu.VMEM((TABLE, BLOCK), F32), pltpu.SemaphoreType.DMA((len(operands),))],
        place,
        [far(value) for value in operands],
        spaces=[pltpu.HBM] * len(operands),
        micros=7,
    )
    keep, send, row = lax.optimization_barrier((keep, send, row))
    part = add_halves(keep, send)
    other_row = lax.ppermute(row, "yh", [(0, 1), (1, 0)])
    part, other_row = lax.optimization_barrier((part, other_row))
    classes = jnp.concatenate([row, other_row], axis=0)
    (weights,) = call_whole(
        functools.partial(weights_kernel, prefactor),
        [shape_of((2, SLAB, CHANNELS), F32)],
        [],
        place,
        [classes],
    )
    mine, other = sum_fields(part)
    fields, *products = call_whole(
        potential_kernel,
        [shape_of((TABLE, BLOCK), BF16)] + [values_shape] * SLABS,
        [pltpu.VMEM((TABLE, BLOCK), F32)],
        place,
        [weights, mine, other, near(table)],
    )
    arrived = [products[0]] + [shifted(products[shift], shift) for shift in range(1, SLABS)]
    own_atoms = pl.BlockSpec((BLOCK, CHANNELS), lambda step, place: (2 * place[0] + place[1], 0))
    own_labels = pl.BlockSpec((1, BLOCK), lambda step, place: (0, 2 * place[0] + place[1]))
    values_own, hidden_grad = call(
        middle_kernel,
        [values_block] * SLABS
        + [own_labels, own_atoms, own_atoms, matrices, matrices, gains_spec],
        (values_shape, shape_of((BLOCK, CHANNELS), BF16)),
        (values_block, whole((BLOCK, CHANNELS))),
        (
            place,
            *arrived,
            labels,
            atomic_descriptors,
            upstream_gradient,
            feature_to_latent_matrix,
            latent_to_feature_matrix,
            multiplier,
        ),
    )
    seconds = [values_own] + [shifted(values_own, SLABS - other) for other in range(1, SLABS)]
    values_two, keep, send = call_whole(
        second_kernel,
        [shape_of((BLOCK, atoms_here), BF16), pieces_shape, pieces_shape],
        [pltpu.VMEM((TABLE, BLOCK), F32)],
        place,
        [near(table), *seconds],
    )
    mine, other = sum_fields(add_halves(keep, send))
    result_shape = shape_of((CHANNELS + 16, BLOCK), BF16)
    result_spec = whole((CHANNELS + 16, BLOCK))
    results = call_whole(
        gradient_kernel,
        [result_shape] * SLABS,
        [
            pltpu.VMEM((TABLE, BLOCK), F32),
            pltpu.VMEM((TABLE, 2 * BLOCK), BF16),
            pltpu.VMEM((2 * BLOCK, atoms_here), BF16),
            pltpu.VMEM((SLAB, atoms_here), BF16),
            pltpu.VMEM((TABLE, BLOCK), BF16),
            pltpu.SemaphoreType.DMA((3,)),
        ],
        place,
        [weights, mine, other, near(table), far(fields), far(values_one), far(values_two)],
        spaces=[pltpu.VMEM] * 4 + [pltpu.HBM] * 3,
        micros=5,
    )
    arrived = [results[0]] + [shifted(results[shift], shift) for shift in range(1, SLABS)]
    return call(
        final_kernel,
        [result_spec] * SLABS
        + [own_labels, whole((BLOCK, CHANNELS)), matrices, gains_spec],
        (shape_of((BLOCK, CHANNELS), BF16), shape_of((3, BLOCK), F32)),
        (whole((BLOCK, CHANNELS)), whole((3, BLOCK))),
        (place, *arrived, labels, hidden_grad, feature_to_latent_matrix, multiplier),
    )


def solution(mesh):
    fine = Mesh(mesh.devices.reshape(SLABS, 2, 2, -1, 2), ("x", "yh", "yl", "z", "core"))
    atom, group = ("yl", "z", "core"), ("x", "yh")
    in_specs = (
        P(atom, None),
        P(None, atom),
        P(atom),
        P(None, group),
        P(),
        P(),
        P(),
        P(atom, None),
    )
    out_specs = (P(atom + group, None), P(None, atom + group))
    return jax.shard_map(
        per_device, mesh=fine, in_specs=in_specs, out_specs=out_specs, check_vma=False
    )
```

```python
import functools
import math

import jax
import jax.numpy as jnp
from jax import lax
from jax.experimental import pallas as pl
from jax.experimental.pallas import tpu as pltpu
from jax.sharding import Mesh
from jax.sharding import PartitionSpec as P

BOX_LENGTH = 100.0
GAUSSIAN_SIGMAS = (200.0, 100.0)
REACH = 8
SPAN = 2 * REACH + 1
CLASSES = (SPAN**3 + 1) // 2
SLABS = 4
SLAB = 640
STRIDE = -(-CLASSES // SLABS)
LAST_FAR = (1, 3, 2)
COUNT_PIECE = 30
COUNT_ROW = 32
TABLE = 2 * SLAB
BLOCK = 256
CHANNELS = 128
ROWS = 40
PIECES = 32
VMEM_LIMIT = 14 * 1024 * 1024
BF16 = jnp.bfloat16
F32 = jnp.float32

COS_SERIES = (
    0.999999660315462,
    -19.739032161520388,
    64.93001235415629,
    -85.28515888817482,
    58.84788533073816,
    -21.15810679384873,
)
SIN_SERIES = (
    6.283183359037432,
    -41.341456424111435,
    81.59687947501621,
    -76.58597187733577,
    41.22756686823296,
    -12.302134397179453,
)


def class_vectors(first_class, shape, axis):
    label = (lax.broadcasted_iota(jnp.int32, shape, axis) + first_class).astype(F32)
    square = SPAN * SPAN
    first = jnp.floor((label + (square // 2 + 0.5)) * (1.0 / square))
    rest = label - square * first
    second = jnp.floor((rest + (REACH + 0.5)) * (1.0 / SPAN))
    return first, second, rest - SPAN * second


def matmul(left, right, left_dim, right_dim):
    return lax.dot_general(
        left, right, (((left_dim,), (right_dim,)), ((), ())), preferred_element_type=F32
    )


def flip(matrix):
    return jnp.transpose(matrix.astype(F32)).astype(BF16)


def gain_columns(multiplier, labels):
    species_count, channels = multiplier.shape
    padding = jnp.zeros((8 - species_count, channels), F32)
    columns = jnp.transpose(jnp.concatenate([multiplier, padding], axis=0))
    result = jnp.zeros((channels, labels.shape[1]), F32)
    for species in range(species_count):
        result = jnp.where(labels == species, columns[:, species : species + 1], result)
    return result


def series(coefficients, square):
    result = coefficients[-1] * square + coefficients[-2]
    for coefficient in coefficients[-3::-1]:
        result = result * square + coefficient
    return result


def write_pieces(place, total_ref, keep_ref, send_ref):
    core = place[2]
    for target, half in ((keep_ref, core), (send_ref, 1 - core)):
        for index in range(PIECES):
            row, side = index // 2, index % 2
            start = pl.multiple_of(half * SLAB + row * ROWS, 8)
            target[index] = total_ref[
                pl.ds(start, ROWS), side * CHANNELS : (side + 1) * CHANNELS
            ].astype(BF16)


def read_pieces(place, mine_ref, other_ref, total_ref):
    core = place[2]
    for source, half in ((mine_ref, core), (other_ref, 1 - core)):
        for index in range(PIECES):
            row, side = index // 2, index % 2
            start = pl.multiple_of(half * SLAB + row * ROWS, 8)
            total_ref[pl.ds(start, ROWS), side * CHANNELS : (side + 1) * CHANNELS] = source[
                index
            ].astype(F32)


def slot(index):
    return slice(index * BLOCK, (index + 1) * BLOCK)


def tables_kernel(
    place,
    coordinates_hbm,
    labels_hbm,
    features_hbm,
    upstream_hbm,
    inward_hbm,
    outward_hbm,
    multiplier_hbm,
    table_ref,
    values_hbm,
    keep_ref,
    send_ref,
    values_ref,
    coordinates_ref,
    labels_ref,
    features_ref,
    upstream_ref,
    inward_ref,
    outward_ref,
    multiplier_ref,
    total_ref,
    arrivals,
):
    copies = [
        pltpu.make_async_copy(source, target, arrivals.at[index])
        for index, (source, target) in enumerate(
            (
                (coordinates_hbm, coordinates_ref),
                (labels_hbm, labels_ref),
                (features_hbm.at[:, place[1]], features_ref),
                (upstream_hbm.at[:, place[1]], upstream_ref),
                (inward_hbm, inward_ref),
                (outward_hbm, outward_ref),
                (multiplier_hbm, multiplier_ref),
            )
        )
    ]
    for copy in copies:
        copy.start()
    copies[0].wait()
    blocks = [lax.rem(place[0] + index, SLABS) for index in range(SLABS)]
    sides = [
        pl.ds(pl.multiple_of((2 * block + place[1]) * BLOCK + side * CHANNELS, CHANNELS), CHANNELS)
        for block in blocks
        for side in range(BLOCK // CHANNELS)
    ]
    chunk = 64
    for start in range(0, SLAB, chunk):
        vectors = class_vectors(place[0] * STRIDE + start, (chunk, CHANNELS), 0)
        for index, side in enumerate(sides):
            columns = slice(index * CHANNELS, (index + 1) * CHANNELS)
            turns = vectors[0] * coordinates_ref[0:1, side]
            turns += vectors[1] * coordinates_ref[1:2, side]
            turns += vectors[2] * coordinates_ref[2:3, side]
            turns -= jnp.floor(turns + 0.5)
            square = turns * turns
            table_ref[start : start + chunk, columns] = series(COS_SERIES, square).astype(BF16)
            table_ref[SLAB + start : SLAB + start + chunk, columns] = (
                turns * series(SIN_SERIES, square)
            ).astype(BF16)
    for copy in copies[1:]:
        copy.wait()
    inward = flip(inward_ref[0])
    for index, block in enumerate(blocks):
        labels = labels_ref[:, pl.ds(pl.multiple_of((2 * block + place[1]) * BLOCK, BLOCK), BLOCK)]
        gains = gain_columns(multiplier_ref[:, 0, :], labels)
        charges = matmul(inward, features_ref[block], 1, 1) * gains
        grad_pot = matmul(outward_ref[1], upstream_ref[block], 1, 1)
        values_ref[:CHANNELS, slot(index)] = charges.astype(BF16)
        values_ref[CHANNELS:, slot(index)] = grad_pot.astype(BF16)
    leaving = pltpu.make_async_copy(values_ref, values_hbm, arrivals.at[len(copies)])
    leaving.start()
    total_ref[...] = matmul(table_ref[...], values_ref[...], 1, 1)
    for half in range(2):
        total_ref[(half + 1) * SLAB - 8 : (half + 1) * SLAB, :CHANNELS] = jnp.zeros((8, CHANNELS), F32)
    write_pieces(place, total_ref, keep_ref, send_ref)
    leaving.wait()


def counts_kernel(copies, place, momenta_ref, counts_ref):
    momenta = momenta_ref[...].astype(F32)
    label = jnp.abs(
        momenta[0:1] * float(SPAN * SPAN) + momenta[1:2] * float(SPAN) + momenta[2:3]
    ) - (place[0] * STRIDE).astype(F32)
    column = jnp.transpose(jnp.broadcast_to(label, (8, label.shape[1])))[:, 0:1]
    column = jnp.broadcast_to(column, (column.shape[0], CHANNELS))
    lane = lax.broadcasted_iota(jnp.int32, column.shape, 1).astype(F32)
    counts_ref[...] = jnp.zeros(counts_ref.shape, BF16)
    rows = []
    for start in range(0, SLAB, CHANNELS):
        here = (column == lane + float(start)) & (lane < float(STRIDE - start))
        rows.append(jnp.sum(jnp.where(here, 1.0 / copies, 0.0), axis=0, keepdims=True))
    rows.append(jnp.zeros((8 - len(rows), CHANNELS), F32))
    counts_ref[COUNT_PIECE, COUNT_ROW:, :] = jnp.concatenate(rows, axis=0).astype(BF16)


def weights_kernel(prefactor, place, pieces_ref, weights_ref):
    counts = jnp.transpose(pieces_ref[COUNT_PIECE, COUNT_ROW:, :].astype(F32))
    for index in range(SLAB // CHANNELS):
        start = index * CHANNELS
        count = counts[:, index : index + 1]
        vectors = class_vectors(place[0] * STRIDE + start, (CHANNELS, CHANNELS), 0)
        norm = vectors[0] * vectors[0] + vectors[1] * vectors[1] + vectors[2] * vectors[2]
        for block, spread in enumerate(GAUSSIAN_SIGMAS):
            weights_ref[block, start : start + CHANNELS, :] = count * (
                prefactor * jnp.exp(norm * (-1.0 / spread))
            )


def weigh(total_ref, weights_ref, first):
    for half in range(2):
        rows = pl.ds(half * SLAB, SLAB)
        for side in range(2):
            columns = pl.ds(side * CHANNELS, CHANNELS)
            total_ref[rows, columns] = total_ref[rows, columns] * weights_ref[(first + side) % 2]


def potential_kernel(
    place, weights_ref, mine_ref, other_ref, table_ref, fields_ref, p0, p1, p2, p3, total_ref
):
    read_pieces(place, mine_ref, other_ref, total_ref)
    weigh(total_ref, weights_ref, 0)
    fields_ref[...] = total_ref[...].astype(BF16)
    flipped = jnp.transpose(total_ref[...]).astype(BF16)
    for index, target in enumerate((p0, p1, p2, p3)):
        target[...] = matmul(flipped, table_ref[:, slot(index)], 1, 0).astype(BF16)


def middle_kernel(
    place,
    q0,
    q1,
    q2,
    q3,
    labels_ref,
    features_ref,
    upstream_ref,
    inward_ref,
    outward_ref,
    multiplier_ref,
    values_ref,
    hidden_grad_ref,
):
    total = (q0[...].astype(F32) + q1[...].astype(F32)) + (q2[...].astype(F32) + q3[...].astype(F32))
    potential = total[:CHANNELS].astype(BF16)
    grad_charge = total[CHANNELS:]
    gains = gain_columns(multiplier_ref[:, 1, :], labels_ref[...])
    hidden = (
        features_ref[...].astype(F32)
        + matmul(jnp.transpose(potential.astype(F32)).astype(BF16), outward_ref[0], 1, 0)
    ).astype(BF16)
    inward_flipped = flip(inward_ref[1])
    charges = matmul(inward_flipped, hidden, 1, 1) * gains
    scaled = jnp.transpose(grad_charge * gains).astype(BF16)
    hidden_grad = (
        upstream_ref[...].astype(F32) + matmul(scaled, inward_flipped, 1, 0)
    ).astype(BF16)
    hidden_grad_ref[...] = hidden_grad
    grad_pot = matmul(outward_ref[0], hidden_grad, 1, 1)
    values_ref[...] = jnp.concatenate([charges, grad_pot], axis=0).astype(BF16)


def second_kernel(place, table_ref, v0, v1, v2, v3, values_ref, keep_ref, send_ref, total_ref):
    for index, source in zip((0, *LAST_FAR), (v0, v1, v2, v3)):
        values_ref[:, slot(index)] = source[...]
    total_ref[...] = matmul(table_ref[...], values_ref[...], 1, 1)
    write_pieces(place, total_ref, keep_ref, send_ref)


def gradient_kernel(
    place,
    weights_ref,
    mine_ref,
    other_ref,
    table_ref,
    fields_hbm,
    first_hbm,
    second_hbm,
    o0,
    o1,
    o2,
    o3,
    total_ref,
    pairs_ref,
    values_ref,
    theta_ref,
    fields_ref,
    arrivals,
):
    copies = [
        pltpu.make_async_copy(source, target, arrivals.at[index])
        for index, (source, target) in enumerate(
            (
                (fields_hbm, fields_ref),
                (first_hbm, values_ref.at[:BLOCK]),
                (second_hbm, values_ref.at[BLOCK:]),
            )
        )
    ]
    for copy in copies:
        copy.start()
    read_pieces(place, mine_ref, other_ref, total_ref)
    weigh(total_ref, weights_ref, 1)
    grad_one = total_ref[:, CHANNELS:]
    pairs_ref[:, 0:CHANNELS] = grad_one.astype(BF16)
    pairs_ref[:, CHANNELS : 2 * CHANNELS] = total_ref[:, :CHANNELS].astype(BF16)
    flipped = jnp.transpose(grad_one).astype(BF16)
    vectors = class_vectors(place[0] * STRIDE, (16, SLAB), 1)
    row = lax.broadcasted_iota(jnp.int32, (16, SLAB), 0)
    directions = jnp.where(row == 0, vectors[0], jnp.where(row == 1, vectors[1], vectors[2]))
    directions = jnp.where(row < 3, directions, 0.0).astype(BF16)
    for copy in copies:
        copy.wait()
    pairs_ref[:, 2 * CHANNELS : 3 * CHANNELS] = fields_ref[:, CHANNELS:]
    pairs_ref[:, 3 * CHANNELS :] = fields_ref[:, :CHANNELS]
    for index, target in enumerate((o0, o1, o2, o3)):
        columns = slot(index)
        along_real = matmul(pairs_ref[:SLAB], values_ref[:, columns], 1, 0)
        along_imag = matmul(pairs_ref[SLAB:], values_ref[:, columns], 1, 0)
        theta_ref[:, columns] = (
            table_ref[:SLAB, columns].astype(F32) * along_imag
            - table_ref[SLAB:, columns].astype(F32) * along_real
        ).astype(BF16)
        charge = matmul(flipped, table_ref[:, columns], 1, 0)
        position = matmul(directions, theta_ref[:, columns], 1, 0)
        target[:CHANNELS] = charge.astype(BF16)
        target[CHANNELS:] = (position * (2.0 * math.pi / BOX_LENGTH)).astype(BF16)


def final_kernel(
    place, q0, q1, q2, q3, labels_ref, hidden_grad_ref, inward_ref, multiplier_ref, features_ref, positions_ref
):
    total = (q0[...].astype(F32) + q1[...].astype(F32)) + (q2[...].astype(F32) + q3[...].astype(F32))
    gains = gain_columns(multiplier_ref[:, 0, :], labels_ref[...])
    scaled = jnp.transpose(total[:CHANNELS] * gains).astype(BF16)
    features_ref[...] = (
        hidden_grad_ref[...].astype(F32) + matmul(scaled, flip(inward_ref[0]), 1, 0)
    ).astype(BF16)
    positions_ref[...] = total[CHANNELS : CHANNELS + 3]


def shape_of(shape, dtype):
    return jax.ShapeDtypeStruct(shape, dtype)


def far(value):
    return pltpu.with_memory_space_constraint(value, pltpu.HBM)


def near(value):
    return pltpu.with_memory_space_constraint(value, pltpu.VMEM)


def whole(shape):
    return pl.BlockSpec(shape, lambda step, place: (0,) * len(shape))


def compiler(micros):
    return dict(
        compiler_params=pltpu.CompilerParams(vmem_limit_bytes=VMEM_LIMIT),
        cost_estimate=pl.CostEstimate(
            flops=micros * 10**9, bytes_accessed=micros * 10**6, transcendentals=0
        ),
    )


def call(kernel, in_specs, outs, out_specs, operands, micros=2):
    return pl.pallas_call(
        kernel,
        grid_spec=pltpu.PrefetchScalarGridSpec(
            num_scalar_prefetch=1, grid=(1,), in_specs=in_specs, out_specs=out_specs
        ),
        out_shape=outs,
        **compiler(micros),
    )(*operands)


def call_whole(kernel, outs, scratch, place, operands, spaces=None, out_spaces=None, micros=2):
    spaces = spaces or [pltpu.VMEM] * len(operands)
    out_spaces = out_spaces or [pltpu.VMEM] * len(outs)
    return pl.pallas_call(
        kernel,
        in_specs=[pl.BlockSpec(memory_space=pltpu.SMEM)]
        + [pl.BlockSpec(memory_space=space) for space in spaces],
        out_specs=[pl.BlockSpec(memory_space=space) for space in out_spaces],
        out_shape=outs,
        scratch_shapes=scratch,
        **compiler(micros),
    )(place, *operands)


ATOM_REST = ("yh", "yl", "z")


def shifted(value, shift):
    return lax.ppermute(value, "x", [(i, (i + shift) % SLABS) for i in range(SLABS)])


def spread_out(send, own, order):
    return [own] + [send(shift) for shift in order]


def swapped(value):
    return lax.ppermute(value, "core", [(0, 1), (1, 0)])


def add_halves(keep, send, *more):
    total = keep.astype(F32) + swapped(send).astype(F32)
    for value in more:
        total = total + value.astype(F32)
    return total.astype(BF16)


def sum_fields(part):
    parts = lax.all_to_all(part, ATOM_REST, 0, 0, tiled=True)
    total = jnp.sum(parts.astype(F32), axis=0).astype(BF16)
    spread = jnp.broadcast_to(total[None], (PIECES,) + total.shape)
    mine = lax.all_to_all(spread, ATOM_REST, 0, 0, tiled=True)
    return mine, swapped(mine)


def per_device(
    atomic_descriptors,
    unit_cell_coordinates,
    element_labels,
    lattice_momenta,
    feature_to_latent_matrix,
    latent_to_feature_matrix,
    element_latent_multiplier,
    upstream_gradient,
):
    place = jnp.stack(
        [lax.axis_index("x"), lax.axis_index("yh"), lax.axis_index("core")]
    ).astype(jnp.int32)
    prefactor = 1.0 / math.sqrt(
        atomic_descriptors.shape[0]
        * lattice_momenta.shape[1]
        * lax.axis_size(("x", "yh", "yl", "z", "core"))
    )
    labels = element_labels[None, :]
    multiplier = jnp.swapaxes(element_latent_multiplier, 0, 1)
    lengths = {axis: lax.axis_size(axis) for axis in ("x", "yl", "z")}
    copies = lengths["yl"] * lengths["z"] // SLABS
    pairs = []
    for yl in range(lengths["yl"]):
        for z in range(lengths["z"]):
            for x in range(SLABS):
                place_of = lambda x: (x * lengths["yl"] + yl) * lengths["z"] + z
                pairs.append((place_of((x + 2 * (z % 2) + yl) % SLABS), place_of(x)))
    fetched = lax.ppermute(lattice_momenta, ("x", "yl", "z"), pairs)

    matrices = whole((2, CHANNELS, CHANNELS))
    gains_spec = whole(multiplier.shape)
    pieces_shape = shape_of((PIECES, ROWS, CHANNELS), BF16)
    values_block = whole((BLOCK, BLOCK))
    values_shape = shape_of((BLOCK, BLOCK), BF16)
    atoms_here = SLABS * BLOCK

    blocked = (SLABS, 2, BLOCK, CHANNELS)
    operands = [
        unit_cell_coordinates,
        labels,
        atomic_descriptors.reshape(blocked),
        upstream_gradient.reshape(blocked),
        feature_to_latent_matrix,
        latent_to_feature_matrix,
        multiplier,
    ]
    local = [shape_of(value.shape, value.dtype) for value in operands]
    local[2] = local[3] = shape_of((SLABS, BLOCK, CHANNELS), BF16)
    table, values_one, keep, send = call_whole(
        tables_kernel,
        (
            pltpu.VMEM((TABLE, atoms_here), BF16),
            pltpu.HBM((BLOCK, atoms_here), BF16),
            pieces_shape,
            pieces_shape,
        ),
        [pltpu.VMEM((BLOCK, atoms_here), BF16)]
        + [pltpu.VMEM(value.shape, value.dtype) for value in local]
        + [pltpu.VMEM((TABLE, BLOCK), F32), pltpu.SemaphoreType.DMA((len(operands) + 1,))],
        place,
        [far(value) for value in operands],
        spaces=[pltpu.HBM] * len(operands),
        out_spaces=[pltpu.VMEM, pltpu.HBM, pltpu.VMEM, pltpu.VMEM],
        micros=7,
    )
    (counts,) = call_whole(
        functools.partial(counts_kernel, float(copies)), [pieces_shape], [], place, [fetched]
    )
    part = add_halves(keep, send, counts)
    mine, other = sum_fields(part)
    (weights,) = call_whole(
        functools.partial(weights_kernel, prefactor),
        [shape_of((2, SLAB, CHANNELS), F32)],
        [],
        place,
        [mine],
    )
    fields, *products = call_whole(
        potential_kernel,
        [shape_of((TABLE, BLOCK), BF16)] + [values_shape] * SLABS,
        [pltpu.VMEM((TABLE, BLOCK), F32)],
        place,
        [weights, mine, other, near(table)],
    )
    arrived = spread_out(lambda shift: shifted(products[shift], shift), products[0], (2, 1, 3))
    own_atoms = pl.BlockSpec((BLOCK, CHANNELS), lambda step, place: (2 * place[0] + place[1], 0))
    own_labels = pl.BlockSpec((1, BLOCK), lambda step, place: (0, 2 * place[0] + place[1]))
    values_own, hidden_grad = call(
        middle_kernel,
        [values_block] * SLABS
        + [own_labels, own_atoms, own_atoms, matrices, matrices, gains_spec],
        (values_shape, shape_of((BLOCK, CHANNELS), BF16)),
        (values_block, whole((BLOCK, CHANNELS))),
        (
            place,
            *arrived,
            labels,
            atomic_descriptors,
            upstream_gradient,
            feature_to_latent_matrix,
            latent_to_feature_matrix,
            multiplier,
        ),
    )
    seconds = spread_out(lambda shift: shifted(values_own, SLABS - shift), values_own, LAST_FAR)
    values_two, keep, send = call_whole(
        second_kernel,
        [shape_of((BLOCK, atoms_here), BF16), pieces_shape, pieces_shape],
        [pltpu.VMEM((TABLE, BLOCK), F32)],
        place,
        [near(table), *seconds],
    )
    mine, other = sum_fields(add_halves(keep, send))
    result_shape = shape_of((CHANNELS + 16, BLOCK), BF16)
    result_spec = whole((CHANNELS + 16, BLOCK))
    results = call_whole(
        gradient_kernel,
        [result_shape] * SLABS,
        [
            pltpu.VMEM((TABLE, BLOCK), F32),
            pltpu.VMEM((TABLE, 2 * BLOCK), BF16),
            pltpu.VMEM((2 * BLOCK, atoms_here), BF16),
            pltpu.VMEM((SLAB, atoms_here), BF16),
            pltpu.VMEM((TABLE, BLOCK), BF16),
            pltpu.SemaphoreType.DMA((3,)),
        ],
        place,
        [weights, mine, other, near(table), far(fields), far(values_one), far(values_two)],
        spaces=[pltpu.VMEM] * 4 + [pltpu.HBM] * 3,
        micros=5,
    )
    arrived = spread_out(lambda shift: shifted(results[shift], shift), results[0], (2, 1, 3))
    return call(
        final_kernel,
        [result_spec] * SLABS
        + [own_labels, whole((BLOCK, CHANNELS)), matrices, gains_spec],
        (shape_of((BLOCK, CHANNELS), BF16), shape_of((3, BLOCK), F32)),
        (whole((BLOCK, CHANNELS)), whole((3, BLOCK))),
        (place, *arrived, labels, hidden_grad, feature_to_latent_matrix, multiplier),
    )


def solution(mesh):
    fine = Mesh(mesh.devices.reshape(SLABS, 2, 2, -1, 2), ("x", "yh", "yl", "z", "core"))
    atom, group = ("yl", "z", "core"), ("x", "yh")
    in_specs = (
        P(atom, None),
        P(None, atom),
        P(atom),
        P(None, group),
        P(),
        P(),
        P(),
        P(atom, None),
    )
    out_specs = (P(atom + group, None), P(None, atom + group))
    return jax.shard_map(
        per_device, mesh=fine, in_specs=in_specs, out_specs=out_specs, check_vma=False
    )
```

```python
import functools
import math

import jax
import jax.numpy as jnp
from jax import lax
from jax.experimental import pallas as pl
from jax.experimental.pallas import tpu as pltpu
from jax.sharding import Mesh
from jax.sharding import PartitionSpec as P

BOX_LENGTH = 100.0
GAUSSIAN_SIGMAS = (200.0, 100.0)
REACH = 8
SPAN = 2 * REACH + 1
CLASSES = (SPAN**3 + 1) // 2
SLABS = 4
SLAB = 640
STRIDE = -(-CLASSES // SLABS)
LAST_FAR = (2, 3, 1)
LEAP = REACH * SPAN
FIRST_ROWS = ((0, LEAP // 2 + 4), (LEAP // 2 + 4, LEAP))
COUNT_PIECE = 30
COUNT_ROW = 32
TABLE = 2 * SLAB
BLOCK = 256
CHANNELS = 128
ROWS = 40
PIECES = 32
VMEM_LIMIT = 14 * 1024 * 1024
BF16 = jnp.bfloat16
F32 = jnp.float32

COS_SERIES = (
    0.999999660315462,
    -19.739032161520388,
    64.93001235415629,
    -85.28515888817482,
    58.84788533073816,
    -21.15810679384873,
)
SIN_SERIES = (
    6.283183359037432,
    -41.341456424111435,
    81.59687947501621,
    -76.58597187733577,
    41.22756686823296,
    -12.302134397179453,
)


def class_vectors(first_class, shape, axis):
    label = (lax.broadcasted_iota(jnp.int32, shape, axis) + first_class).astype(F32)
    square = SPAN * SPAN
    first = jnp.floor((label + (square // 2 + 0.5)) * (1.0 / square))
    rest = label - square * first
    second = jnp.floor((rest + (REACH + 0.5)) * (1.0 / SPAN))
    return first, second, rest - SPAN * second


def matmul(left, right, left_dim, right_dim):
    return lax.dot_general(
        left, right, (((left_dim,), (right_dim,)), ((), ())), preferred_element_type=F32
    )


def flip(matrix):
    return jnp.transpose(matrix.astype(F32)).astype(BF16)


def gain_columns(multiplier, labels):
    species_count, channels = multiplier.shape
    padding = jnp.zeros((8 - species_count, channels), F32)
    columns = jnp.transpose(jnp.concatenate([multiplier, padding], axis=0))
    result = jnp.zeros((channels, labels.shape[1]), F32)
    for species in range(species_count):
        result = jnp.where(labels == species, columns[:, species : species + 1], result)
    return result


def series(coefficients, square):
    result = coefficients[-1] * square + coefficients[-2]
    for coefficient in coefficients[-3::-1]:
        result = result * square + coefficient
    return result


def cosine_and_sine(turns):
    turns = turns - jnp.floor(turns + 0.5)
    square = turns * turns
    return series(COS_SERIES, square), turns * series(SIN_SERIES, square)


def write_pieces(place, total_ref, keep_ref, send_ref):
    core = place[2]
    for target, half in ((keep_ref, core), (send_ref, 1 - core)):
        for index in range(PIECES):
            row, side = index // 2, index % 2
            start = pl.multiple_of(half * SLAB + row * ROWS, 8)
            target[index] = total_ref[
                pl.ds(start, ROWS), side * CHANNELS : (side + 1) * CHANNELS
            ].astype(BF16)


def weigh_pieces(pieces_ref, weights_ref, first, total_ref):
    for index in range(PIECES):
        row, side = index // 2, index % 2
        rows = slice(row * ROWS, (row + 1) * ROWS)
        total_ref[rows, side * CHANNELS : (side + 1) * CHANNELS] = (
            pieces_ref[index].astype(F32) * weights_ref[(first + side) % 2, rows]
        )


def half_rows(half):
    return pl.ds(pl.multiple_of(half * SLAB, SLAB), SLAB)


def slot(index):
    return slice(index * BLOCK, (index + 1) * BLOCK)


def tables_kernel(
    place,
    coordinates_hbm,
    labels_hbm,
    features_hbm,
    upstream_hbm,
    inward_hbm,
    outward_hbm,
    multiplier_hbm,
    table_ref,
    values_hbm,
    keep_ref,
    send_ref,
    values_ref,
    coordinates_ref,
    labels_ref,
    features_ref,
    upstream_ref,
    inward_ref,
    outward_ref,
    multiplier_ref,
    total_ref,
    cosine_ref,
    sine_ref,
    second_ref,
    arrivals,
):
    copies = [
        pltpu.make_async_copy(source, target, arrivals.at[index])
        for index, (source, target) in enumerate(
            (
                (coordinates_hbm, coordinates_ref),
                (labels_hbm, labels_ref),
                (features_hbm.at[:, place[1]], features_ref),
                (upstream_hbm.at[:, place[1]], upstream_ref),
                (inward_hbm, inward_ref),
                (outward_hbm, outward_ref),
                (multiplier_hbm, multiplier_ref),
            )
        )
    ]
    for copy in copies:
        copy.start()
    blocks = [lax.rem(place[0] + index, SLABS) for index in range(SLABS)]
    sides = [
        pl.ds(pl.multiple_of((2 * block + place[1]) * BLOCK + side * CHANNELS, CHANNELS), CHANNELS)
        for block in blocks
        for side in range(BLOCK // CHANNELS)
    ]
    first_vectors = [
        class_vectors(place[0] * STRIDE + start, (stop - start, CHANNELS), 0)
        for start, stop in FIRST_ROWS
    ]
    for start in range(0, SLAB - LEAP, LEAP):
        stop = min(start + LEAP, SLAB - LEAP)
        vectors = class_vectors(place[0] * STRIDE + start, (stop - start, CHANNELS), 0)
        second_ref[start:stop] = vectors[1]
    copies[0].wait()
    for index, side in enumerate(sides):
        columns = slice(index * CHANNELS, (index + 1) * CHANNELS)
        where = [coordinates_ref[axis : axis + 1, side] for axis in range(3)]
        for (start, stop), vectors in zip(FIRST_ROWS, first_vectors):
            turns = vectors[0] * where[0] + vectors[1] * where[1] + vectors[2] * where[2]
            cosine, sine = cosine_and_sine(turns)
            cosine_ref[start:stop, columns] = cosine
            sine_ref[start:stop, columns] = sine
            table_ref[start:stop, columns] = cosine.astype(BF16)
            table_ref[SLAB + start : SLAB + stop, columns] = sine.astype(BF16)
        plain = cosine_and_sine(REACH * where[1])
        carried = cosine_and_sine(where[0] - (REACH + 1) * where[1])
        for start in range(LEAP, SLAB, 72):
            stop = min(start + 72, SLAB)
            before = slice(start - LEAP, stop - LEAP)
            carry = second_ref[before] > 0.5
            turn_cosine = jnp.where(carry, carried[0], plain[0])
            turn_sine = jnp.where(carry, carried[1], plain[1])
            old_cosine, old_sine = cosine_ref[before, columns], sine_ref[before, columns]
            cosine = old_cosine * turn_cosine - old_sine * turn_sine
            sine = old_sine * turn_cosine + old_cosine * turn_sine
            cosine_ref[start:stop, columns] = cosine
            sine_ref[start:stop, columns] = sine
            table_ref[start:stop, columns] = cosine.astype(BF16)
            table_ref[SLAB + start : SLAB + stop, columns] = sine.astype(BF16)
    for copy in copies[1:]:
        copy.wait()
    inward = flip(inward_ref[0])
    for index, block in enumerate(blocks):
        labels = labels_ref[:, pl.ds(pl.multiple_of((2 * block + place[1]) * BLOCK, BLOCK), BLOCK)]
        gains = gain_columns(multiplier_ref[:, 0, :], labels)
        charges = matmul(inward, features_ref[block], 1, 1) * gains
        grad_pot = matmul(outward_ref[1], upstream_ref[block], 1, 1)
        values_ref[:CHANNELS, slot(index)] = charges.astype(BF16)
        values_ref[CHANNELS:, slot(index)] = grad_pot.astype(BF16)
    leaving = pltpu.make_async_copy(values_ref, values_hbm, arrivals.at[len(copies)])
    leaving.start()
    total_ref[...] = matmul(table_ref[...], values_ref[...], 1, 1)
    for half in range(2):
        total_ref[(half + 1) * SLAB - 8 : (half + 1) * SLAB, :CHANNELS] = jnp.zeros((8, CHANNELS), F32)
    write_pieces(place, total_ref, keep_ref, send_ref)
    leaving.wait()


def counts_kernel(copies, place, momenta_ref, counts_ref):
    momenta = momenta_ref[...].astype(F32)
    label = jnp.abs(
        momenta[0:1] * float(SPAN * SPAN) + momenta[1:2] * float(SPAN) + momenta[2:3]
    ) - (place[0] * STRIDE).astype(F32)
    column = jnp.transpose(jnp.broadcast_to(label, (8, label.shape[1])))[:, 0:1]
    column = jnp.broadcast_to(column, (column.shape[0], CHANNELS))
    lane = lax.broadcasted_iota(jnp.int32, column.shape, 1).astype(F32)
    counts_ref[...] = jnp.zeros(counts_ref.shape, BF16)
    rows = []
    for start in range(0, SLAB, CHANNELS):
        here = (column == lane + float(start)) & (lane < float(STRIDE - start))
        rows.append(jnp.sum(jnp.where(here, 1.0 / copies, 0.0), axis=0, keepdims=True))
    rows.append(jnp.zeros((8 - len(rows), CHANNELS), F32))
    counts_ref[COUNT_PIECE, COUNT_ROW:, :] = jnp.concatenate(rows, axis=0).astype(BF16)


def write_fields(total_ref, fields_ref):
    fields_ref[:, :CHANNELS] = total_ref[:, CHANNELS:].astype(BF16)
    fields_ref[:, CHANNELS:] = total_ref[:, :CHANNELS].astype(BF16)


def first_potential_kernel(
    prefactor,
    place,
    mine_ref,
    table_ref,
    weights_ref,
    fields_hbm,
    potential_ref,
    total_ref,
    fields_ref,
    leaves,
):
    counts = jnp.transpose(mine_ref[COUNT_PIECE, COUNT_ROW:, :].astype(F32))
    for index in range(SLAB // CHANNELS):
        start = index * CHANNELS
        count = counts[:, index : index + 1]
        vectors = class_vectors(place[0] * STRIDE + start, (CHANNELS, CHANNELS), 0)
        norm = vectors[0] * vectors[0] + vectors[1] * vectors[1] + vectors[2] * vectors[2]
        for block, spread in enumerate(GAUSSIAN_SIGMAS):
            weights_ref[block, start : start + CHANNELS, :] = count * (
                prefactor * jnp.exp(norm * (-1.0 / spread))
            )
    weigh_pieces(mine_ref, weights_ref, 0, total_ref)
    write_fields(total_ref, fields_ref)
    leaving = pltpu.make_async_copy(fields_ref, fields_hbm, leaves)
    leaving.start()
    flipped = jnp.transpose(total_ref[...]).astype(BF16)
    potential_ref[...] = matmul(flipped, table_ref[half_rows(place[2]), :], 1, 0)
    leaving.wait()


def potential_kernel(
    place, weights_ref, other_ref, table_ref, before_ref, fields_ref, flipped_ref, p2, p1, p3, total_ref
):
    weigh_pieces(other_ref, weights_ref, 0, total_ref)
    write_fields(total_ref, fields_ref)
    flipped_ref[...] = jnp.transpose(total_ref[...]).astype(BF16)
    for index, target in ((2, p2), (1, p1), (3, p3)):
        rest = matmul(flipped_ref[...], table_ref[half_rows(1 - place[2]), slot(index)], 1, 0)
        target[...] = (before_ref[:, slot(index)] + rest).astype(BF16)


def own_potential_kernel(place, table_ref, before_ref, flipped_ref, p0):
    rest = matmul(flipped_ref[...], table_ref[half_rows(1 - place[2]), slot(0)], 1, 0)
    p0[...] = (before_ref[:, slot(0)] + rest).astype(BF16)


def own_atoms_kernel(
    place,
    labels_ref,
    features_ref,
    upstream_ref,
    inward_ref,
    multiplier_ref,
    own_features_ref,
    own_upstream_ref,
    gains_one_ref,
    gains_two_ref,
    flipped_ref,
):
    own_features_ref[...] = features_ref[...]
    own_upstream_ref[...] = upstream_ref[...]
    gains_one_ref[...] = jnp.transpose(gain_columns(multiplier_ref[:, 0, :], labels_ref[...]))
    gains_two_ref[...] = gain_columns(multiplier_ref[:, 1, :], labels_ref[...])
    for block in range(2):
        flipped_ref[block] = flip(inward_ref[block])


def middle_kernel(
    place,
    q0,
    q1,
    q2,
    q3,
    features_ref,
    upstream_ref,
    gains_ref,
    flipped_ref,
    outward_ref,
    values_ref,
    hidden_grad_ref,
):
    total = (q0[...].astype(F32) + q1[...].astype(F32)) + (q2[...].astype(F32) + q3[...].astype(F32))
    grad_charge = total[CHANNELS:]
    scaled = jnp.transpose(grad_charge * gains_ref[...]).astype(BF16)
    hidden_grad = (
        upstream_ref[...].astype(F32) + matmul(scaled, flipped_ref[1], 1, 0)
    ).astype(BF16)
    hidden_grad_ref[...] = hidden_grad
    values_ref[CHANNELS:] = matmul(outward_ref[0], hidden_grad, 1, 1).astype(BF16)
    potential = jnp.transpose(total[:CHANNELS]).astype(BF16)
    hidden = (features_ref[...].astype(F32) + matmul(potential, outward_ref[0], 1, 0)).astype(BF16)
    values_ref[:CHANNELS] = (matmul(flipped_ref[1], hidden, 1, 1) * gains_ref[...]).astype(BF16)


def second_kernel(place, table_ref, v0, v1, v2, v3, values_ref, keep_ref, send_ref, total_ref):
    for index, source in zip((0, *LAST_FAR), (v0, v1, v2, v3)):
        values_ref[:, slot(index)] = source[...]
    total_ref[...] = matmul(table_ref[...], values_ref[...], 1, 1)
    write_pieces(place, total_ref, keep_ref, send_ref)


def half_theta(half, table_ref, columns, pairs, values):
    sign = (2 * half - 1).astype(F32)
    along = matmul(pairs, values, 1, 0)
    return (sign * table_ref[half_rows(1 - half), columns].astype(F32)) * along


def write_pairs(total_ref, fields_ref, pairs_ref):
    pairs_ref[:, :CHANNELS] = total_ref[:, CHANNELS:].astype(BF16)
    pairs_ref[:, CHANNELS : 2 * CHANNELS] = total_ref[:, :CHANNELS].astype(BF16)
    pairs_ref[:, 2 * CHANNELS :] = fields_ref[...]


def first_gradient_kernel(
    place,
    weights_ref,
    mine_ref,
    table_ref,
    fields_hbm,
    first_hbm,
    second_hbm,
    values_ref,
    theta_ref,
    charge_ref,
    total_ref,
    pairs_ref,
    fields_ref,
    arrivals,
):
    copies = [
        pltpu.make_async_copy(source, target, arrivals.at[index])
        for index, (source, target) in enumerate(
            (
                (fields_hbm, fields_ref),
                (first_hbm, values_ref.at[:BLOCK]),
                (second_hbm, values_ref.at[BLOCK:]),
            )
        )
    ]
    for copy in copies:
        copy.start()
    weigh_pieces(mine_ref, weights_ref, 1, total_ref)
    flipped = jnp.transpose(total_ref[:, CHANNELS:]).astype(BF16)
    charge_ref[...] = matmul(flipped, table_ref[half_rows(place[2]), :], 1, 0)
    for copy in copies:
        copy.wait()
    write_pairs(total_ref, fields_ref, pairs_ref)
    for index in range(SLABS):
        columns = slot(index)
        theta_ref[:, columns] = half_theta(
            place[2], table_ref, columns, pairs_ref[...], values_ref[:, columns]
        )


def finish_gradient(
    index, place, table_ref, pairs_ref, flipped_ref, values_ref, theta_ref, charge_ref, directions, target
):
    columns = slot(index)
    theta = half_theta(1 - place[2], table_ref, columns, pairs_ref[...], values_ref[:, columns])
    charge = matmul(flipped_ref[...], table_ref[half_rows(1 - place[2]), columns], 1, 0)
    position = matmul(directions, (theta + theta_ref[:, columns]).astype(BF16), 1, 0)
    target[:CHANNELS] = (charge + charge_ref[:, columns]).astype(BF16)
    target[CHANNELS:] = (position * (2.0 * math.pi / BOX_LENGTH)).astype(BF16)


def class_directions(place):
    vectors = class_vectors(place[0] * STRIDE, (16, SLAB), 1)
    row = lax.broadcasted_iota(jnp.int32, (16, SLAB), 0)
    directions = jnp.where(row == 0, vectors[0], jnp.where(row == 1, vectors[1], vectors[2]))
    return jnp.where(row < 3, directions, 0.0).astype(BF16)


def gradient_kernel(
    place,
    weights_ref,
    other_ref,
    table_ref,
    fields_ref,
    values_ref,
    theta_ref,
    charge_ref,
    pairs_ref,
    flipped_ref,
    o2,
    o1,
    o3,
    total_ref,
):
    weigh_pieces(other_ref, weights_ref, 1, total_ref)
    write_pairs(total_ref, fields_ref, pairs_ref)
    flipped_ref[...] = jnp.transpose(total_ref[:, CHANNELS:]).astype(BF16)
    directions = class_directions(place)
    rest = (place, table_ref, pairs_ref, flipped_ref, values_ref, theta_ref, charge_ref, directions)
    for index, target in ((2, o2), (1, o1), (3, o3)):
        finish_gradient(index, *rest, target)


def own_gradient_kernel(
    place, table_ref, pairs_ref, flipped_ref, values_ref, theta_ref, charge_ref, o0
):
    rest = (place, table_ref, pairs_ref, flipped_ref, values_ref, theta_ref, charge_ref)
    finish_gradient(0, *rest, class_directions(place), o0)


def sum_kernel(place, parts_ref, spread_ref):
    total = parts_ref[0].astype(F32)
    for index in range(1, PIECES):
        total += parts_ref[index].astype(F32)
    total = total.astype(BF16)
    for index in range(PIECES):
        spread_ref[index] = total


def final_kernel(
    place, q0, q1, q2, q3, gains_ref, hidden_grad_ref, flipped_ref, features_ref, positions_ref
):
    total = (q0[...].astype(F32) + q1[...].astype(F32)) + (q2[...].astype(F32) + q3[...].astype(F32))
    scaled = (jnp.transpose(total[:CHANNELS]) * gains_ref[...]).astype(BF16)
    features_ref[...] = (
        hidden_grad_ref[...].astype(F32) + matmul(scaled, flipped_ref[0], 1, 0)
    ).astype(BF16)
    positions_ref[...] = total[CHANNELS : CHANNELS + 3]


def shape_of(shape, dtype):
    return jax.ShapeDtypeStruct(shape, dtype)


def far(value):
    return pltpu.with_memory_space_constraint(value, pltpu.HBM)


def near(value):
    return pltpu.with_memory_space_constraint(value, pltpu.VMEM)


def whole(shape):
    return pl.BlockSpec(shape, lambda step, place: (0,) * len(shape))


def compiler(micros):
    return dict(
        compiler_params=pltpu.CompilerParams(vmem_limit_bytes=VMEM_LIMIT),
        cost_estimate=pl.CostEstimate(
            flops=int(micros * 10**9), bytes_accessed=int(micros * 10**6), transcendentals=0
        ),
    )


def call(kernel, in_specs, outs, out_specs, operands, micros=2):
    return pl.pallas_call(
        kernel,
        grid_spec=pltpu.PrefetchScalarGridSpec(
            num_scalar_prefetch=1, grid=(1,), in_specs=in_specs, out_specs=out_specs
        ),
        out_shape=outs,
        **compiler(micros),
    )(*operands)


def call_whole(kernel, outs, scratch, place, operands, spaces=None, out_spaces=None, micros=2):
    spaces = spaces or [pltpu.VMEM] * len(operands)
    out_spaces = out_spaces or [pltpu.VMEM] * len(outs)
    return pl.pallas_call(
        kernel,
        in_specs=[pl.BlockSpec(memory_space=pltpu.SMEM)]
        + [pl.BlockSpec(memory_space=space) for space in spaces],
        out_specs=[pl.BlockSpec(memory_space=space) for space in out_spaces],
        out_shape=outs,
        scratch_shapes=scratch,
        **compiler(micros),
    )(place, *operands)


ATOM_REST = ("yh", "yl", "z")


def shifted(value, shift):
    return lax.ppermute(value, "x", [(i, (i + shift) % SLABS) for i in range(SLABS)])


def spread_out(send, own, order):
    return [own] + [send(shift) for shift in order]


def swapped(value):
    return lax.ppermute(value, "core", [(0, 1), (1, 0)])


def add_halves(keep, send, *more):
    total = keep.astype(F32) + swapped(send).astype(F32)
    for value in more:
        total = total + value.astype(F32)
    return total.astype(BF16)


def sum_fields(place, part):
    parts = lax.all_to_all(part, ATOM_REST, 0, 0, tiled=True)
    if place is None:
        total = jnp.sum(parts.astype(F32), axis=0).astype(BF16)
        spread = jnp.broadcast_to(total[None], parts.shape)
    else:
        (spread,) = call_whole(
            sum_kernel, [pltpu.VMEM(parts.shape, BF16)], [], place, [near(parts)], micros=1
        )
    mine = lax.all_to_all(spread, ATOM_REST, 0, 0, tiled=True)
    return mine, swapped(mine)


def per_device(
    atomic_descriptors,
    unit_cell_coordinates,
    element_labels,
    lattice_momenta,
    feature_to_latent_matrix,
    latent_to_feature_matrix,
    element_latent_multiplier,
    upstream_gradient,
):
    place = jnp.stack(
        [lax.axis_index("x"), lax.axis_index("yh"), lax.axis_index("core")]
    ).astype(jnp.int32)
    prefactor = 1.0 / math.sqrt(
        atomic_descriptors.shape[0]
        * lattice_momenta.shape[1]
        * lax.axis_size(("x", "yh", "yl", "z", "core"))
    )
    labels = element_labels[None, :]
    multiplier = jnp.swapaxes(element_latent_multiplier, 0, 1)
    lengths = {axis: lax.axis_size(axis) for axis in ("x", "yl", "z")}
    copies = lengths["yl"] * lengths["z"] // SLABS
    pairs = []
    for yl in range(lengths["yl"]):
        for z in range(lengths["z"]):
            for x in range(SLABS):
                place_of = lambda x: (x * lengths["yl"] + yl) * lengths["z"] + z
                pairs.append((place_of((x + 2 * (z % 2) + yl) % SLABS), place_of(x)))
    fetched = lax.ppermute(lattice_momenta, ("x", "yl", "z"), pairs)

    matrices = whole((2, CHANNELS, CHANNELS))
    gains_spec = whole(multiplier.shape)
    pieces_shape = shape_of((PIECES, ROWS, CHANNELS), BF16)
    values_block = whole((BLOCK, BLOCK))
    values_shape = shape_of((BLOCK, BLOCK), BF16)
    atoms_here = SLABS * BLOCK

    blocked = (SLABS, 2, BLOCK, CHANNELS)
    operands = [
        unit_cell_coordinates,
        labels,
        atomic_descriptors.reshape(blocked),
        upstream_gradient.reshape(blocked),
        feature_to_latent_matrix,
        latent_to_feature_matrix,
        multiplier,
    ]
    local = [shape_of(value.shape, value.dtype) for value in operands]
    local[2] = local[3] = shape_of((SLABS, BLOCK, CHANNELS), BF16)
    table, values_one, keep, send = call_whole(
        tables_kernel,
        (
            pltpu.VMEM((TABLE, atoms_here), BF16),
            pltpu.HBM((BLOCK, atoms_here), BF16),
            pieces_shape,
            pieces_shape,
        ),
        [pltpu.VMEM((BLOCK, atoms_here), BF16)]
        + [pltpu.VMEM(value.shape, value.dtype) for value in local]
        + [
            pltpu.VMEM((TABLE, BLOCK), F32),
            pltpu.VMEM((SLAB, atoms_here), F32),
            pltpu.VMEM((SLAB, atoms_here), F32),
            pltpu.VMEM((SLAB - LEAP, CHANNELS), F32),
            pltpu.SemaphoreType.DMA((len(operands) + 1,)),
        ],
        place,
        [far(value) for value in operands],
        spaces=[pltpu.HBM] * len(operands),
        out_spaces=[pltpu.VMEM, pltpu.HBM, pltpu.VMEM, pltpu.VMEM],
        micros=7,
    )
    (counts,) = call_whole(
        functools.partial(counts_kernel, float(copies)), [pieces_shape], [], place, [fetched]
    )
    part = add_halves(keep, send, counts)
    mine, other = sum_fields(None, part)
    half = (SLAB, BLOCK)
    weights, fields_mine, before = call_whole(
        functools.partial(first_potential_kernel, prefactor),
        [
            shape_of((2, SLAB, CHANNELS), F32),
            pltpu.HBM(half, BF16),
            shape_of((BLOCK, atoms_here), F32),
        ],
        [pltpu.VMEM(half, F32), pltpu.VMEM(half, BF16), pltpu.SemaphoreType.DMA],
        place,
        [mine, near(table)],
        out_spaces=[pltpu.VMEM, pltpu.HBM, pltpu.VMEM],
    )
    fields_other, flipped, p2, p1, p3 = call_whole(
        potential_kernel,
        [shape_of(half, BF16), shape_of((BLOCK, SLAB), BF16)] + [values_shape] * 3,
        [pltpu.VMEM(half, F32)],
        place,
        [weights, other, near(table), before],
    )
    (p0,) = call_whole(
        own_potential_kernel,
        [values_shape],
        [],
        place,
        [near(table), before, flipped],
        micros=0.1,
    )
    own_atoms = pl.BlockSpec((BLOCK, CHANNELS), lambda step, place: (2 * place[0] + place[1], 0))
    own_labels = pl.BlockSpec((1, BLOCK), lambda step, place: (0, 2 * place[0] + place[1]))
    own_block = (BLOCK, CHANNELS)
    labels, p0 = lax.optimization_barrier((labels, p0))
    products = (p0, p1, p2, p3)
    arrived = spread_out(lambda shift: shifted(products[shift], shift), products[0], (2, 1, 3))
    own_features, own_upstream, gains_one, gains_two, inward_flipped = call(
        own_atoms_kernel,
        [own_labels, own_atoms, own_atoms, matrices, gains_spec],
        (
            shape_of(own_block, BF16),
            shape_of(own_block, BF16),
            shape_of(own_block, F32),
            shape_of((CHANNELS, BLOCK), F32),
            shape_of((2, CHANNELS, CHANNELS), BF16),
        ),
        (
            whole(own_block),
            whole(own_block),
            whole(own_block),
            whole((CHANNELS, BLOCK)),
            matrices,
        ),
        (
            place,
            labels,
            atomic_descriptors,
            upstream_gradient,
            feature_to_latent_matrix,
            multiplier,
        ),
        micros=0.1,
    )
    values_own, hidden_grad = call_whole(
        middle_kernel,
        [values_shape, shape_of(own_block, BF16)],
        [],
        place,
        [*arrived, own_features, own_upstream, gains_two, inward_flipped, latent_to_feature_matrix],
    )
    seconds = spread_out(lambda shift: shifted(values_own, SLABS - shift), values_own, LAST_FAR)
    values_two, keep, send = call_whole(
        second_kernel,
        [shape_of((BLOCK, atoms_here), BF16), pieces_shape, pieces_shape],
        [pltpu.VMEM((TABLE, BLOCK), F32)],
        place,
        [near(table), *seconds],
    )
    mine, other = sum_fields(place, add_halves(keep, send))
    result_shape = shape_of((CHANNELS + 16, BLOCK), BF16)
    result_spec = whole((CHANNELS + 16, BLOCK))
    values, theta, charge = call_whole(
        first_gradient_kernel,
        [
            shape_of((2 * BLOCK, atoms_here), BF16),
            shape_of((SLAB, atoms_here), F32),
            shape_of((CHANNELS, atoms_here), F32),
        ],
        [
            pltpu.VMEM(half, F32),
            pltpu.VMEM((SLAB, 2 * BLOCK), BF16),
            pltpu.VMEM(half, BF16),
            pltpu.SemaphoreType.DMA((3,)),
        ],
        place,
        [weights, mine, near(table), far(fields_mine), far(values_one), far(values_two)],
        spaces=[pltpu.VMEM] * 3 + [pltpu.HBM] * 3,
    )
    pairs, flipped, o2, o1, o3 = call_whole(
        gradient_kernel,
        [shape_of((SLAB, 2 * BLOCK), BF16), shape_of((CHANNELS, SLAB), BF16)] + [result_shape] * 3,
        [pltpu.VMEM(half, F32)],
        place,
        [weights, other, near(table), fields_other, values, theta, charge],
    )
    (o0,) = call_whole(
        own_gradient_kernel,
        [result_shape],
        [],
        place,
        [near(table), pairs, flipped, values, theta, charge],
        micros=0.1,
    )
    results = (o0, o1, o2, o3)
    arrived = spread_out(lambda shift: shifted(results[shift], shift), results[0], (2, 1, 3))
    return tuple(
        call_whole(
            final_kernel,
            [shape_of(own_block, BF16), shape_of((3, BLOCK), F32)],
            [],
            place,
            [*arrived, gains_one, hidden_grad, inward_flipped],
        )
    )


def solution(mesh):
    fine = Mesh(mesh.devices.reshape(SLABS, 2, 2, -1, 2), ("x", "yh", "yl", "z", "core"))
    atom, group = ("yl", "z", "core"), ("x", "yh")
    in_specs = (
        P(atom, None),
        P(None, atom),
        P(atom),
        P(None, group),
        P(),
        P(),
        P(),
        P(atom, None),
    )
    out_specs = (P(atom + group, None), P(None, atom + group))
    return jax.shard_map(
        per_device, mesh=fine, in_specs=in_specs, out_specs=out_specs, check_vma=False
    )
```

```python
import functools
import math

import jax
import jax.numpy as jnp
from jax import lax
from jax.experimental import pallas as pl
from jax.experimental.pallas import tpu as pltpu
from jax.sharding import Mesh
from jax.sharding import PartitionSpec as P

BOX_LENGTH = 100.0
GAUSSIAN_SIGMAS = (200.0, 100.0)
REACH = 8
SPAN = 2 * REACH + 1
CLASSES = (SPAN**3 + 1) // 2
SLABS = 4
SLAB = 640
STRIDE = -(-CLASSES // SLABS)
LAST_FAR = (2, 3, 1)
LEAP = REACH * SPAN
FIRST_ROWS = ((0, LEAP // 2 + 4), (LEAP // 2 + 4, LEAP))
COUNT_PIECE = 30
COUNT_ROW = 32
TABLE = 2 * SLAB
BLOCK = 256
CHANNELS = 128
ROWS = 40
PIECES = 32
VMEM_LIMIT = 14 * 1024 * 1024
BF16 = jnp.bfloat16
F32 = jnp.float32

COS_SERIES = (
    0.999999660315462,
    -19.739032161520388,
    64.93001235415629,
    -85.28515888817482,
    58.84788533073816,
    -21.15810679384873,
)
SIN_SERIES = (
    6.283183359037432,
    -41.341456424111435,
    81.59687947501621,
    -76.58597187733577,
    41.22756686823296,
    -12.302134397179453,
)


def class_vectors(first_class, shape, axis):
    label = (lax.broadcasted_iota(jnp.int32, shape, axis) + first_class).astype(F32)
    square = SPAN * SPAN
    first = jnp.floor((label + (square // 2 + 0.5)) * (1.0 / square))
    rest = label - square * first
    second = jnp.floor((rest + (REACH + 0.5)) * (1.0 / SPAN))
    return first, second, rest - SPAN * second


def matmul(left, right, left_dim, right_dim):
    return lax.dot_general(
        left, right, (((left_dim,), (right_dim,)), ((), ())), preferred_element_type=F32
    )


def flip(matrix):
    return jnp.transpose(matrix.astype(F32)).astype(BF16)


def gain_columns(multiplier, labels):
    species_count, channels = multiplier.shape
    padding = jnp.zeros((8 - species_count, channels), F32)
    columns = jnp.transpose(jnp.concatenate([multiplier, padding], axis=0))
    result = jnp.zeros((channels, labels.shape[1]), F32)
    for species in range(species_count):
        result = jnp.where(labels == species, columns[:, species : species + 1], result)
    return result


def series(coefficients, square):
    result = coefficients[-1] * square + coefficients[-2]
    for coefficient in coefficients[-3::-1]:
        result = result * square + coefficient
    return result


def cosine_and_sine(turns):
    turns = turns - jnp.floor(turns + 0.5)
    square = turns * turns
    return series(COS_SERIES, square), turns * series(SIN_SERIES, square)


def write_half(half, table_ref, values_ref, pieces_ref, total_ref):
    total_ref[...] = matmul(table_ref[half_rows(half), :], values_ref[...], 1, 1)
    total_ref[SLAB - 8 :, :CHANNELS] = jnp.zeros((8, CHANNELS), F32)
    for index in range(PIECES):
        row, side = index // 2, index % 2
        pieces_ref[index] = total_ref[
            row * ROWS : (row + 1) * ROWS, side * CHANNELS : (side + 1) * CHANNELS
        ].astype(BF16)


def keep_kernel(place, table_ref, values_ref, keep_ref, total_ref):
    write_half(place[2], table_ref, values_ref, keep_ref, total_ref)


def weigh_pieces(pieces_ref, weights_ref, first, total_ref):
    for index in range(PIECES):
        row, side = index // 2, index % 2
        rows = slice(row * ROWS, (row + 1) * ROWS)
        total_ref[rows, side * CHANNELS : (side + 1) * CHANNELS] = (
            pieces_ref[index].astype(F32) * weights_ref[(first + side) % 2, rows]
        )


def half_rows(half):
    return pl.ds(pl.multiple_of(half * SLAB, SLAB), SLAB)


def slot(index):
    return slice(index * BLOCK, (index + 1) * BLOCK)


def tables_kernel(
    place,
    coordinates_hbm,
    labels_hbm,
    features_hbm,
    upstream_hbm,
    inward_hbm,
    outward_hbm,
    multiplier_hbm,
    table_ref,
    keep_ref,
    send_ref,
    coordinates_ref,
    labels_ref,
    features_ref,
    upstream_ref,
    inward_ref,
    outward_ref,
    multiplier_ref,
    total_ref,
    cosine_ref,
    sine_ref,
    second_ref,
    arrivals,
):
    copies = [
        pltpu.make_async_copy(source, target, arrivals.at[index])
        for index, (source, target) in enumerate(
            (
                (coordinates_hbm, coordinates_ref),
                (labels_hbm, labels_ref),
                (features_hbm.at[:, place[1]], features_ref),
                (upstream_hbm.at[:, place[1]], upstream_ref),
                (inward_hbm, inward_ref),
                (outward_hbm, outward_ref),
                (multiplier_hbm, multiplier_ref),
            )
        )
    ]
    for copy in copies:
        copy.start()
    blocks = [lax.rem(place[0] + index, SLABS) for index in range(SLABS)]
    sides = [
        pl.ds(pl.multiple_of((2 * block + place[1]) * BLOCK + side * CHANNELS, CHANNELS), CHANNELS)
        for block in blocks
        for side in range(BLOCK // CHANNELS)
    ]
    first_vectors = [
        class_vectors(place[0] * STRIDE + start, (stop - start, CHANNELS), 0)
        for start, stop in FIRST_ROWS
    ]
    for start in range(0, SLAB - LEAP, LEAP):
        stop = min(start + LEAP, SLAB - LEAP)
        vectors = class_vectors(place[0] * STRIDE + start, (stop - start, CHANNELS), 0)
        second_ref[start:stop] = vectors[1]
    copies[0].wait()
    for index, side in enumerate(sides):
        columns = slice(index * CHANNELS, (index + 1) * CHANNELS)
        where = [coordinates_ref[axis : axis + 1, side] for axis in range(3)]
        for (start, stop), vectors in zip(FIRST_ROWS, first_vectors):
            turns = vectors[0] * where[0] + vectors[1] * where[1] + vectors[2] * where[2]
            cosine, sine = cosine_and_sine(turns)
            cosine_ref[start:stop, columns] = cosine
            sine_ref[start:stop, columns] = sine
            table_ref[start:stop, columns] = cosine.astype(BF16)
            table_ref[SLAB + start : SLAB + stop, columns] = sine.astype(BF16)
        plain = cosine_and_sine(REACH * where[1])
        carried = cosine_and_sine(where[0] - (REACH + 1) * where[1])
        for start in range(LEAP, SLAB, 72):
            stop = min(start + 72, SLAB)
            before = slice(start - LEAP, stop - LEAP)
            carry = second_ref[before] > 0.5
            turn_cosine = jnp.where(carry, carried[0], plain[0])
            turn_sine = jnp.where(carry, carried[1], plain[1])
            old_cosine, old_sine = cosine_ref[before, columns], sine_ref[before, columns]
            cosine = old_cosine * turn_cosine - old_sine * turn_sine
            sine = old_sine * turn_cosine + old_cosine * turn_sine
            cosine_ref[start:stop, columns] = cosine
            sine_ref[start:stop, columns] = sine
            table_ref[start:stop, columns] = cosine.astype(BF16)
            table_ref[SLAB + start : SLAB + stop, columns] = sine.astype(BF16)
    for copy in copies[1:]:
        copy.wait()
    atoms = (SLABS * BLOCK, CHANNELS)
    charges = matmul(flip(inward_ref[0]), features_ref[...].reshape(atoms), 1, 1)
    grad_pot = matmul(outward_ref[1], upstream_ref[...].reshape(atoms), 1, 1).astype(BF16)
    for block in range(SLABS):
        labels = labels_ref[:, pl.ds(pl.multiple_of((2 * block + place[1]) * BLOCK, BLOCK), BLOCK)]
        gains = gain_columns(multiplier_ref[:, 0, :], labels)
        target = lax.rem(block - place[0] + SLABS, SLABS)
        columns = pl.ds(pl.multiple_of(target * BLOCK, BLOCK), BLOCK)
        table_ref[TABLE : TABLE + CHANNELS, columns] = (charges[:, slot(block)] * gains).astype(BF16)
        table_ref[TABLE + CHANNELS :, columns] = grad_pot[:, slot(block)]
    values_ref = table_ref.at[TABLE:]
    write_half(1 - place[2], table_ref, values_ref, send_ref, total_ref)
    write_half(place[2], table_ref, values_ref, keep_ref, total_ref)


def counts_kernel(copies, place, momenta_ref, counts_ref):
    momenta = momenta_ref[...].astype(F32)
    label = jnp.abs(
        momenta[0:1] * float(SPAN * SPAN) + momenta[1:2] * float(SPAN) + momenta[2:3]
    ) - (place[0] * STRIDE).astype(F32)
    column = jnp.transpose(jnp.broadcast_to(label, (8, label.shape[1])))[:, 0:1]
    column = jnp.broadcast_to(column, (column.shape[0], CHANNELS))
    lane = lax.broadcasted_iota(jnp.int32, column.shape, 1).astype(F32)
    counts_ref[...] = jnp.zeros(counts_ref.shape, BF16)
    rows = []
    for start in range(0, SLAB, CHANNELS):
        here = (column == lane + float(start)) & (lane < float(STRIDE - start))
        rows.append(jnp.sum(jnp.where(here, 1.0 / copies, 0.0), axis=0, keepdims=True))
    rows.append(jnp.zeros((8 - len(rows), CHANNELS), F32))
    counts_ref[COUNT_PIECE, COUNT_ROW:, :] = jnp.concatenate(rows, axis=0).astype(BF16)


def write_fields(total_ref, fields_ref):
    fields_ref[:, :CHANNELS] = total_ref[:, CHANNELS:].astype(BF16)
    fields_ref[:, CHANNELS:] = total_ref[:, :CHANNELS].astype(BF16)


def first_potential_kernel(
    prefactor,
    place,
    mine_ref,
    table_ref,
    weights_ref,
    fields_hbm,
    potential_ref,
    total_ref,
    fields_ref,
    leaves,
):
    counts = jnp.transpose(mine_ref[COUNT_PIECE, COUNT_ROW:, :].astype(F32))
    for index in range(SLAB // CHANNELS):
        start = index * CHANNELS
        count = counts[:, index : index + 1]
        vectors = class_vectors(place[0] * STRIDE + start, (CHANNELS, CHANNELS), 0)
        norm = vectors[0] * vectors[0] + vectors[1] * vectors[1] + vectors[2] * vectors[2]
        for block, spread in enumerate(GAUSSIAN_SIGMAS):
            weights_ref[block, start : start + CHANNELS, :] = count * (
                prefactor * jnp.exp(norm * (-1.0 / spread))
            )
    weigh_pieces(mine_ref, weights_ref, 0, total_ref)
    write_fields(total_ref, fields_ref)
    leaving = pltpu.make_async_copy(fields_ref, fields_hbm, leaves)
    leaving.start()
    flipped = jnp.transpose(total_ref[...]).astype(BF16)
    potential_ref[...] = matmul(flipped, table_ref[half_rows(place[2]), :], 1, 0)
    leaving.wait()


def potential_kernel(
    place, weights_ref, other_ref, table_ref, before_ref, fields_ref, flipped_ref, p2, p1, p3, total_ref
):
    weigh_pieces(other_ref, weights_ref, 0, total_ref)
    write_fields(total_ref, fields_ref)
    flipped_ref[...] = jnp.transpose(total_ref[...]).astype(BF16)
    for index, target in ((2, p2), (1, p1), (3, p3)):
        rest = matmul(flipped_ref[...], table_ref[half_rows(1 - place[2]), slot(index)], 1, 0)
        target[...] = (before_ref[:, slot(index)] + rest).astype(BF16)


def own_potential_kernel(place, table_ref, before_ref, flipped_ref, p0):
    rest = matmul(flipped_ref[...], table_ref[half_rows(1 - place[2]), slot(0)], 1, 0)
    p0[...] = (before_ref[:, slot(0)] + rest).astype(BF16)


def own_atoms_kernel(
    place,
    labels_ref,
    features_ref,
    upstream_ref,
    inward_ref,
    multiplier_ref,
    own_features_ref,
    own_upstream_ref,
    gains_one_ref,
    gains_two_ref,
    flipped_ref,
):
    own_features_ref[...] = features_ref[...]
    own_upstream_ref[...] = upstream_ref[...]
    gains_one_ref[...] = jnp.transpose(gain_columns(multiplier_ref[:, 0, :], labels_ref[...]))
    gains_two_ref[...] = gain_columns(multiplier_ref[:, 1, :], labels_ref[...])
    for block in range(2):
        flipped_ref[block] = flip(inward_ref[block])


def middle_kernel(
    place,
    q0,
    q1,
    q2,
    q3,
    features_ref,
    upstream_ref,
    gains_ref,
    flipped_ref,
    outward_ref,
    values_ref,
    hidden_grad_ref,
):
    total = (q0[...].astype(F32) + q1[...].astype(F32)) + (q2[...].astype(F32) + q3[...].astype(F32))
    grad_charge = total[CHANNELS:]
    scaled = jnp.transpose(grad_charge * gains_ref[...]).astype(BF16)
    hidden_grad = (
        upstream_ref[...].astype(F32) + matmul(scaled, flipped_ref[1], 1, 0)
    ).astype(BF16)
    hidden_grad_ref[...] = hidden_grad
    values_ref[CHANNELS:] = matmul(outward_ref[0], hidden_grad, 1, 1).astype(BF16)
    potential = jnp.transpose(total[:CHANNELS]).astype(BF16)
    hidden = (features_ref[...].astype(F32) + matmul(potential, outward_ref[0], 1, 0)).astype(BF16)
    values_ref[:CHANNELS] = (matmul(flipped_ref[1], hidden, 1, 1) * gains_ref[...]).astype(BF16)


def second_kernel(place, table_ref, v0, v1, v2, v3, values_ref, send_ref, total_ref):
    for index, source in zip((0, *LAST_FAR), (v0, v1, v2, v3)):
        values_ref[:, slot(index)] = source[...]
    write_half(1 - place[2], table_ref, values_ref, send_ref, total_ref)


def half_theta(half, table_ref, columns, along):
    sign = (2 * half - 1).astype(F32)
    return (sign * table_ref[half_rows(1 - half), columns].astype(F32)) * along


def write_pairs(total_ref, pairs_ref):
    pairs_ref[:, :CHANNELS] = total_ref[:, CHANNELS:].astype(BF16)
    pairs_ref[:, CHANNELS : 2 * CHANNELS] = total_ref[:, :CHANNELS].astype(BF16)


def first_gradient_kernel(
    place,
    weights_ref,
    mine_ref,
    table_ref,
    fields_hbm,
    second_hbm,
    values_ref,
    theta_ref,
    charge_ref,
    total_ref,
    pairs_ref,
    fields_ref,
    arrivals,
):
    copies = [
        pltpu.make_async_copy(fields_hbm, fields_ref, arrivals.at[0]),
        pltpu.make_async_copy(second_hbm, values_ref.at[BLOCK:], arrivals.at[1]),
    ]
    for copy in copies:
        copy.start()
    weigh_pieces(mine_ref, weights_ref, 1, total_ref)
    write_pairs(total_ref, pairs_ref)
    flipped = jnp.transpose(total_ref[:, CHANNELS:]).astype(BF16)
    charge_ref[...] = matmul(flipped, table_ref[half_rows(place[2]), :], 1, 0)
    values_ref[:BLOCK] = table_ref[TABLE:]
    for index in range(SLABS):
        columns = slot(index)
        along = matmul(pairs_ref[...], table_ref[TABLE:, columns], 1, 0)
        theta_ref[:, columns] = half_theta(place[2], table_ref, columns, along)
    for copy in copies:
        copy.wait()
    for index in range(SLABS):
        columns = slot(index)
        along = matmul(fields_ref[...], values_ref[BLOCK:, columns], 1, 0)
        theta_ref[:, columns] += half_theta(place[2], table_ref, columns, along)


def finish_gradient(
    index, place, table_ref, pairs_ref, flipped_ref, values_ref, theta_ref, charge_ref, directions, target
):
    columns = slot(index)
    pairs = pairs_ref[...]
    theta = theta_ref[:, columns] + half_theta(
        1 - place[2], table_ref, columns, matmul(pairs, values_ref[:, columns], 1, 0)
    )
    charge = matmul(flipped_ref[...], table_ref[half_rows(1 - place[2]), columns], 1, 0)
    target[:CHANNELS] = (charge + charge_ref[:, columns]).astype(BF16)
    for side in range(BLOCK // CHANNELS):
        part = slice(side * CHANNELS, (side + 1) * CHANNELS)
        sums = [
            jnp.sum(direction * theta[:, part], axis=0, keepdims=True) for direction in directions
        ]
        position = jnp.concatenate(sums + [jnp.zeros((13, CHANNELS), F32)], axis=0)
        target[CHANNELS:, part] = (position * (2.0 * math.pi / BOX_LENGTH)).astype(BF16)


def gradient_kernel(
    place,
    weights_ref,
    other_ref,
    table_ref,
    fields_ref,
    values_ref,
    theta_ref,
    charge_ref,
    pairs_ref,
    flipped_ref,
    o2,
    o1,
    o3,
    total_ref,
):
    weigh_pieces(other_ref, weights_ref, 1, total_ref)
    write_pairs(total_ref, pairs_ref)
    pairs_ref[:, 2 * CHANNELS :] = fields_ref[...]
    flipped_ref[...] = jnp.transpose(total_ref[:, CHANNELS:]).astype(BF16)
    directions = class_vectors(place[0] * STRIDE, (SLAB, CHANNELS), 0)
    rest = (place, table_ref, pairs_ref, flipped_ref, values_ref, theta_ref, charge_ref, directions)
    for index, target in ((2, o2), (1, o1), (3, o3)):
        finish_gradient(index, *rest, target)


def own_gradient_kernel(
    place, table_ref, pairs_ref, flipped_ref, values_ref, theta_ref, charge_ref, o0
):
    rest = (place, table_ref, pairs_ref, flipped_ref, values_ref, theta_ref, charge_ref)
    directions = class_vectors(place[0] * STRIDE, (SLAB, CHANNELS), 0)
    finish_gradient(0, *rest, directions, o0)


def sum_kernel(place, parts_ref, spread_ref):
    total = parts_ref[0].astype(F32)
    for index in range(1, PIECES):
        total += parts_ref[index].astype(F32)
    total = total.astype(BF16)
    for index in range(PIECES):
        spread_ref[index] = total


def final_kernel(
    place, q0, q1, q2, q3, gains_ref, hidden_grad_ref, flipped_ref, features_ref, positions_ref
):
    total = (q0[...].astype(F32) + q1[...].astype(F32)) + (q2[...].astype(F32) + q3[...].astype(F32))
    scaled = (jnp.transpose(total[:CHANNELS]) * gains_ref[...]).astype(BF16)
    features_ref[...] = (
        hidden_grad_ref[...].astype(F32) + matmul(scaled, flipped_ref[0], 1, 0)
    ).astype(BF16)
    positions_ref[...] = total[CHANNELS : CHANNELS + 3]


def shape_of(shape, dtype):
    return jax.ShapeDtypeStruct(shape, dtype)


def far(value):
    return pltpu.with_memory_space_constraint(value, pltpu.HBM)


def near(value):
    return pltpu.with_memory_space_constraint(value, pltpu.VMEM)


def whole(shape):
    return pl.BlockSpec(shape, lambda step, place: (0,) * len(shape))


def compiler(micros):
    return dict(
        compiler_params=pltpu.CompilerParams(vmem_limit_bytes=VMEM_LIMIT),
        cost_estimate=pl.CostEstimate(
            flops=int(micros * 10**9), bytes_accessed=int(micros * 10**6), transcendentals=0
        ),
    )


def call(kernel, in_specs, outs, out_specs, operands, micros=2):
    return pl.pallas_call(
        kernel,
        grid_spec=pltpu.PrefetchScalarGridSpec(
            num_scalar_prefetch=1, grid=(1,), in_specs=in_specs, out_specs=out_specs
        ),
        out_shape=outs,
        **compiler(micros),
    )(*operands)


def call_whole(kernel, outs, scratch, place, operands, spaces=None, out_spaces=None, micros=2):
    spaces = spaces or [pltpu.VMEM] * len(operands)
    out_spaces = out_spaces or [pltpu.VMEM] * len(outs)
    return pl.pallas_call(
        kernel,
        in_specs=[pl.BlockSpec(memory_space=pltpu.SMEM)]
        + [pl.BlockSpec(memory_space=space) for space in spaces],
        out_specs=[pl.BlockSpec(memory_space=space) for space in out_spaces],
        out_shape=outs,
        scratch_shapes=scratch,
        **compiler(micros),
    )(place, *operands)


ATOM_REST = ("yh", "yl", "z")


def shifted(value, shift):
    return lax.ppermute(value, "x", [(i, (i + shift) % SLABS) for i in range(SLABS)])


def spread_out(send, own, order):
    return [own] + [send(shift) for shift in order]


def swapped(value):
    return lax.ppermute(value, "core", [(0, 1), (1, 0)])


def add_halves(keep, send, *more):
    total = keep.astype(F32) + swapped(send).astype(F32)
    for value in more:
        total = total + value.astype(F32)
    return total.astype(BF16)


def sum_fields(place, part):
    parts = lax.all_to_all(part, ATOM_REST, 0, 0, tiled=True)
    if place is None:
        total = jnp.sum(parts.astype(F32), axis=0).astype(BF16)
        spread = jnp.broadcast_to(total[None], parts.shape)
    else:
        (spread,) = call_whole(
            sum_kernel, [pltpu.VMEM(parts.shape, BF16)], [], place, [near(parts)], micros=1
        )
    mine = lax.all_to_all(spread, ATOM_REST, 0, 0, tiled=True)
    return mine, swapped(mine)


def per_device(
    atomic_descriptors,
    unit_cell_coordinates,
    element_labels,
    lattice_momenta,
    feature_to_latent_matrix,
    latent_to_feature_matrix,
    element_latent_multiplier,
    upstream_gradient,
):
    place = jnp.stack(
        [lax.axis_index("x"), lax.axis_index("yh"), lax.axis_index("core")]
    ).astype(jnp.int32)
    prefactor = 1.0 / math.sqrt(
        atomic_descriptors.shape[0]
        * lattice_momenta.shape[1]
        * lax.axis_size(("x", "yh", "yl", "z", "core"))
    )
    labels = element_labels[None, :]
    multiplier = jnp.swapaxes(element_latent_multiplier, 0, 1)
    lengths = {axis: lax.axis_size(axis) for axis in ("x", "yl", "z")}
    copies = lengths["yl"] * lengths["z"] // SLABS
    pairs = []
    for yl in range(lengths["yl"]):
        for z in range(lengths["z"]):
            for x in range(SLABS):
                place_of = lambda x: (x * lengths["yl"] + yl) * lengths["z"] + z
                pairs.append((place_of((x + 2 * (z % 2) + yl) % SLABS), place_of(x)))
    fetched = lax.ppermute(lattice_momenta, ("x", "yl", "z"), pairs)

    matrices = whole((2, CHANNELS, CHANNELS))
    gains_spec = whole(multiplier.shape)
    pieces_shape = shape_of((PIECES, ROWS, CHANNELS), BF16)
    values_block = whole((BLOCK, BLOCK))
    values_shape = shape_of((BLOCK, BLOCK), BF16)
    atoms_here = SLABS * BLOCK

    blocked = (SLABS, 2, BLOCK, CHANNELS)
    operands = [
        unit_cell_coordinates,
        labels,
        atomic_descriptors.reshape(blocked),
        upstream_gradient.reshape(blocked),
        feature_to_latent_matrix,
        latent_to_feature_matrix,
        multiplier,
    ]
    local = [shape_of(value.shape, value.dtype) for value in operands]
    local[2] = local[3] = shape_of((SLABS, BLOCK, CHANNELS), BF16)
    table, keep, send = call_whole(
        tables_kernel,
        (
            pltpu.VMEM((TABLE + BLOCK, atoms_here), BF16),
            pieces_shape,
            pieces_shape,
        ),
        [pltpu.VMEM(value.shape, value.dtype) for value in local]
        + [
            pltpu.VMEM((SLAB, BLOCK), F32),
            pltpu.VMEM((SLAB, atoms_here), F32),
            pltpu.VMEM((SLAB, atoms_here), F32),
            pltpu.VMEM((SLAB - LEAP, CHANNELS), F32),
            pltpu.SemaphoreType.DMA((len(operands),)),
        ],
        place,
        [far(value) for value in operands],
        spaces=[pltpu.HBM] * len(operands),
        micros=7,
    )
    (counts,) = call_whole(
        functools.partial(counts_kernel, float(copies)), [pieces_shape], [], place, [fetched]
    )
    part = add_halves(keep, send, counts)
    mine, other = sum_fields(None, part)
    half = (SLAB, BLOCK)
    weights, fields_mine, before = call_whole(
        functools.partial(first_potential_kernel, prefactor),
        [
            shape_of((2, SLAB, CHANNELS), F32),
            pltpu.HBM(half, BF16),
            shape_of((BLOCK, atoms_here), F32),
        ],
        [pltpu.VMEM(half, F32), pltpu.VMEM(half, BF16), pltpu.SemaphoreType.DMA],
        place,
        [mine, near(table)],
        out_spaces=[pltpu.VMEM, pltpu.HBM, pltpu.VMEM],
    )
    fields_other, flipped, p2, p1, p3 = call_whole(
        potential_kernel,
        [shape_of(half, BF16), shape_of((BLOCK, SLAB), BF16)] + [values_shape] * 3,
        [pltpu.VMEM(half, F32)],
        place,
        [weights, other, near(table), before],
    )
    (p0,) = call_whole(
        own_potential_kernel,
        [values_shape],
        [],
        place,
        [near(table), before, flipped],
        micros=0.1,
    )
    own_atoms = pl.BlockSpec((BLOCK, CHANNELS), lambda step, place: (2 * place[0] + place[1], 0))
    own_labels = pl.BlockSpec((1, BLOCK), lambda step, place: (0, 2 * place[0] + place[1]))
    own_block = (BLOCK, CHANNELS)
    labels, p0 = lax.optimization_barrier((labels, p0))
    products = (p0, p1, p2, p3)
    arrived = spread_out(lambda shift: shifted(products[shift], shift), products[0], (2, 1, 3))
    own_features, own_upstream, gains_one, gains_two, inward_flipped = call(
        own_atoms_kernel,
        [own_labels, own_atoms, own_atoms, matrices, gains_spec],
        (
            shape_of(own_block, BF16),
            shape_of(own_block, BF16),
            shape_of(own_block, F32),
            shape_of((CHANNELS, BLOCK), F32),
            shape_of((2, CHANNELS, CHANNELS), BF16),
        ),
        (
            whole(own_block),
            whole(own_block),
            whole(own_block),
            whole((CHANNELS, BLOCK)),
            matrices,
        ),
        (
            place,
            labels,
            atomic_descriptors,
            upstream_gradient,
            feature_to_latent_matrix,
            multiplier,
        ),
        micros=0.1,
    )
    values_own, hidden_grad = call_whole(
        middle_kernel,
        [values_shape, shape_of(own_block, BF16)],
        [],
        place,
        [*arrived, own_features, own_upstream, gains_two, inward_flipped, latent_to_feature_matrix],
    )
    seconds = spread_out(lambda shift: shifted(values_own, SLABS - shift), values_own, LAST_FAR)
    values_two, send = call_whole(
        second_kernel,
        [shape_of((BLOCK, atoms_here), BF16), pieces_shape],
        [pltpu.VMEM((SLAB, BLOCK), F32)],
        place,
        [near(table), *seconds],
    )
    (keep,) = call_whole(
        keep_kernel,
        [pieces_shape],
        [pltpu.VMEM((SLAB, BLOCK), F32)],
        place,
        [near(table), near(values_two)],
        micros=0.1,
    )
    mine, other = sum_fields(place, add_halves(keep, send))
    result_shape = shape_of((CHANNELS + 16, BLOCK), BF16)
    result_spec = whole((CHANNELS + 16, BLOCK))
    values, theta, charge = call_whole(
        first_gradient_kernel,
        [
            shape_of((2 * BLOCK, atoms_here), BF16),
            shape_of((SLAB, atoms_here), F32),
            shape_of((CHANNELS, atoms_here), F32),
        ],
        [
            pltpu.VMEM(half, F32),
            pltpu.VMEM(half, BF16),
            pltpu.VMEM(half, BF16),
            pltpu.SemaphoreType.DMA((2,)),
        ],
        place,
        [weights, mine, near(table), far(fields_mine), far(values_two)],
        spaces=[pltpu.VMEM] * 3 + [pltpu.HBM] * 2,
    )
    pairs, flipped, o2, o1, o3 = call_whole(
        gradient_kernel,
        [shape_of((SLAB, 2 * BLOCK), BF16), shape_of((CHANNELS, SLAB), BF16)] + [result_shape] * 3,
        [pltpu.VMEM(half, F32)],
        place,
        [weights, other, near(table), fields_other, values, theta, charge],
    )
    (o0,) = call_whole(
        own_gradient_kernel,
        [result_shape],
        [],
        place,
        [near(table), pairs, flipped, values, theta, charge],
        micros=0.1,
    )
    results = (o0, o1, o2, o3)
    arrived = spread_out(lambda shift: shifted(results[shift], shift), results[0], (2, 1, 3))
    return tuple(
        call_whole(
            final_kernel,
            [shape_of(own_block, BF16), shape_of((3, BLOCK), F32)],
            [],
            place,
            [*arrived, gains_one, hidden_grad, inward_flipped],
        )
    )


def solution(mesh):
    fine = Mesh(mesh.devices.reshape(SLABS, 2, 2, -1, 2), ("x", "yh", "yl", "z", "core"))
    atom, group = ("yl", "z", "core"), ("x", "yh")
    in_specs = (
        P(atom, None),
        P(None, atom),
        P(atom),
        P(None, group),
        P(),
        P(),
        P(),
        P(atom, None),
    )
    out_specs = (P(atom + group, None), P(None, atom + group))
    return jax.shard_map(
        per_device, mesh=fine, in_specs=in_specs, out_specs=out_specs, check_vma=False
    )
```

```python
import functools
import math

import jax
import jax.numpy as jnp
from jax import lax
from jax.experimental import pallas as pl
from jax.experimental.pallas import tpu as pltpu
from jax.sharding import Mesh
from jax.sharding import PartitionSpec as P

BOX_LENGTH = 100.0
GAUSSIAN_SIGMAS = (200.0, 100.0)
REACH = 8
SPAN = 2 * REACH + 1
CLASSES = (SPAN**3 + 1) // 2
SLABS = 4
SLAB = 640
STRIDE = -(-CLASSES // SLABS)
LAST_FAR = (2, 3, 1)
LEAP = REACH * SPAN
FIRST_ROWS = ((0, 64), (64, 144))
COUNT_PIECE = 30
COUNT_ROW = 32
TABLE = 2 * SLAB
BLOCK = 256
CHANNELS = 128
ROWS = 40
PIECES = 32
VMEM_LIMIT = 14 * 1024 * 1024
BF16 = jnp.bfloat16
F32 = jnp.float32

COS_SERIES = (
    0.999999660315462,
    -19.739032161520388,
    64.93001235415629,
    -85.28515888817482,
    58.84788533073816,
    -21.15810679384873,
)
SIN_SERIES = (
    6.283183359037432,
    -41.341456424111435,
    81.59687947501621,
    -76.58597187733577,
    41.22756686823296,
    -12.302134397179453,
)


def class_vectors(first_class, shape, axis):
    label = (lax.broadcasted_iota(jnp.int32, shape, axis) + first_class).astype(F32)
    square = SPAN * SPAN
    first = jnp.floor((label + (square // 2 + 0.5)) * (1.0 / square))
    rest = label - square * first
    second = jnp.floor((rest + (REACH + 0.5)) * (1.0 / SPAN))
    return first, second, rest - SPAN * second


def matmul(left, right, left_dim, right_dim):
    return lax.dot_general(
        left, right, (((left_dim,), (right_dim,)), ((), ())), preferred_element_type=F32
    )


def flip(matrix):
    return jnp.transpose(matrix.astype(F32)).astype(BF16)


def gain_columns(multiplier, labels):
    species_count, channels = multiplier.shape
    padding = jnp.zeros((8 - species_count, channels), F32)
    columns = jnp.transpose(jnp.concatenate([multiplier, padding], axis=0))
    result = jnp.zeros((channels, labels.shape[1]), F32)
    for species in range(species_count):
        result = jnp.where(labels == species, columns[:, species : species + 1], result)
    return result


def series(coefficients, square):
    result = coefficients[-1] * square + coefficients[-2]
    for coefficient in coefficients[-3::-1]:
        result = result * square + coefficient
    return result


def cosine_and_sine(turns):
    turns = turns - jnp.floor(turns + 0.5)
    square = turns * turns
    return series(COS_SERIES, square), turns * series(SIN_SERIES, square)


def write_half(half, table_ref, values_ref, pieces_ref, total_ref):
    total_ref[...] = matmul(table_ref[half_rows(half), :], values_ref[...], 1, 1)
    total_ref[SLAB - 8 :, :CHANNELS] = jnp.zeros((8, CHANNELS), F32)
    for index in range(PIECES):
        row, side = index // 2, index % 2
        pieces_ref[index] = total_ref[
            row * ROWS : (row + 1) * ROWS, side * CHANNELS : (side + 1) * CHANNELS
        ].astype(BF16)


def keep_kernel(place, table_ref, values_ref, keep_ref, total_ref):
    write_half(place[2], table_ref, values_ref, keep_ref, total_ref)


def weigh_pieces(pieces_ref, weights_ref, first, total_ref):
    for index in range(PIECES):
        row, side = index // 2, index % 2
        rows = slice(row * ROWS, (row + 1) * ROWS)
        total_ref[rows, side * CHANNELS : (side + 1) * CHANNELS] = (
            pieces_ref[index].astype(F32) * weights_ref[(first + side) % 2, rows]
        )


def half_rows(half):
    return pl.ds(pl.multiple_of(half * SLAB, SLAB), SLAB)


def slot(index):
    return slice(index * BLOCK, (index + 1) * BLOCK)


def tables_kernel(
    place,
    coordinates_hbm,
    labels_hbm,
    features_hbm,
    upstream_hbm,
    inward_hbm,
    outward_hbm,
    multiplier_hbm,
    table_ref,
    keep_ref,
    send_ref,
    coordinates_ref,
    labels_ref,
    features_ref,
    upstream_ref,
    inward_ref,
    outward_ref,
    multiplier_ref,
    total_ref,
    cosine_ref,
    sine_ref,
    second_ref,
    arrivals,
):
    copies = [
        pltpu.make_async_copy(source, target, arrivals.at[index])
        for index, (source, target) in enumerate(
            (
                (coordinates_hbm, coordinates_ref),
                (labels_hbm, labels_ref),
                (features_hbm.at[:, place[1]], features_ref),
                (upstream_hbm.at[:, place[1]], upstream_ref),
                (inward_hbm, inward_ref),
                (outward_hbm, outward_ref),
                (multiplier_hbm, multiplier_ref),
            )
        )
    ]
    for copy in copies:
        copy.start()
    blocks = [lax.rem(place[0] + index, SLABS) for index in range(SLABS)]
    sides = [
        pl.ds(pl.multiple_of((2 * block + place[1]) * BLOCK + side * CHANNELS, CHANNELS), CHANNELS)
        for block in blocks
        for side in range(BLOCK // CHANNELS)
    ]
    first_vectors = [
        class_vectors(place[0] * STRIDE + start, (stop - start, CHANNELS), 0)
        for start, stop in FIRST_ROWS
    ]
    for start in range(0, SLAB - LEAP, LEAP):
        stop = min(start + LEAP, SLAB - LEAP)
        vectors = class_vectors(place[0] * STRIDE + start, (stop - start, CHANNELS), 0)
        second_ref[start:stop] = vectors[1]
    copies[0].wait()
    for index, side in enumerate(sides):
        columns = slice(index * CHANNELS, (index + 1) * CHANNELS)
        where = [coordinates_ref[axis : axis + 1, side] for axis in range(3)]
        for (start, stop), vectors in zip(FIRST_ROWS, first_vectors):
            turns = vectors[0] * where[0] + vectors[1] * where[1] + vectors[2] * where[2]
            cosine, sine = cosine_and_sine(turns)
            cosine_ref[start:stop, columns] = cosine
            sine_ref[start:stop, columns] = sine
            table_ref[start:stop, columns] = cosine.astype(BF16)
            table_ref[SLAB + start : SLAB + stop, columns] = sine.astype(BF16)
        plain = cosine_and_sine(REACH * where[1])
        carried = cosine_and_sine(where[0] - (REACH + 1) * where[1])
        for start in range(FIRST_ROWS[-1][1], SLAB, 80):
            stop = min(start + 80, SLAB)
            before = slice(start - LEAP, stop - LEAP)
            carry = second_ref[before] > 0.5
            turn_cosine = jnp.where(carry, carried[0], plain[0])
            turn_sine = jnp.where(carry, carried[1], plain[1])
            old_cosine, old_sine = cosine_ref[before, columns], sine_ref[before, columns]
            cosine = old_cosine * turn_cosine - old_sine * turn_sine
            sine = old_sine * turn_cosine + old_cosine * turn_sine
            cosine_ref[start:stop, columns] = cosine
            sine_ref[start:stop, columns] = sine
            table_ref[start:stop, columns] = cosine.astype(BF16)
            table_ref[SLAB + start : SLAB + stop, columns] = sine.astype(BF16)
    for copy in copies[1:]:
        copy.wait()
    atoms = (SLABS * BLOCK, CHANNELS)
    charges = matmul(flip(inward_ref[0]), features_ref[...].reshape(atoms), 1, 1)
    grad_pot = matmul(outward_ref[1], upstream_ref[...].reshape(atoms), 1, 1).astype(BF16)
    for block in range(SLABS):
        labels = labels_ref[:, pl.ds(pl.multiple_of((2 * block + place[1]) * BLOCK, BLOCK), BLOCK)]
        gains = gain_columns(multiplier_ref[:, 0, :], labels)
        target = lax.rem(block - place[0] + SLABS, SLABS)
        columns = pl.ds(pl.multiple_of(target * BLOCK, BLOCK), BLOCK)
        table_ref[TABLE : TABLE + CHANNELS, columns] = (charges[:, slot(block)] * gains).astype(BF16)
        table_ref[TABLE + CHANNELS :, columns] = grad_pot[:, slot(block)]
    values_ref = table_ref.at[TABLE:]
    write_half(1 - place[2], table_ref, values_ref, send_ref, total_ref)
    write_half(place[2], table_ref, values_ref, keep_ref, total_ref)


def counts_kernel(copies, place, momenta_ref, counts_ref):
    momenta = momenta_ref[...].astype(F32)
    label = jnp.abs(
        momenta[0:1] * float(SPAN * SPAN) + momenta[1:2] * float(SPAN) + momenta[2:3]
    ) - (place[0] * STRIDE).astype(F32)
    column = jnp.transpose(jnp.broadcast_to(label, (8, label.shape[1])))[:, 0:1]
    column = jnp.broadcast_to(column, (column.shape[0], CHANNELS))
    lane = lax.broadcasted_iota(jnp.int32, column.shape, 1).astype(F32)
    counts_ref[...] = jnp.zeros(counts_ref.shape, BF16)
    rows = []
    for start in range(0, SLAB, CHANNELS):
        here = (column == lane + float(start)) & (lane < float(STRIDE - start))
        rows.append(jnp.sum(jnp.where(here, 1.0 / copies, 0.0), axis=0, keepdims=True))
    rows = [jnp.zeros((COUNT_ROW, CHANNELS), F32)] + rows
    rows.append(jnp.zeros((ROWS + 1 - COUNT_ROW - len(rows), CHANNELS), F32))
    counts_ref[COUNT_PIECE] = jnp.concatenate(rows, axis=0).astype(BF16)


def write_fields(total_ref, fields_ref):
    fields_ref[:, :CHANNELS] = total_ref[:, CHANNELS:].astype(BF16)
    fields_ref[:, CHANNELS:] = total_ref[:, :CHANNELS].astype(BF16)


def first_potential_kernel(
    prefactor,
    place,
    mine_ref,
    table_ref,
    weights_ref,
    fields_hbm,
    potential_ref,
    total_ref,
    fields_ref,
    leaves,
):
    counts = jnp.transpose(mine_ref[COUNT_PIECE].astype(F32)[COUNT_ROW:])
    for index in range(SLAB // CHANNELS):
        start = index * CHANNELS
        count = counts[:, index : index + 1]
        vectors = class_vectors(place[0] * STRIDE + start, (CHANNELS, CHANNELS), 0)
        norm = vectors[0] * vectors[0] + vectors[1] * vectors[1] + vectors[2] * vectors[2]
        for block, spread in enumerate(GAUSSIAN_SIGMAS):
            weights_ref[block, start : start + CHANNELS, :] = count * (
                prefactor * jnp.exp(norm * (-1.0 / spread))
            )
    weigh_pieces(mine_ref, weights_ref, 0, total_ref)
    write_fields(total_ref, fields_ref)
    leaving = pltpu.make_async_copy(fields_ref, fields_hbm, leaves)
    leaving.start()
    flipped = jnp.transpose(total_ref[...]).astype(BF16)
    potential_ref[...] = matmul(flipped, table_ref[half_rows(place[2]), :], 1, 0)
    leaving.wait()


def potential_kernel(
    place, weights_ref, other_ref, table_ref, before_ref, fields_ref, flipped_ref, p2, p1, p3, total_ref
):
    weigh_pieces(other_ref, weights_ref, 0, total_ref)
    write_fields(total_ref, fields_ref)
    flipped_ref[...] = jnp.transpose(total_ref[...]).astype(BF16)
    for index, target in ((2, p2), (1, p1), (3, p3)):
        rest = matmul(flipped_ref[...], table_ref[half_rows(1 - place[2]), slot(index)], 1, 0)
        target[...] = (before_ref[:, slot(index)] + rest).astype(BF16)


def own_potential_kernel(place, table_ref, before_ref, flipped_ref, p0):
    rest = matmul(flipped_ref[...], table_ref[half_rows(1 - place[2]), slot(0)], 1, 0)
    p0[...] = (before_ref[:, slot(0)] + rest).astype(BF16)


def own_atoms_kernel(
    place,
    labels_ref,
    features_ref,
    upstream_ref,
    inward_ref,
    multiplier_ref,
    own_features_ref,
    own_upstream_ref,
    gains_one_ref,
    gains_two_ref,
    flipped_ref,
):
    own_features_ref[...] = features_ref[...]
    own_upstream_ref[...] = upstream_ref[...]
    gains_one_ref[...] = jnp.transpose(gain_columns(multiplier_ref[:, 0, :], labels_ref[...]))
    gains_two_ref[...] = gain_columns(multiplier_ref[:, 1, :], labels_ref[...])
    for block in range(2):
        flipped_ref[block] = flip(inward_ref[block])


def middle_kernel(
    place,
    q0,
    q1,
    q2,
    q3,
    features_ref,
    upstream_ref,
    gains_ref,
    flipped_ref,
    outward_ref,
    values_ref,
    hidden_grad_ref,
):
    total = (q0[...].astype(F32) + q1[...].astype(F32)) + (q2[...].astype(F32) + q3[...].astype(F32))
    grad_charge = total[CHANNELS:]
    scaled = jnp.transpose(grad_charge * gains_ref[...]).astype(BF16)
    hidden_grad = (
        upstream_ref[...].astype(F32) + matmul(scaled, flipped_ref[1], 1, 0)
    ).astype(BF16)
    hidden_grad_ref[...] = hidden_grad
    values_ref[CHANNELS:] = matmul(outward_ref[0], hidden_grad, 1, 1).astype(BF16)
    potential = jnp.transpose(total[:CHANNELS]).astype(BF16)
    hidden = (features_ref[...].astype(F32) + matmul(potential, outward_ref[0], 1, 0)).astype(BF16)
    values_ref[:CHANNELS] = (matmul(flipped_ref[1], hidden, 1, 1) * gains_ref[...]).astype(BF16)


def second_kernel(place, table_ref, v0, v1, v2, v3, values_ref, send_ref, total_ref):
    for index, source in zip((0, *LAST_FAR), (v0, v1, v2, v3)):
        values_ref[:, slot(index)] = source[...]
    write_half(1 - place[2], table_ref, values_ref, send_ref, total_ref)


def half_theta(half, table_ref, columns, along):
    sign = (2 * half - 1).astype(F32)
    return (sign * table_ref[half_rows(1 - half), columns].astype(F32)) * along


def write_pairs(total_ref, pairs_ref):
    pairs_ref[:, :CHANNELS] = total_ref[:, CHANNELS:].astype(BF16)
    pairs_ref[:, CHANNELS : 2 * CHANNELS] = total_ref[:, :CHANNELS].astype(BF16)


def first_gradient_kernel(
    place,
    weights_ref,
    mine_ref,
    table_ref,
    fields_hbm,
    second_hbm,
    values_ref,
    theta_ref,
    charge_ref,
    total_ref,
    pairs_ref,
    fields_ref,
    arrivals,
):
    copies = [
        pltpu.make_async_copy(fields_hbm, fields_ref, arrivals.at[0]),
        pltpu.make_async_copy(second_hbm, values_ref.at[BLOCK:], arrivals.at[1]),
    ]
    for copy in copies:
        copy.start()
    weigh_pieces(mine_ref, weights_ref, 1, total_ref)
    write_pairs(total_ref, pairs_ref)
    flipped = jnp.transpose(total_ref[:, CHANNELS:]).astype(BF16)
    charge_ref[...] = matmul(flipped, table_ref[half_rows(place[2]), :], 1, 0)
    values_ref[:BLOCK] = table_ref[TABLE:]
    for index in range(SLABS):
        columns = slot(index)
        along = matmul(pairs_ref[...], table_ref[TABLE:, columns], 1, 0)
        theta_ref[:, columns] = half_theta(place[2], table_ref, columns, along)
    for copy in copies:
        copy.wait()
    for index in range(SLABS):
        columns = slot(index)
        along = matmul(fields_ref[...], values_ref[BLOCK:, columns], 1, 0)
        theta_ref[:, columns] += half_theta(place[2], table_ref, columns, along)


def finish_gradient(
    index, place, table_ref, pairs_ref, flipped_ref, values_ref, theta_ref, charge_ref, directions, target
):
    columns = slot(index)
    pairs = pairs_ref[...]
    theta = theta_ref[:, columns] + half_theta(
        1 - place[2], table_ref, columns, matmul(pairs, values_ref[:, columns], 1, 0)
    )
    charge = matmul(flipped_ref[...], table_ref[half_rows(1 - place[2]), columns], 1, 0)
    target[:CHANNELS] = (charge + charge_ref[:, columns]).astype(BF16)
    for side in range(BLOCK // CHANNELS):
        part = slice(side * CHANNELS, (side + 1) * CHANNELS)
        sums = [
            jnp.sum(direction * theta[:, part], axis=0, keepdims=True) for direction in directions
        ]
        position = jnp.concatenate(sums + [jnp.zeros((13, CHANNELS), F32)], axis=0)
        target[CHANNELS:, part] = (position * (2.0 * math.pi / BOX_LENGTH)).astype(BF16)


def gradient_kernel(
    place,
    weights_ref,
    other_ref,
    table_ref,
    fields_ref,
    values_ref,
    theta_ref,
    charge_ref,
    pairs_ref,
    flipped_ref,
    o2,
    o1,
    o3,
    total_ref,
):
    weigh_pieces(other_ref, weights_ref, 1, total_ref)
    write_pairs(total_ref, pairs_ref)
    pairs_ref[:, 2 * CHANNELS :] = fields_ref[...]
    flipped_ref[...] = jnp.transpose(total_ref[:, CHANNELS:]).astype(BF16)
    directions = class_vectors(place[0] * STRIDE, (SLAB, CHANNELS), 0)
    rest = (place, table_ref, pairs_ref, flipped_ref, values_ref, theta_ref, charge_ref, directions)
    for index, target in ((2, o2), (1, o1), (3, o3)):
        finish_gradient(index, *rest, target)


def own_gradient_kernel(
    place, table_ref, pairs_ref, flipped_ref, values_ref, theta_ref, charge_ref, o0
):
    rest = (place, table_ref, pairs_ref, flipped_ref, values_ref, theta_ref, charge_ref)
    directions = class_vectors(place[0] * STRIDE, (SLAB, CHANNELS), 0)
    finish_gradient(0, *rest, directions, o0)


def sum_kernel(place, parts_ref, spread_ref):
    total = parts_ref[0].astype(F32)
    for index in range(1, PIECES):
        total += parts_ref[index].astype(F32)
    total = total.astype(BF16)
    for index in range(PIECES):
        spread_ref[index] = total


def final_kernel(
    place, q0, q1, q2, q3, gains_ref, hidden_grad_ref, flipped_ref, features_ref, positions_ref
):
    total = (q0[...].astype(F32) + q1[...].astype(F32)) + (q2[...].astype(F32) + q3[...].astype(F32))
    scaled = (jnp.transpose(total[:CHANNELS]) * gains_ref[...]).astype(BF16)
    features_ref[...] = (
        hidden_grad_ref[...].astype(F32) + matmul(scaled, flipped_ref[0], 1, 0)
    ).astype(BF16)
    positions_ref[...] = total[CHANNELS : CHANNELS + 3]


def shape_of(shape, dtype):
    return jax.ShapeDtypeStruct(shape, dtype)


def far(value):
    return pltpu.with_memory_space_constraint(value, pltpu.HBM)


def near(value):
    return pltpu.with_memory_space_constraint(value, pltpu.VMEM)


def whole(shape):
    return pl.BlockSpec(shape, lambda step, place: (0,) * len(shape))


def compiler(micros):
    return dict(
        compiler_params=pltpu.CompilerParams(vmem_limit_bytes=VMEM_LIMIT),
        cost_estimate=pl.CostEstimate(
            flops=int(micros * 10**9), bytes_accessed=int(micros * 10**6), transcendentals=0
        ),
    )


def call(kernel, in_specs, outs, out_specs, operands, micros=2):
    return pl.pallas_call(
        kernel,
        grid_spec=pltpu.PrefetchScalarGridSpec(
            num_scalar_prefetch=1, grid=(1,), in_specs=in_specs, out_specs=out_specs
        ),
        out_shape=outs,
        **compiler(micros),
    )(*operands)


def call_whole(kernel, outs, scratch, place, operands, spaces=None, out_spaces=None, micros=2):
    spaces = spaces or [pltpu.VMEM] * len(operands)
    out_spaces = out_spaces or [pltpu.VMEM] * len(outs)
    return pl.pallas_call(
        kernel,
        in_specs=[pl.BlockSpec(memory_space=pltpu.SMEM)]
        + [pl.BlockSpec(memory_space=space) for space in spaces],
        out_specs=[pl.BlockSpec(memory_space=space) for space in out_spaces],
        out_shape=outs,
        scratch_shapes=scratch,
        **compiler(micros),
    )(place, *operands)


ATOM_REST = ("yh", "yl", "z")


def shifted(value, shift):
    return lax.ppermute(value, "x", [(i, (i + shift) % SLABS) for i in range(SLABS)])


def spread_out(send, own, order):
    return [own] + [send(shift) for shift in order]


def swapped(value):
    return lax.ppermute(value, "core", [(0, 1), (1, 0)])


def add_halves(keep, send, *more):
    total = keep.astype(F32) + swapped(send).astype(F32)
    for value in more:
        total = total + value.astype(F32)
    return total.astype(BF16)


def sum_fields(place, part):
    parts = lax.all_to_all(part, ATOM_REST, 0, 0, tiled=True)
    if place is None:
        total = jnp.sum(parts.astype(F32), axis=0).astype(BF16)
        spread = jnp.broadcast_to(total[None], parts.shape)
    else:
        (spread,) = call_whole(
            sum_kernel, [pltpu.VMEM(parts.shape, BF16)], [], place, [near(parts)], micros=1
        )
    mine = lax.all_to_all(spread, ATOM_REST, 0, 0, tiled=True)
    return mine, swapped(mine)


def per_device(
    atomic_descriptors,
    unit_cell_coordinates,
    element_labels,
    lattice_momenta,
    feature_to_latent_matrix,
    latent_to_feature_matrix,
    element_latent_multiplier,
    upstream_gradient,
):
    place = jnp.stack(
        [lax.axis_index("x"), lax.axis_index("yh"), lax.axis_index("core")]
    ).astype(jnp.int32)
    prefactor = 1.0 / math.sqrt(
        atomic_descriptors.shape[0]
        * lattice_momenta.shape[1]
        * lax.axis_size(("x", "yh", "yl", "z", "core"))
    )
    labels = element_labels[None, :]
    multiplier = jnp.swapaxes(element_latent_multiplier, 0, 1)
    lengths = {axis: lax.axis_size(axis) for axis in ("x", "yl", "z")}
    copies = lengths["yl"] * lengths["z"] // SLABS
    pairs = []
    for yl in range(lengths["yl"]):
        for z in range(lengths["z"]):
            for x in range(SLABS):
                place_of = lambda x: (x * lengths["yl"] + yl) * lengths["z"] + z
                pairs.append((place_of((x + 2 * (z % 2) + yl) % SLABS), place_of(x)))
    fetched = lax.ppermute(lattice_momenta, ("x", "yl", "z"), pairs)

    matrices = whole((2, CHANNELS, CHANNELS))
    gains_spec = whole(multiplier.shape)
    pieces_shape = shape_of((PIECES, ROWS, CHANNELS), BF16)
    values_block = whole((BLOCK, BLOCK))
    values_shape = shape_of((BLOCK, BLOCK), BF16)
    atoms_here = SLABS * BLOCK

    blocked = (SLABS, 2, BLOCK, CHANNELS)
    operands = [
        unit_cell_coordinates,
        labels,
        atomic_descriptors.reshape(blocked),
        upstream_gradient.reshape(blocked),
        feature_to_latent_matrix,
        latent_to_feature_matrix,
        multiplier,
    ]
    local = [shape_of(value.shape, value.dtype) for value in operands]
    local[2] = local[3] = shape_of((SLABS, BLOCK, CHANNELS), BF16)
    table, keep, send = call_whole(
        tables_kernel,
        (
            pltpu.VMEM((TABLE + BLOCK, atoms_here), BF16),
            pieces_shape,
            pieces_shape,
        ),
        [pltpu.VMEM(value.shape, value.dtype) for value in local]
        + [
            pltpu.VMEM((SLAB, BLOCK), F32),
            pltpu.VMEM((SLAB, atoms_here), F32),
            pltpu.VMEM((SLAB, atoms_here), F32),
            pltpu.VMEM((SLAB - LEAP, CHANNELS), F32),
            pltpu.SemaphoreType.DMA((len(operands),)),
        ],
        place,
        [far(value) for value in operands],
        spaces=[pltpu.HBM] * len(operands),
        micros=7,
    )
    (counts,) = call_whole(
        functools.partial(counts_kernel, float(copies)), [pieces_shape], [], place, [fetched]
    )
    part = add_halves(keep, send, counts)
    mine, other = sum_fields(None, part)
    half = (SLAB, BLOCK)
    weights, fields_mine, before = call_whole(
        functools.partial(first_potential_kernel, prefactor),
        [
            shape_of((2, SLAB, CHANNELS), F32),
            pltpu.HBM(half, BF16),
            shape_of((BLOCK, atoms_here), F32),
        ],
        [pltpu.VMEM(half, F32), pltpu.VMEM(half, BF16), pltpu.SemaphoreType.DMA],
        place,
        [mine, near(table)],
        out_spaces=[pltpu.VMEM, pltpu.HBM, pltpu.VMEM],
    )
    fields_other, flipped, p2, p1, p3 = call_whole(
        potential_kernel,
        [shape_of(half, BF16), shape_of((BLOCK, SLAB), BF16)] + [values_shape] * 3,
        [pltpu.VMEM(half, F32)],
        place,
        [weights, other, near(table), before],
    )
    (p0,) = call_whole(
        own_potential_kernel,
        [values_shape],
        [],
        place,
        [near(table), before, flipped],
        micros=0.1,
    )
    own_atoms = pl.BlockSpec((BLOCK, CHANNELS), lambda step, place: (2 * place[0] + place[1], 0))
    own_labels = pl.BlockSpec((1, BLOCK), lambda step, place: (0, 2 * place[0] + place[1]))
    own_block = (BLOCK, CHANNELS)
    labels, p0 = lax.optimization_barrier((labels, p0))
    products = (p0, p1, p2, p3)
    arrived = spread_out(lambda shift: shifted(products[shift], shift), products[0], (2, 1, 3))
    own_features, own_upstream, gains_one, gains_two, inward_flipped = call(
        own_atoms_kernel,
        [own_labels, own_atoms, own_atoms, matrices, gains_spec],
        (
            shape_of(own_block, BF16),
            shape_of(own_block, BF16),
            shape_of(own_block, F32),
            shape_of((CHANNELS, BLOCK), F32),
            shape_of((2, CHANNELS, CHANNELS), BF16),
        ),
        (
            whole(own_block),
            whole(own_block),
            whole(own_block),
            whole((CHANNELS, BLOCK)),
            matrices,
        ),
        (
            place,
            labels,
            atomic_descriptors,
            upstream_gradient,
            feature_to_latent_matrix,
            multiplier,
        ),
        micros=0.1,
    )
    values_own, hidden_grad = call_whole(
        middle_kernel,
        [values_shape, shape_of(own_block, BF16)],
        [],
        place,
        [*arrived, own_features, own_upstream, gains_two, inward_flipped, latent_to_feature_matrix],
    )
    seconds = spread_out(lambda shift: shifted(values_own, SLABS - shift), values_own, LAST_FAR)
    values_two, send = call_whole(
        second_kernel,
        [shape_of((BLOCK, atoms_here), BF16), pieces_shape],
        [pltpu.VMEM((SLAB, BLOCK), F32)],
        place,
        [near(table), *seconds],
    )
    (keep,) = call_whole(
        keep_kernel,
        [pieces_shape],
        [pltpu.VMEM((SLAB, BLOCK), F32)],
        place,
        [near(table), near(values_two)],
        micros=0.1,
    )
    mine, other = sum_fields(place, add_halves(keep, send))
    result_shape = shape_of((CHANNELS + 16, BLOCK), BF16)
    result_spec = whole((CHANNELS + 16, BLOCK))
    values, theta, charge = call_whole(
        first_gradient_kernel,
        [
            shape_of((2 * BLOCK, atoms_here), BF16),
            shape_of((SLAB, atoms_here), F32),
            shape_of((CHANNELS, atoms_here), F32),
        ],
        [
            pltpu.VMEM(half, F32),
            pltpu.VMEM(half, BF16),
            pltpu.VMEM(half, BF16),
            pltpu.SemaphoreType.DMA((2,)),
        ],
        place,
        [weights, mine, near(table), far(fields_mine), far(values_two)],
        spaces=[pltpu.VMEM] * 3 + [pltpu.HBM] * 2,
    )
    pairs, flipped, o2, o1, o3 = call_whole(
        gradient_kernel,
        [shape_of((SLAB, 2 * BLOCK), BF16), shape_of((CHANNELS, SLAB), BF16)] + [result_shape] * 3,
        [pltpu.VMEM(half, F32)],
        place,
        [weights, other, near(table), fields_other, values, theta, charge],
    )
    (o0,) = call_whole(
        own_gradient_kernel,
        [result_shape],
        [],
        place,
        [near(table), pairs, flipped, values, theta, charge],
        micros=0.1,
    )
    results = (o0, o1, o2, o3)
    arrived = spread_out(lambda shift: shifted(results[shift], shift), results[0], (2, 1, 3))
    return tuple(
        call_whole(
            final_kernel,
            [shape_of(own_block, BF16), shape_of((3, BLOCK), F32)],
            [],
            place,
            [*arrived, gains_one, hidden_grad, inward_flipped],
        )
    )


def solution(mesh):
    fine = Mesh(mesh.devices.reshape(SLABS, 2, 2, -1, 2), ("x", "yh", "yl", "z", "core"))
    atom, group = ("yl", "z", "core"), ("x", "yh")
    in_specs = (
        P(atom, None),
        P(None, atom),
        P(atom),
        P(None, group),
        P(),
        P(),
        P(),
        P(atom, None),
    )
    out_specs = (P(atom + group, None), P(None, atom + group))
    return jax.shard_map(
        per_device, mesh=fine, in_specs=in_specs, out_specs=out_specs, check_vma=False
    )
```

```python
import functools
import math

import jax
import jax.numpy as jnp
from jax import lax
from jax.experimental import pallas as pl
from jax.experimental.pallas import tpu as pltpu
from jax.sharding import Mesh
from jax.sharding import PartitionSpec as P

BOX_LENGTH = 100.0
GAUSSIAN_SIGMAS = (200.0, 100.0)
REACH = 8
SPAN = 2 * REACH + 1
CLASSES = (SPAN**3 + 1) // 2
SLABS = 4
SLAB = 640
STRIDE = -(-CLASSES // SLABS)
LAST_FAR = (2, 3, 1)
LEAP = REACH * SPAN
FIRST_ROWS = ((0, 64), (64, 144))
COUNT_PIECE = 30
COUNT_BASE = 8
COUNT_ROWS = (16, 24, 32)
TABLE = 2 * SLAB
BLOCK = 256
CHANNELS = 128
ROWS = 40
PIECES = 32
VMEM_LIMIT = 14 * 1024 * 1024
BF16 = jnp.bfloat16
F32 = jnp.float32

COS_SERIES = (
    0.999999660315462,
    -19.739032161520388,
    64.93001235415629,
    -85.28515888817482,
    58.84788533073816,
    -21.15810679384873,
)
SIN_SERIES = (
    6.283183359037432,
    -41.341456424111435,
    81.59687947501621,
    -76.58597187733577,
    41.22756686823296,
    -12.302134397179453,
)


def class_vectors(first_class, shape, axis):
    label = (lax.broadcasted_iota(jnp.int32, shape, axis) + first_class).astype(F32)
    square = SPAN * SPAN
    first = jnp.floor((label + (square // 2 + 0.5)) * (1.0 / square))
    rest = label - square * first
    second = jnp.floor((rest + (REACH + 0.5)) * (1.0 / SPAN))
    return first, second, rest - SPAN * second


def matmul(left, right, left_dim, right_dim):
    return lax.dot_general(
        left, right, (((left_dim,), (right_dim,)), ((), ())), preferred_element_type=F32
    )


def flip(matrix):
    return jnp.transpose(matrix.astype(F32)).astype(BF16)


def gain_columns(multiplier, labels):
    species_count, channels = multiplier.shape
    padding = jnp.zeros((8 - species_count, channels), F32)
    columns = jnp.transpose(jnp.concatenate([multiplier, padding], axis=0))
    result = jnp.zeros((channels, labels.shape[1]), F32)
    for species in range(species_count):
        result = jnp.where(labels == species, columns[:, species : species + 1], result)
    return result


def series(coefficients, square):
    result = coefficients[-1] * square + coefficients[-2]
    for coefficient in coefficients[-3::-1]:
        result = result * square + coefficient
    return result


def cosine_and_sine(turns):
    turns = turns - jnp.floor(turns + 0.5)
    square = turns * turns
    return series(COS_SERIES, square), turns * series(SIN_SERIES, square)


def write_half(half, table_ref, values_ref, pieces_ref, total_ref):
    total_ref[...] = matmul(table_ref[half_rows(half), :], values_ref[...], 1, 1)
    spare = ROWS - COUNT_ROWS[0]
    total_ref[SLAB - spare :, :CHANNELS] = jnp.zeros((spare, CHANNELS), F32)
    for index in range(PIECES):
        row, side = index // 2, index % 2
        pieces_ref[index] = total_ref[
            row * ROWS : (row + 1) * ROWS, side * CHANNELS : (side + 1) * CHANNELS
        ].astype(BF16)


def keep_kernel(place, table_ref, values_ref, keep_ref, total_ref):
    write_half(place[2], table_ref, values_ref, keep_ref, total_ref)


def weigh_pieces(pieces_ref, weights_ref, first, total_ref):
    for index in range(PIECES):
        row, side = index // 2, index % 2
        rows = slice(row * ROWS, (row + 1) * ROWS)
        total_ref[rows, side * CHANNELS : (side + 1) * CHANNELS] = (
            pieces_ref[index].astype(F32) * weights_ref[(first + side) % 2, rows]
        )


def half_rows(half):
    return pl.ds(pl.multiple_of(half * SLAB, SLAB), SLAB)


def slot(index):
    return slice(index * BLOCK, (index + 1) * BLOCK)


def tables_kernel(
    place,
    coordinates_hbm,
    labels_hbm,
    features_hbm,
    upstream_hbm,
    inward_hbm,
    outward_hbm,
    multiplier_hbm,
    table_ref,
    keep_ref,
    send_ref,
    coordinates_ref,
    labels_ref,
    features_ref,
    upstream_ref,
    inward_ref,
    outward_ref,
    multiplier_ref,
    total_ref,
    cosine_ref,
    sine_ref,
    second_ref,
    arrivals,
):
    copies = [
        pltpu.make_async_copy(source, target, arrivals.at[index])
        for index, (source, target) in enumerate(
            (
                (coordinates_hbm, coordinates_ref),
                (labels_hbm, labels_ref),
                (features_hbm.at[:, place[1]], features_ref),
                (upstream_hbm.at[:, place[1]], upstream_ref),
                (inward_hbm, inward_ref),
                (outward_hbm, outward_ref),
                (multiplier_hbm, multiplier_ref),
            )
        )
    ]
    for copy in copies:
        copy.start()
    blocks = [lax.rem(place[0] + index, SLABS) for index in range(SLABS)]
    sides = [
        pl.ds(pl.multiple_of((2 * block + place[1]) * BLOCK + side * CHANNELS, CHANNELS), CHANNELS)
        for block in blocks
        for side in range(BLOCK // CHANNELS)
    ]
    first_vectors = [
        class_vectors(place[0] * STRIDE + start, (stop - start, CHANNELS), 0)
        for start, stop in FIRST_ROWS
    ]
    for start in range(0, SLAB - LEAP, LEAP):
        stop = min(start + LEAP, SLAB - LEAP)
        vectors = class_vectors(place[0] * STRIDE + start, (stop - start, CHANNELS), 0)
        second_ref[start:stop] = vectors[1]
    copies[0].wait()
    for index, side in enumerate(sides):
        columns = slice(index * CHANNELS, (index + 1) * CHANNELS)
        where = [coordinates_ref[axis : axis + 1, side] for axis in range(3)]
        for (start, stop), vectors in zip(FIRST_ROWS, first_vectors):
            turns = vectors[0] * where[0] + vectors[1] * where[1] + vectors[2] * where[2]
            cosine, sine = cosine_and_sine(turns)
            cosine_ref[start:stop, columns] = cosine
            sine_ref[start:stop, columns] = sine
            table_ref[start:stop, columns] = cosine.astype(BF16)
            table_ref[SLAB + start : SLAB + stop, columns] = sine.astype(BF16)
        plain = cosine_and_sine(REACH * where[1])
        carried = cosine_and_sine(where[0] - (REACH + 1) * where[1])
        for start in range(FIRST_ROWS[-1][1], SLAB, 80):
            stop = min(start + 80, SLAB)
            before = slice(start - LEAP, stop - LEAP)
            carry = second_ref[before] > 0.5
            turn_cosine = jnp.where(carry, carried[0], plain[0])
            turn_sine = jnp.where(carry, carried[1], plain[1])
            old_cosine, old_sine = cosine_ref[before, columns], sine_ref[before, columns]
            cosine = old_cosine * turn_cosine - old_sine * turn_sine
            sine = old_sine * turn_cosine + old_cosine * turn_sine
            cosine_ref[start:stop, columns] = cosine
            sine_ref[start:stop, columns] = sine
            table_ref[start:stop, columns] = cosine.astype(BF16)
            table_ref[SLAB + start : SLAB + stop, columns] = sine.astype(BF16)
    for copy in copies[1:]:
        copy.wait()
    atoms = (SLABS * BLOCK, CHANNELS)
    charges = matmul(flip(inward_ref[0]), features_ref[...].reshape(atoms), 1, 1)
    grad_pot = matmul(outward_ref[1], upstream_ref[...].reshape(atoms), 1, 1).astype(BF16)
    for block in range(SLABS):
        labels = labels_ref[:, pl.ds(pl.multiple_of((2 * block + place[1]) * BLOCK, BLOCK), BLOCK)]
        gains = gain_columns(multiplier_ref[:, 0, :], labels)
        target = lax.rem(block - place[0] + SLABS, SLABS)
        columns = pl.ds(pl.multiple_of(target * BLOCK, BLOCK), BLOCK)
        table_ref[TABLE : TABLE + CHANNELS, columns] = (charges[:, slot(block)] * gains).astype(BF16)
        table_ref[TABLE + CHANNELS :, columns] = grad_pot[:, slot(block)]
    values_ref = table_ref.at[TABLE:]
    write_half(1 - place[2], table_ref, values_ref, send_ref, total_ref)
    write_half(place[2], table_ref, values_ref, keep_ref, total_ref)


def counts_kernel(copies, place, momenta_ref, counts_ref):
    momenta = momenta_ref[...].astype(F32)
    label = jnp.abs(
        momenta[0:1] * float(SPAN * SPAN) + momenta[1:2] * float(SPAN) + momenta[2:3]
    ) - (place[0] * STRIDE).astype(F32)
    column = jnp.transpose(jnp.broadcast_to(label, (8, label.shape[1])))[:, 0:1]
    column = jnp.broadcast_to(column, (column.shape[0], CHANNELS))
    lane = lax.broadcasted_iota(jnp.int32, column.shape, 1).astype(F32)
    counts_ref[...] = jnp.zeros(counts_ref.shape, BF16)
    rows = []
    for start in range(0, SLAB, CHANNELS):
        here = (column == lane + float(start)) & (lane < float(STRIDE - start))
        rows.append(jnp.sum(jnp.where(here, 1.0, 0.0), axis=0, keepdims=True))
    rows.append(jnp.zeros((8 - len(rows), CHANNELS), F32))
    rest = jnp.concatenate(rows, axis=0)
    digits = [jnp.zeros((COUNT_ROWS[0], CHANNELS), F32)]
    for _ in COUNT_ROWS[1:]:
        higher = jnp.floor(rest * (1.0 / COUNT_BASE))
        digits.append((rest - COUNT_BASE * higher) * (1.0 / copies))
        rest = higher
    digits.append(rest * (1.0 / copies))
    counts_ref[COUNT_PIECE] = jnp.concatenate(digits, axis=0).astype(BF16)


def write_fields(total_ref, fields_ref):
    fields_ref[:, :CHANNELS] = total_ref[:, CHANNELS:].astype(BF16)
    fields_ref[:, CHANNELS:] = total_ref[:, :CHANNELS].astype(BF16)


def first_potential_kernel(
    prefactor,
    place,
    mine_ref,
    table_ref,
    weights_ref,
    fields_hbm,
    potential_ref,
    total_ref,
    fields_ref,
    leaves,
):
    digits = mine_ref[COUNT_PIECE].astype(F32)
    counts = sum(digits[row : row + 8] * COUNT_BASE**power for power, row in enumerate(COUNT_ROWS))
    counts = jnp.transpose(counts)
    for index in range(SLAB // CHANNELS):
        start = index * CHANNELS
        count = counts[:, index : index + 1]
        vectors = class_vectors(place[0] * STRIDE + start, (CHANNELS, CHANNELS), 0)
        norm = vectors[0] * vectors[0] + vectors[1] * vectors[1] + vectors[2] * vectors[2]
        for block, spread in enumerate(GAUSSIAN_SIGMAS):
            weights_ref[block, start : start + CHANNELS, :] = count * (
                prefactor * jnp.exp(norm * (-1.0 / spread))
            )
    weigh_pieces(mine_ref, weights_ref, 0, total_ref)
    write_fields(total_ref, fields_ref)
    leaving = pltpu.make_async_copy(fields_ref, fields_hbm, leaves)
    leaving.start()
    flipped = jnp.transpose(total_ref[...]).astype(BF16)
    potential_ref[...] = matmul(flipped, table_ref[half_rows(place[2]), :], 1, 0)
    leaving.wait()


def potential_kernel(
    place, weights_ref, other_ref, table_ref, before_ref, fields_ref, flipped_ref, p2, p1, p3, total_ref
):
    weigh_pieces(other_ref, weights_ref, 0, total_ref)
    write_fields(total_ref, fields_ref)
    flipped_ref[...] = jnp.transpose(total_ref[...]).astype(BF16)
    for index, target in ((2, p2), (1, p1), (3, p3)):
        rest = matmul(flipped_ref[...], table_ref[half_rows(1 - place[2]), slot(index)], 1, 0)
        target[...] = (before_ref[:, slot(index)] + rest).astype(BF16)


def own_potential_kernel(place, table_ref, before_ref, flipped_ref, p0):
    rest = matmul(flipped_ref[...], table_ref[half_rows(1 - place[2]), slot(0)], 1, 0)
    p0[...] = (before_ref[:, slot(0)] + rest).astype(BF16)


def own_atoms_kernel(
    place,
    labels_ref,
    features_ref,
    upstream_ref,
    inward_ref,
    multiplier_ref,
    own_features_ref,
    own_upstream_ref,
    gains_one_ref,
    gains_two_ref,
    flipped_ref,
):
    own_features_ref[...] = features_ref[...]
    own_upstream_ref[...] = upstream_ref[...]
    gains_one_ref[...] = jnp.transpose(gain_columns(multiplier_ref[:, 0, :], labels_ref[...]))
    gains_two_ref[...] = gain_columns(multiplier_ref[:, 1, :], labels_ref[...])
    for block in range(2):
        flipped_ref[block] = flip(inward_ref[block])


def middle_kernel(
    place,
    q0,
    q1,
    q2,
    q3,
    features_ref,
    upstream_ref,
    gains_ref,
    flipped_ref,
    outward_ref,
    values_ref,
    hidden_grad_ref,
):
    total = (q0[...].astype(F32) + q1[...].astype(F32)) + (q2[...].astype(F32) + q3[...].astype(F32))
    grad_charge = total[CHANNELS:]
    scaled = jnp.transpose(grad_charge * gains_ref[...]).astype(BF16)
    hidden_grad = (
        upstream_ref[...].astype(F32) + matmul(scaled, flipped_ref[1], 1, 0)
    ).astype(BF16)
    hidden_grad_ref[...] = hidden_grad
    values_ref[CHANNELS:] = matmul(outward_ref[0], hidden_grad, 1, 1).astype(BF16)
    potential = jnp.transpose(total[:CHANNELS]).astype(BF16)
    hidden = (features_ref[...].astype(F32) + matmul(potential, outward_ref[0], 1, 0)).astype(BF16)
    values_ref[:CHANNELS] = (matmul(flipped_ref[1], hidden, 1, 1) * gains_ref[...]).astype(BF16)


def second_kernel(place, table_ref, v0, v1, v2, v3, values_ref, send_ref, total_ref):
    for index, source in zip((0, *LAST_FAR), (v0, v1, v2, v3)):
        values_ref[:, slot(index)] = source[...]
    write_half(1 - place[2], table_ref, values_ref, send_ref, total_ref)


def half_theta(half, table_ref, columns, along):
    sign = (2 * half - 1).astype(F32)
    return (sign * table_ref[half_rows(1 - half), columns].astype(F32)) * along


def write_pairs(total_ref, pairs_ref):
    pairs_ref[:, :CHANNELS] = total_ref[:, CHANNELS:].astype(BF16)
    pairs_ref[:, CHANNELS : 2 * CHANNELS] = total_ref[:, :CHANNELS].astype(BF16)


def first_gradient_kernel(
    place,
    weights_ref,
    mine_ref,
    table_ref,
    fields_hbm,
    second_hbm,
    values_ref,
    theta_ref,
    charge_ref,
    total_ref,
    pairs_ref,
    fields_ref,
    arrivals,
):
    copies = [
        pltpu.make_async_copy(fields_hbm, fields_ref, arrivals.at[0]),
        pltpu.make_async_copy(second_hbm, values_ref.at[BLOCK:], arrivals.at[1]),
    ]
    for copy in copies:
        copy.start()
    weigh_pieces(mine_ref, weights_ref, 1, total_ref)
    write_pairs(total_ref, pairs_ref)
    flipped = jnp.transpose(total_ref[:, CHANNELS:]).astype(BF16)
    charge_ref[...] = matmul(flipped, table_ref[half_rows(place[2]), :], 1, 0)
    values_ref[:BLOCK] = table_ref[TABLE:]
    for index in range(SLABS):
        columns = slot(index)
        along = matmul(pairs_ref[...], table_ref[TABLE:, columns], 1, 0)
        theta_ref[:, columns] = half_theta(place[2], table_ref, columns, along)
    for copy in copies:
        copy.wait()
    for index in range(SLABS):
        columns = slot(index)
        along = matmul(fields_ref[...], values_ref[BLOCK:, columns], 1, 0)
        theta_ref[:, columns] += half_theta(place[2], table_ref, columns, along)


def finish_gradient(
    index, place, table_ref, pairs_ref, flipped_ref, values_ref, theta_ref, charge_ref, directions, target
):
    columns = slot(index)
    pairs = pairs_ref[...]
    theta = theta_ref[:, columns] + half_theta(
        1 - place[2], table_ref, columns, matmul(pairs, values_ref[:, columns], 1, 0)
    )
    charge = matmul(flipped_ref[...], table_ref[half_rows(1 - place[2]), columns], 1, 0)
    target[:CHANNELS] = (charge + charge_ref[:, columns]).astype(BF16)
    for side in range(BLOCK // CHANNELS):
        part = slice(side * CHANNELS, (side + 1) * CHANNELS)
        sums = [
            jnp.sum(direction * theta[:, part], axis=0, keepdims=True) for direction in directions
        ]
        position = jnp.concatenate(sums + [jnp.zeros((13, CHANNELS), F32)], axis=0)
        target[CHANNELS:, part] = (position * (2.0 * math.pi / BOX_LENGTH)).astype(BF16)


def gradient_kernel(
    place,
    weights_ref,
    other_ref,
    table_ref,
    fields_ref,
    values_ref,
    theta_ref,
    charge_ref,
    pairs_ref,
    flipped_ref,
    o2,
    o1,
    o3,
    total_ref,
):
    weigh_pieces(other_ref, weights_ref, 1, total_ref)
    write_pairs(total_ref, pairs_ref)
    pairs_ref[:, 2 * CHANNELS :] = fields_ref[...]
    flipped_ref[...] = jnp.transpose(total_ref[:, CHANNELS:]).astype(BF16)
    directions = class_vectors(place[0] * STRIDE, (SLAB, CHANNELS), 0)
    rest = (place, table_ref, pairs_ref, flipped_ref, values_ref, theta_ref, charge_ref, directions)
    for index, target in ((2, o2), (1, o1), (3, o3)):
        finish_gradient(index, *rest, target)


def own_gradient_kernel(
    place, table_ref, pairs_ref, flipped_ref, values_ref, theta_ref, charge_ref, o0
):
    rest = (place, table_ref, pairs_ref, flipped_ref, values_ref, theta_ref, charge_ref)
    directions = class_vectors(place[0] * STRIDE, (SLAB, CHANNELS), 0)
    finish_gradient(0, *rest, directions, o0)


def sum_kernel(place, parts_ref, spread_ref):
    total = parts_ref[0].astype(F32)
    for index in range(1, PIECES):
        total += parts_ref[index].astype(F32)
    total = total.astype(BF16)
    for index in range(PIECES):
        spread_ref[index] = total


def final_kernel(
    place, q0, q1, q2, q3, gains_ref, hidden_grad_ref, flipped_ref, features_ref, positions_ref
):
    total = (q0[...].astype(F32) + q1[...].astype(F32)) + (q2[...].astype(F32) + q3[...].astype(F32))
    scaled = (jnp.transpose(total[:CHANNELS]) * gains_ref[...]).astype(BF16)
    features_ref[...] = (
        hidden_grad_ref[...].astype(F32) + matmul(scaled, flipped_ref[0], 1, 0)
    ).astype(BF16)
    positions_ref[...] = total[CHANNELS : CHANNELS + 3]


def shape_of(shape, dtype):
    return jax.ShapeDtypeStruct(shape, dtype)


def far(value):
    return pltpu.with_memory_space_constraint(value, pltpu.HBM)


def near(value):
    return pltpu.with_memory_space_constraint(value, pltpu.VMEM)


def whole(shape):
    return pl.BlockSpec(shape, lambda step, place: (0,) * len(shape))


def compiler(micros):
    return dict(
        compiler_params=pltpu.CompilerParams(vmem_limit_bytes=VMEM_LIMIT),
        cost_estimate=pl.CostEstimate(
            flops=int(micros * 10**9), bytes_accessed=int(micros * 10**6), transcendentals=0
        ),
    )


def call(kernel, in_specs, outs, out_specs, operands, micros=2):
    return pl.pallas_call(
        kernel,
        grid_spec=pltpu.PrefetchScalarGridSpec(
            num_scalar_prefetch=1, grid=(1,), in_specs=in_specs, out_specs=out_specs
        ),
        out_shape=outs,
        **compiler(micros),
    )(*operands)


def call_whole(kernel, outs, scratch, place, operands, spaces=None, out_spaces=None, micros=2):
    spaces = spaces or [pltpu.VMEM] * len(operands)
    out_spaces = out_spaces or [pltpu.VMEM] * len(outs)
    return pl.pallas_call(
        kernel,
        in_specs=[pl.BlockSpec(memory_space=pltpu.SMEM)]
        + [pl.BlockSpec(memory_space=space) for space in spaces],
        out_specs=[pl.BlockSpec(memory_space=space) for space in out_spaces],
        out_shape=outs,
        scratch_shapes=scratch,
        **compiler(micros),
    )(place, *operands)


ATOM_REST = ("yh", "yl", "z")


def shifted(value, shift):
    return lax.ppermute(value, "x", [(i, (i + shift) % SLABS) for i in range(SLABS)])


def spread_out(send, own, order):
    return [own] + [send(shift) for shift in order]


def swapped(value):
    return lax.ppermute(value, "core", [(0, 1), (1, 0)])


def add_halves(keep, send, *more):
    total = keep.astype(F32) + swapped(send).astype(F32)
    for value in more:
        total = total + value.astype(F32)
    return total.astype(BF16)


def sum_fields(place, part):
    parts = lax.all_to_all(part, ATOM_REST, 0, 0, tiled=True)
    if place is None:
        total = jnp.sum(parts.astype(F32), axis=0).astype(BF16)
        spread = jnp.broadcast_to(total[None], parts.shape)
    else:
        (spread,) = call_whole(
            sum_kernel, [pltpu.VMEM(parts.shape, BF16)], [], place, [near(parts)], micros=1
        )
    mine = lax.all_to_all(spread, ATOM_REST, 0, 0, tiled=True)
    return mine, swapped(mine)


def per_device(
    atomic_descriptors,
    unit_cell_coordinates,
    element_labels,
    lattice_momenta,
    feature_to_latent_matrix,
    latent_to_feature_matrix,
    element_latent_multiplier,
    upstream_gradient,
):
    place = jnp.stack(
        [lax.axis_index("x"), lax.axis_index("yh"), lax.axis_index("core")]
    ).astype(jnp.int32)
    prefactor = 1.0 / math.sqrt(
        atomic_descriptors.shape[0]
        * lattice_momenta.shape[1]
        * lax.axis_size(("x", "yh", "yl", "z", "core"))
    )
    labels = element_labels[None, :]
    multiplier = jnp.swapaxes(element_latent_multiplier, 0, 1)
    lengths = {axis: lax.axis_size(axis) for axis in ("x", "yl", "z")}
    copies = lengths["yl"] * lengths["z"] // SLABS
    pairs = []
    for yl in range(lengths["yl"]):
        for z in range(lengths["z"]):
            for x in range(SLABS):
                place_of = lambda x: (x * lengths["yl"] + yl) * lengths["z"] + z
                pairs.append((place_of((x + 2 * (z % 2) + yl) % SLABS), place_of(x)))
    fetched = lax.ppermute(lattice_momenta, ("x", "yl", "z"), pairs)

    matrices = whole((2, CHANNELS, CHANNELS))
    gains_spec = whole(multiplier.shape)
    pieces_shape = shape_of((PIECES, ROWS, CHANNELS), BF16)
    values_block = whole((BLOCK, BLOCK))
    values_shape = shape_of((BLOCK, BLOCK), BF16)
    atoms_here = SLABS * BLOCK

    blocked = (SLABS, 2, BLOCK, CHANNELS)
    operands = [
        unit_cell_coordinates,
        labels,
        atomic_descriptors.reshape(blocked),
        upstream_gradient.reshape(blocked),
        feature_to_latent_matrix,
        latent_to_feature_matrix,
        multiplier,
    ]
    local = [shape_of(value.shape, value.dtype) for value in operands]
    local[2] = local[3] = shape_of((SLABS, BLOCK, CHANNELS), BF16)
    table, keep, send = call_whole(
        tables_kernel,
        (
            pltpu.VMEM((TABLE + BLOCK, atoms_here), BF16),
            pieces_shape,
            pieces_shape,
        ),
        [pltpu.VMEM(value.shape, value.dtype) for value in local]
        + [
            pltpu.VMEM((SLAB, BLOCK), F32),
            pltpu.VMEM((SLAB, atoms_here), F32),
            pltpu.VMEM((SLAB, atoms_here), F32),
            pltpu.VMEM((SLAB - LEAP, CHANNELS), F32),
            pltpu.SemaphoreType.DMA((len(operands),)),
        ],
        place,
        [far(value) for value in operands],
        spaces=[pltpu.HBM] * len(operands),
        micros=7,
    )
    (counts,) = call_whole(
        functools.partial(counts_kernel, float(copies)), [pieces_shape], [], place, [fetched]
    )
    part = add_halves(keep, send, counts)
    mine, other = sum_fields(None, part)
    half = (SLAB, BLOCK)
    weights, fields_mine, before = call_whole(
        functools.partial(first_potential_kernel, prefactor),
        [
            shape_of((2, SLAB, CHANNELS), F32),
            pltpu.HBM(half, BF16),
            shape_of((BLOCK, atoms_here), F32),
        ],
        [pltpu.VMEM(half, F32), pltpu.VMEM(half, BF16), pltpu.SemaphoreType.DMA],
        place,
        [mine, near(table)],
        out_spaces=[pltpu.VMEM, pltpu.HBM, pltpu.VMEM],
    )
    fields_other, flipped, p2, p1, p3 = call_whole(
        potential_kernel,
        [shape_of(half, BF16), shape_of((BLOCK, SLAB), BF16)] + [values_shape] * 3,
        [pltpu.VMEM(half, F32)],
        place,
        [weights, other, near(table), before],
    )
    (p0,) = call_whole(
        own_potential_kernel,
        [values_shape],
        [],
        place,
        [near(table), before, flipped],
        micros=0.1,
    )
    own_atoms = pl.BlockSpec((BLOCK, CHANNELS), lambda step, place: (2 * place[0] + place[1], 0))
    own_labels = pl.BlockSpec((1, BLOCK), lambda step, place: (0, 2 * place[0] + place[1]))
    own_block = (BLOCK, CHANNELS)
    labels, p0 = lax.optimization_barrier((labels, p0))
    products = (p0, p1, p2, p3)
    arrived = spread_out(lambda shift: shifted(products[shift], shift), products[0], (2, 1, 3))
    own_features, own_upstream, gains_one, gains_two, inward_flipped = call(
        own_atoms_kernel,
        [own_labels, own_atoms, own_atoms, matrices, gains_spec],
        (
            shape_of(own_block, BF16),
            shape_of(own_block, BF16),
            shape_of(own_block, F32),
            shape_of((CHANNELS, BLOCK), F32),
            shape_of((2, CHANNELS, CHANNELS), BF16),
        ),
        (
            whole(own_block),
            whole(own_block),
            whole(own_block),
            whole((CHANNELS, BLOCK)),
            matrices,
        ),
        (
            place,
            labels,
            atomic_descriptors,
            upstream_gradient,
            feature_to_latent_matrix,
            multiplier,
        ),
        micros=0.1,
    )
    values_own, hidden_grad = call_whole(
        middle_kernel,
        [values_shape, shape_of(own_block, BF16)],
        [],
        place,
        [*arrived, own_features, own_upstream, gains_two, inward_flipped, latent_to_feature_matrix],
    )
    seconds = spread_out(lambda shift: shifted(values_own, SLABS - shift), values_own, LAST_FAR)
    values_two, send = call_whole(
        second_kernel,
        [shape_of((BLOCK, atoms_here), BF16), pieces_shape],
        [pltpu.VMEM((SLAB, BLOCK), F32)],
        place,
        [near(table), *seconds],
    )
    (keep,) = call_whole(
        keep_kernel,
        [pieces_shape],
        [pltpu.VMEM((SLAB, BLOCK), F32)],
        place,
        [near(table), near(values_two)],
        micros=0.1,
    )
    mine, other = sum_fields(place, add_halves(keep, send))
    result_shape = shape_of((CHANNELS + 16, BLOCK), BF16)
    result_spec = whole((CHANNELS + 16, BLOCK))
    values, theta, charge = call_whole(
        first_gradient_kernel,
        [
            shape_of((2 * BLOCK, atoms_here), BF16),
            shape_of((SLAB, atoms_here), F32),
            shape_of((CHANNELS, atoms_here), F32),
        ],
        [
            pltpu.VMEM(half, F32),
            pltpu.VMEM(half, BF16),
            pltpu.VMEM(half, BF16),
            pltpu.SemaphoreType.DMA((2,)),
        ],
        place,
        [weights, mine, near(table), far(fields_mine), far(values_two)],
        spaces=[pltpu.VMEM] * 3 + [pltpu.HBM] * 2,
    )
    pairs, flipped, o2, o1, o3 = call_whole(
        gradient_kernel,
        [shape_of((SLAB, 2 * BLOCK), BF16), shape_of((CHANNELS, SLAB), BF16)] + [result_shape] * 3,
        [pltpu.VMEM(half, F32)],
        place,
        [weights, other, near(table), fields_other, values, theta, charge],
    )
    (o0,) = call_whole(
        own_gradient_kernel,
        [result_shape],
        [],
        place,
        [near(table), pairs, flipped, values, theta, charge],
        micros=0.1,
    )
    results = (o0, o1, o2, o3)
    arrived = spread_out(lambda shift: shifted(results[shift], shift), results[0], (2, 1, 3))
    return tuple(
        call_whole(
            final_kernel,
            [shape_of(own_block, BF16), shape_of((3, BLOCK), F32)],
            [],
            place,
            [*arrived, gains_one, hidden_grad, inward_flipped],
        )
    )


def solution(mesh):
    fine = Mesh(mesh.devices.reshape(SLABS, 2, 2, -1, 2), ("x", "yh", "yl", "z", "core"))
    atom, group = ("yl", "z", "core"), ("x", "yh")
    in_specs = (
        P(atom, None),
        P(None, atom),
        P(atom),
        P(None, group),
        P(),
        P(),
        P(),
        P(atom, None),
    )
    out_specs = (P(atom + group, None), P(None, atom + group))
    return jax.shard_map(
        per_device, mesh=fine, in_specs=in_specs, out_specs=out_specs, check_vma=False
    )
```

```python
import functools
import math

import jax
import jax.numpy as jnp
from jax import lax
from jax.experimental import pallas as pl
from jax.experimental.pallas import tpu as pltpu
from jax.sharding import Mesh
from jax.sharding import PartitionSpec as P

BOX_LENGTH = 100.0
GAUSSIAN_SIGMAS = (200.0, 100.0)
REACH = 8
SPAN = 2 * REACH + 1
CLASSES = (SPAN**3 + 1) // 2
SLABS = 4
SLAB = 640
STRIDE = -(-CLASSES // SLABS)
LAST_FAR = (2, 3, 1)
LEAP = REACH * SPAN
FIRST_ROWS = ((0, 64), (64, 144))
COUNT_PIECE = 30
COUNT_BASE = 8
COUNT_ROWS = (16, 24, 32)
TABLE = 2 * SLAB
BLOCK = 256
CHANNELS = 128
ROWS = 40
PIECES = 32
VMEM_LIMIT = 14 * 1024 * 1024
BF16 = jnp.bfloat16
F32 = jnp.float32

COS_SERIES = (
    0.999999660315462,
    -19.739032161520388,
    64.93001235415629,
    -85.28515888817482,
    58.84788533073816,
    -21.15810679384873,
)
SIN_SERIES = (
    6.283183359037432,
    -41.341456424111435,
    81.59687947501621,
    -76.58597187733577,
    41.22756686823296,
    -12.302134397179453,
)


def class_vectors(first_class, shape, axis):
    label = (lax.broadcasted_iota(jnp.int32, shape, axis) + first_class).astype(F32)
    square = SPAN * SPAN
    first = jnp.floor((label + (square // 2 + 0.5)) * (1.0 / square))
    rest = label - square * first
    second = jnp.floor((rest + (REACH + 0.5)) * (1.0 / SPAN))
    return first, second, rest - SPAN * second


def matmul(left, right, left_dim, right_dim):
    return lax.dot_general(
        left, right, (((left_dim,), (right_dim,)), ((), ())), preferred_element_type=F32
    )


def flip(matrix):
    return jnp.transpose(matrix.astype(F32)).astype(BF16)


def gain_columns(multiplier, labels):
    species_count, channels = multiplier.shape
    padding = jnp.zeros((8 - species_count, channels), F32)
    columns = jnp.transpose(jnp.concatenate([multiplier, padding], axis=0))
    result = jnp.zeros((channels, labels.shape[1]), F32)
    for species in range(species_count):
        result = jnp.where(labels == species, columns[:, species : species + 1], result)
    return result


def series(coefficients, square):
    result = coefficients[-1] * square + coefficients[-2]
    for coefficient in coefficients[-3::-1]:
        result = result * square + coefficient
    return result


def cosine_and_sine(turns):
    turns = turns - jnp.floor(turns + 0.5)
    square = turns * turns
    return series(COS_SERIES, square), turns * series(SIN_SERIES, square)


def write_half(half, table_ref, values_ref, pieces_ref, total_ref):
    total_ref[...] = matmul(table_ref[half_rows(half), :], values_ref[...], 1, 1)
    spare = ROWS - COUNT_ROWS[0]
    total_ref[SLAB - spare :, :CHANNELS] = jnp.zeros((spare, CHANNELS), F32)
    for index in range(PIECES):
        row, side = index // 2, index % 2
        pieces_ref[index] = total_ref[
            row * ROWS : (row + 1) * ROWS, side * CHANNELS : (side + 1) * CHANNELS
        ].astype(BF16)


def keep_kernel(place, table_ref, values_ref, keep_ref, total_ref):
    write_half(place[2], table_ref, values_ref, keep_ref, total_ref)


def weigh_pieces(pieces_ref, weights_ref, first, total_ref):
    for index in range(PIECES):
        row, side = index // 2, index % 2
        rows = slice(row * ROWS, (row + 1) * ROWS)
        total_ref[rows, side * CHANNELS : (side + 1) * CHANNELS] = (
            pieces_ref[index].astype(F32) * weights_ref[(first + side) % 2, rows]
        )


def half_rows(half):
    return pl.ds(pl.multiple_of(half * SLAB, SLAB), SLAB)


def slot(index):
    return slice(index * BLOCK, (index + 1) * BLOCK)


def tables_kernel(
    place,
    coordinates_hbm,
    labels_hbm,
    features_hbm,
    upstream_hbm,
    inward_hbm,
    outward_hbm,
    multiplier_hbm,
    table_ref,
    keep_ref,
    send_ref,
    coordinates_ref,
    labels_ref,
    features_ref,
    upstream_ref,
    inward_ref,
    outward_ref,
    multiplier_ref,
    total_ref,
    cosine_ref,
    sine_ref,
    second_ref,
    arrivals,
):
    copies = [
        pltpu.make_async_copy(source, target, arrivals.at[index])
        for index, (source, target) in enumerate(
            (
                (coordinates_hbm, coordinates_ref),
                (labels_hbm, labels_ref),
                (features_hbm.at[:, place[1]], features_ref),
                (upstream_hbm.at[:, place[1]], upstream_ref),
                (inward_hbm, inward_ref),
                (outward_hbm, outward_ref),
                (multiplier_hbm, multiplier_ref),
            )
        )
    ]
    for copy in copies:
        copy.start()
    blocks = [lax.rem(place[0] + index, SLABS) for index in range(SLABS)]
    sides = [
        pl.ds(pl.multiple_of((2 * block + place[1]) * BLOCK + side * CHANNELS, CHANNELS), CHANNELS)
        for block in blocks
        for side in range(BLOCK // CHANNELS)
    ]
    first_vectors = [
        class_vectors(place[0] * STRIDE + start, (stop - start, CHANNELS), 0)
        for start, stop in FIRST_ROWS
    ]
    for start in range(0, SLAB - LEAP, LEAP):
        stop = min(start + LEAP, SLAB - LEAP)
        vectors = class_vectors(place[0] * STRIDE + start, (stop - start, CHANNELS), 0)
        second_ref[start:stop] = vectors[1]
    copies[0].wait()
    for index, side in enumerate(sides):
        columns = slice(index * CHANNELS, (index + 1) * CHANNELS)
        where = [coordinates_ref[axis : axis + 1, side] for axis in range(3)]
        for (start, stop), vectors in zip(FIRST_ROWS, first_vectors):
            turns = vectors[0] * where[0] + vectors[1] * where[1] + vectors[2] * where[2]
            cosine, sine = cosine_and_sine(turns)
            cosine_ref[start:stop, columns] = cosine
            sine_ref[start:stop, columns] = sine
            table_ref[start:stop, columns] = cosine.astype(BF16)
            table_ref[SLAB + start : SLAB + stop, columns] = sine.astype(BF16)
        plain = cosine_and_sine(REACH * where[1])
        carried = cosine_and_sine(where[0] - (REACH + 1) * where[1])
        for start in range(FIRST_ROWS[-1][1], SLAB, 80):
            stop = min(start + 80, SLAB)
            before = slice(start - LEAP, stop - LEAP)
            carry = second_ref[before] > 0.5
            turn_cosine = jnp.where(carry, carried[0], plain[0])
            turn_sine = jnp.where(carry, carried[1], plain[1])
            old_cosine, old_sine = cosine_ref[before, columns], sine_ref[before, columns]
            cosine = old_cosine * turn_cosine - old_sine * turn_sine
            sine = old_sine * turn_cosine + old_cosine * turn_sine
            cosine_ref[start:stop, columns] = cosine
            sine_ref[start:stop, columns] = sine
            table_ref[start:stop, columns] = cosine.astype(BF16)
            table_ref[SLAB + start : SLAB + stop, columns] = sine.astype(BF16)
    for copy in copies[1:]:
        copy.wait()
    atoms = (SLABS * BLOCK, CHANNELS)
    charges = matmul(flip(inward_ref[0]), features_ref[...].reshape(atoms), 1, 1)
    grad_pot = matmul(outward_ref[1], upstream_ref[...].reshape(atoms), 1, 1).astype(BF16)
    for block in range(SLABS):
        labels = labels_ref[:, pl.ds(pl.multiple_of((2 * block + place[1]) * BLOCK, BLOCK), BLOCK)]
        gains = gain_columns(multiplier_ref[:, 0, :], labels)
        target = lax.rem(block - place[0] + SLABS, SLABS)
        columns = pl.ds(pl.multiple_of(target * BLOCK, BLOCK), BLOCK)
        table_ref[TABLE : TABLE + CHANNELS, columns] = (charges[:, slot(block)] * gains).astype(BF16)
        table_ref[TABLE + CHANNELS :, columns] = grad_pot[:, slot(block)]
    values_ref = table_ref.at[TABLE:]
    write_half(1 - place[2], table_ref, values_ref, send_ref, total_ref)
    write_half(place[2], table_ref, values_ref, keep_ref, total_ref)


def counts_kernel(copies, place, momenta_ref, counts_ref):
    momenta = momenta_ref[...].astype(F32)
    label = jnp.abs(
        momenta[0:1] * float(SPAN * SPAN) + momenta[1:2] * float(SPAN) + momenta[2:3]
    ) - (place[0] * STRIDE).astype(F32)
    column = jnp.transpose(jnp.broadcast_to(label, (8, label.shape[1])))[:, 0:1]
    column = jnp.broadcast_to(column, (column.shape[0], CHANNELS))
    lane = lax.broadcasted_iota(jnp.int32, column.shape, 1).astype(F32)
    counts_ref[...] = jnp.zeros(counts_ref.shape, BF16)
    rows = []
    for start in range(0, SLAB, CHANNELS):
        here = (column == lane + float(start)) & (lane < float(STRIDE - start))
        rows.append(jnp.sum(jnp.where(here, 1.0, 0.0), axis=0, keepdims=True))
    rows.append(jnp.zeros((8 - len(rows), CHANNELS), F32))
    rest = jnp.concatenate(rows, axis=0)
    digits = [jnp.zeros((COUNT_ROWS[0], CHANNELS), F32)]
    for _ in COUNT_ROWS[1:]:
        higher = jnp.floor(rest * (1.0 / COUNT_BASE))
        digits.append((rest - COUNT_BASE * higher) * (1.0 / copies))
        rest = higher
    digits.append(rest * (1.0 / copies))
    counts_ref[COUNT_PIECE] = jnp.concatenate(digits, axis=0).astype(BF16)


def write_fields(total_ref, fields_ref):
    fields_ref[:, :CHANNELS] = total_ref[:, CHANNELS:].astype(BF16)
    fields_ref[:, CHANNELS:] = total_ref[:, :CHANNELS].astype(BF16)


def first_potential_kernel(
    prefactor,
    place,
    mine_ref,
    table_ref,
    weights_ref,
    fields_ref,
    potential_ref,
    total_ref,
):
    digits = mine_ref[COUNT_PIECE].astype(F32)
    counts = sum(digits[row : row + 8] * COUNT_BASE**power for power, row in enumerate(COUNT_ROWS))
    counts = jnp.transpose(counts)
    for index in range(SLAB // CHANNELS):
        start = index * CHANNELS
        count = counts[:, index : index + 1]
        vectors = class_vectors(place[0] * STRIDE + start, (CHANNELS, CHANNELS), 0)
        norm = vectors[0] * vectors[0] + vectors[1] * vectors[1] + vectors[2] * vectors[2]
        for block, spread in enumerate(GAUSSIAN_SIGMAS):
            weights_ref[block, start : start + CHANNELS, :] = count * (
                prefactor * jnp.exp(norm * (-1.0 / spread))
            )
    weigh_pieces(mine_ref, weights_ref, 0, total_ref)
    write_fields(total_ref, fields_ref)
    flipped = jnp.transpose(total_ref[...]).astype(BF16)
    potential_ref[...] = matmul(flipped, table_ref[half_rows(place[2]), :], 1, 0)


def potential_kernel(
    place, weights_ref, other_ref, table_ref, before_ref, fields_ref, flipped_ref, p2, p1, p3, total_ref
):
    weigh_pieces(other_ref, weights_ref, 0, total_ref)
    write_fields(total_ref, fields_ref)
    flipped_ref[...] = jnp.transpose(total_ref[...]).astype(BF16)
    for index, target in ((2, p2), (1, p1), (3, p3)):
        rest = matmul(flipped_ref[...], table_ref[half_rows(1 - place[2]), slot(index)], 1, 0)
        target[...] = (before_ref[:, slot(index)] + rest).astype(BF16)


def own_potential_kernel(
    place, table_ref, before_ref, flipped_ref, fields_ref, p0, fields_hbm, leaves
):
    leaving = pltpu.make_async_copy(fields_ref, fields_hbm, leaves)
    leaving.start()
    rest = matmul(flipped_ref[...], table_ref[half_rows(1 - place[2]), slot(0)], 1, 0)
    p0[...] = (before_ref[:, slot(0)] + rest).astype(BF16)
    leaving.wait()


def own_atoms_kernel(
    place,
    labels_ref,
    features_ref,
    upstream_ref,
    inward_ref,
    multiplier_ref,
    own_features_ref,
    own_upstream_ref,
    gains_one_ref,
    gains_two_ref,
    flipped_ref,
):
    own_features_ref[...] = features_ref[...]
    own_upstream_ref[...] = upstream_ref[...]
    gains_one_ref[...] = jnp.transpose(gain_columns(multiplier_ref[:, 0, :], labels_ref[...]))
    gains_two_ref[...] = gain_columns(multiplier_ref[:, 1, :], labels_ref[...])
    for block in range(2):
        flipped_ref[block] = flip(inward_ref[block])


def middle_kernel(
    place,
    q0,
    q1,
    q2,
    q3,
    features_ref,
    upstream_ref,
    gains_ref,
    flipped_ref,
    outward_ref,
    values_ref,
    hidden_grad_ref,
):
    total = (q0[...].astype(F32) + q1[...].astype(F32)) + (q2[...].astype(F32) + q3[...].astype(F32))
    grad_charge = total[CHANNELS:]
    scaled = jnp.transpose(grad_charge * gains_ref[...]).astype(BF16)
    hidden_grad = (
        upstream_ref[...].astype(F32) + matmul(scaled, flipped_ref[1], 1, 0)
    ).astype(BF16)
    hidden_grad_ref[...] = hidden_grad
    values_ref[CHANNELS:] = matmul(outward_ref[0], hidden_grad, 1, 1).astype(BF16)
    potential = jnp.transpose(total[:CHANNELS]).astype(BF16)
    hidden = (features_ref[...].astype(F32) + matmul(potential, outward_ref[0], 1, 0)).astype(BF16)
    values_ref[:CHANNELS] = (matmul(flipped_ref[1], hidden, 1, 1) * gains_ref[...]).astype(BF16)


def second_kernel(place, table_ref, v0, v1, v2, v3, values_ref, send_ref, total_ref):
    for index, source in zip((0, *LAST_FAR), (v0, v1, v2, v3)):
        values_ref[:, slot(index)] = source[...]
    write_half(1 - place[2], table_ref, values_ref, send_ref, total_ref)


def half_theta(half, table_ref, columns, along):
    sign = (2 * half - 1).astype(F32)
    return (sign * table_ref[half_rows(1 - half), columns].astype(F32)) * along


def write_pairs(total_ref, pairs_ref):
    pairs_ref[:, :CHANNELS] = total_ref[:, CHANNELS:].astype(BF16)
    pairs_ref[:, CHANNELS : 2 * CHANNELS] = total_ref[:, :CHANNELS].astype(BF16)


def first_gradient_kernel(
    place,
    weights_ref,
    mine_ref,
    table_ref,
    fields_hbm,
    second_hbm,
    values_ref,
    theta_ref,
    charge_ref,
    total_ref,
    pairs_ref,
    fields_ref,
    arrivals,
):
    copies = [
        pltpu.make_async_copy(fields_hbm, fields_ref, arrivals.at[0]),
        pltpu.make_async_copy(second_hbm, values_ref.at[BLOCK:], arrivals.at[1]),
    ]
    for copy in copies:
        copy.start()
    weigh_pieces(mine_ref, weights_ref, 1, total_ref)
    write_pairs(total_ref, pairs_ref)
    flipped = jnp.transpose(total_ref[:, CHANNELS:]).astype(BF16)
    charge_ref[...] = matmul(flipped, table_ref[half_rows(place[2]), :], 1, 0)
    values_ref[:BLOCK] = table_ref[TABLE:]
    for index in range(SLABS):
        columns = slot(index)
        along = matmul(pairs_ref[...], table_ref[TABLE:, columns], 1, 0)
        theta_ref[:, columns] = half_theta(place[2], table_ref, columns, along)
    for copy in copies:
        copy.wait()
    for index in range(SLABS):
        columns = slot(index)
        along = matmul(fields_ref[...], values_ref[BLOCK:, columns], 1, 0)
        theta_ref[:, columns] += half_theta(place[2], table_ref, columns, along)


def finish_gradient(
    index, place, table_ref, pairs_ref, flipped_ref, values_ref, theta_ref, charge_ref, directions, target
):
    columns = slot(index)
    pairs = pairs_ref[...]
    theta = theta_ref[:, columns] + half_theta(
        1 - place[2], table_ref, columns, matmul(pairs, values_ref[:, columns], 1, 0)
    )
    charge = matmul(flipped_ref[...], table_ref[half_rows(1 - place[2]), columns], 1, 0)
    target[:CHANNELS] = (charge + charge_ref[:, columns]).astype(BF16)
    for side in range(BLOCK // CHANNELS):
        part = slice(side * CHANNELS, (side + 1) * CHANNELS)
        sums = [
            jnp.sum(direction * theta[:, part], axis=0, keepdims=True) for direction in directions
        ]
        position = jnp.concatenate(sums + [jnp.zeros((13, CHANNELS), F32)], axis=0)
        target[CHANNELS:, part] = (position * (2.0 * math.pi / BOX_LENGTH)).astype(BF16)


def gradient_kernel(
    place,
    weights_ref,
    other_ref,
    table_ref,
    fields_ref,
    values_ref,
    theta_ref,
    charge_ref,
    pairs_ref,
    flipped_ref,
    o2,
    o1,
    o3,
    total_ref,
):
    weigh_pieces(other_ref, weights_ref, 1, total_ref)
    write_pairs(total_ref, pairs_ref)
    pairs_ref[:, 2 * CHANNELS :] = fields_ref[...]
    flipped_ref[...] = jnp.transpose(total_ref[:, CHANNELS:]).astype(BF16)
    directions = class_vectors(place[0] * STRIDE, (SLAB, CHANNELS), 0)
    rest = (place, table_ref, pairs_ref, flipped_ref, values_ref, theta_ref, charge_ref, directions)
    for index, target in ((2, o2), (1, o1), (3, o3)):
        finish_gradient(index, *rest, target)


def own_gradient_kernel(
    place, table_ref, pairs_ref, flipped_ref, values_ref, theta_ref, charge_ref, o0
):
    rest = (place, table_ref, pairs_ref, flipped_ref, values_ref, theta_ref, charge_ref)
    directions = class_vectors(place[0] * STRIDE, (SLAB, CHANNELS), 0)
    finish_gradient(0, *rest, directions, o0)


def sum_kernel(place, parts_ref, spread_ref):
    total = parts_ref[0].astype(F32)
    for index in range(1, PIECES):
        total += parts_ref[index].astype(F32)
    total = total.astype(BF16)
    for index in range(PIECES):
        spread_ref[index] = total


def final_kernel(
    place, q0, q1, q2, q3, gains_ref, hidden_grad_ref, flipped_ref, features_ref, positions_ref
):
    total = (q0[...].astype(F32) + q1[...].astype(F32)) + (q2[...].astype(F32) + q3[...].astype(F32))
    scaled = (jnp.transpose(total[:CHANNELS]) * gains_ref[...]).astype(BF16)
    features_ref[...] = (
        hidden_grad_ref[...].astype(F32) + matmul(scaled, flipped_ref[0], 1, 0)
    ).astype(BF16)
    positions_ref[...] = total[CHANNELS : CHANNELS + 3]


def shape_of(shape, dtype):
    return jax.ShapeDtypeStruct(shape, dtype)


def far(value):
    return pltpu.with_memory_space_constraint(value, pltpu.HBM)


def near(value):
    return pltpu.with_memory_space_constraint(value, pltpu.VMEM)


def whole(shape):
    return pl.BlockSpec(shape, lambda step, place: (0,) * len(shape))


def compiler(micros):
    return dict(
        compiler_params=pltpu.CompilerParams(vmem_limit_bytes=VMEM_LIMIT),
        cost_estimate=pl.CostEstimate(
            flops=int(micros * 10**9), bytes_accessed=int(micros * 10**6), transcendentals=0
        ),
    )


def call(kernel, in_specs, outs, out_specs, operands, micros=2):
    return pl.pallas_call(
        kernel,
        grid_spec=pltpu.PrefetchScalarGridSpec(
            num_scalar_prefetch=1, grid=(1,), in_specs=in_specs, out_specs=out_specs
        ),
        out_shape=outs,
        **compiler(micros),
    )(*operands)


def call_whole(kernel, outs, scratch, place, operands, spaces=None, out_spaces=None, micros=2):
    spaces = spaces or [pltpu.VMEM] * len(operands)
    out_spaces = out_spaces or [pltpu.VMEM] * len(outs)
    return pl.pallas_call(
        kernel,
        in_specs=[pl.BlockSpec(memory_space=pltpu.SMEM)]
        + [pl.BlockSpec(memory_space=space) for space in spaces],
        out_specs=[pl.BlockSpec(memory_space=space) for space in out_spaces],
        out_shape=outs,
        scratch_shapes=scratch,
        **compiler(micros),
    )(place, *operands)


ATOM_REST = ("yh", "yl", "z")


def shifted(value, shift):
    return lax.ppermute(value, "x", [(i, (i + shift) % SLABS) for i in range(SLABS)])


def spread_out(send, own, order):
    return [own] + [send(shift) for shift in order]


def swapped(value):
    return lax.ppermute(value, "core", [(0, 1), (1, 0)])


def add_halves(keep, send, *more):
    total = keep.astype(F32) + swapped(send).astype(F32)
    for value in more:
        total = total + value.astype(F32)
    return total.astype(BF16)


def sum_fields(place, part):
    parts = lax.all_to_all(part, ATOM_REST, 0, 0, tiled=True)
    if place is None:
        total = jnp.sum(parts.astype(F32), axis=0).astype(BF16)
        spread = jnp.broadcast_to(total[None], parts.shape)
    else:
        (spread,) = call_whole(
            sum_kernel, [pltpu.VMEM(parts.shape, BF16)], [], place, [near(parts)], micros=1
        )
    mine = lax.all_to_all(spread, ATOM_REST, 0, 0, tiled=True)
    return mine, swapped(mine)


def per_device(
    atomic_descriptors,
    unit_cell_coordinates,
    element_labels,
    lattice_momenta,
    feature_to_latent_matrix,
    latent_to_feature_matrix,
    element_latent_multiplier,
    upstream_gradient,
):
    place = jnp.stack(
        [lax.axis_index("x"), lax.axis_index("yh"), lax.axis_index("core")]
    ).astype(jnp.int32)
    prefactor = 1.0 / math.sqrt(
        atomic_descriptors.shape[0]
        * lattice_momenta.shape[1]
        * lax.axis_size(("x", "yh", "yl", "z", "core"))
    )
    labels = element_labels[None, :]
    multiplier = jnp.swapaxes(element_latent_multiplier, 0, 1)
    lengths = {axis: lax.axis_size(axis) for axis in ("x", "yl", "z")}
    copies = lengths["yl"] * lengths["z"] // SLABS
    pairs = []
    for yl in range(lengths["yl"]):
        for z in range(lengths["z"]):
            for x in range(SLABS):
                place_of = lambda x: (x * lengths["yl"] + yl) * lengths["z"] + z
                pairs.append((place_of((x + 2 * (z % 2) + yl) % SLABS), place_of(x)))
    fetched = lax.ppermute(lattice_momenta, ("x", "yl", "z"), pairs)

    matrices = whole((2, CHANNELS, CHANNELS))
    gains_spec = whole(multiplier.shape)
    pieces_shape = shape_of((PIECES, ROWS, CHANNELS), BF16)
    values_block = whole((BLOCK, BLOCK))
    values_shape = shape_of((BLOCK, BLOCK), BF16)
    atoms_here = SLABS * BLOCK

    blocked = (SLABS, 2, BLOCK, CHANNELS)
    operands = [
        unit_cell_coordinates,
        labels,
        atomic_descriptors.reshape(blocked),
        upstream_gradient.reshape(blocked),
        feature_to_latent_matrix,
        latent_to_feature_matrix,
        multiplier,
    ]
    local = [shape_of(value.shape, value.dtype) for value in operands]
    local[2] = local[3] = shape_of((SLABS, BLOCK, CHANNELS), BF16)
    table, keep, send = call_whole(
        tables_kernel,
        (
            pltpu.VMEM((TABLE + BLOCK, atoms_here), BF16),
            pieces_shape,
            pieces_shape,
        ),
        [pltpu.VMEM(value.shape, value.dtype) for value in local]
        + [
            pltpu.VMEM((SLAB, BLOCK), F32),
            pltpu.VMEM((SLAB, atoms_here), F32),
            pltpu.VMEM((SLAB, atoms_here), F32),
            pltpu.VMEM((SLAB - LEAP, CHANNELS), F32),
            pltpu.SemaphoreType.DMA((len(operands),)),
        ],
        place,
        [far(value) for value in operands],
        spaces=[pltpu.HBM] * len(operands),
        micros=7,
    )
    (counts,) = call_whole(
        functools.partial(counts_kernel, float(copies)), [pieces_shape], [], place, [fetched]
    )
    part = add_halves(keep, send, counts)
    mine, other = sum_fields(None, part)
    half = (SLAB, BLOCK)
    weights, fields_mine, before = call_whole(
        functools.partial(first_potential_kernel, prefactor),
        [
            shape_of((2, SLAB, CHANNELS), F32),
            shape_of(half, BF16),
            shape_of((BLOCK, atoms_here), F32),
        ],
        [pltpu.VMEM(half, F32)],
        place,
        [mine, near(table)],
    )
    fields_other, flipped, p2, p1, p3 = call_whole(
        potential_kernel,
        [shape_of(half, BF16), shape_of((BLOCK, SLAB), BF16)] + [values_shape] * 3,
        [pltpu.VMEM(half, F32)],
        place,
        [weights, other, near(table), before],
    )
    p0, fields_mine = call_whole(
        own_potential_kernel,
        [values_shape, pltpu.HBM(half, BF16)],
        [pltpu.SemaphoreType.DMA],
        place,
        [near(table), before, flipped, near(fields_mine)],
        out_spaces=[pltpu.VMEM, pltpu.HBM],
        micros=0.1,
    )
    own_atoms = pl.BlockSpec((BLOCK, CHANNELS), lambda step, place: (2 * place[0] + place[1], 0))
    own_labels = pl.BlockSpec((1, BLOCK), lambda step, place: (0, 2 * place[0] + place[1]))
    own_block = (BLOCK, CHANNELS)
    labels, p0 = lax.optimization_barrier((labels, p0))
    products = (p0, p1, p2, p3)
    arrived = spread_out(lambda shift: shifted(products[shift], shift), products[0], (2, 1, 3))
    own_features, own_upstream, gains_one, gains_two, inward_flipped = call(
        own_atoms_kernel,
        [own_labels, own_atoms, own_atoms, matrices, gains_spec],
        (
            shape_of(own_block, BF16),
            shape_of(own_block, BF16),
            shape_of(own_block, F32),
            shape_of((CHANNELS, BLOCK), F32),
            shape_of((2, CHANNELS, CHANNELS), BF16),
        ),
        (
            whole(own_block),
            whole(own_block),
            whole(own_block),
            whole((CHANNELS, BLOCK)),
            matrices,
        ),
        (
            place,
            labels,
            atomic_descriptors,
            upstream_gradient,
            feature_to_latent_matrix,
            multiplier,
        ),
        micros=0.1,
    )
    values_own, hidden_grad = call_whole(
        middle_kernel,
        [values_shape, shape_of(own_block, BF16)],
        [],
        place,
        [*arrived, own_features, own_upstream, gains_two, inward_flipped, latent_to_feature_matrix],
    )
    seconds = spread_out(lambda shift: shifted(values_own, SLABS - shift), values_own, LAST_FAR)
    values_two, send = call_whole(
        second_kernel,
        [shape_of((BLOCK, atoms_here), BF16), pieces_shape],
        [pltpu.VMEM((SLAB, BLOCK), F32)],
        place,
        [near(table), *seconds],
    )
    (keep,) = call_whole(
        keep_kernel,
        [pieces_shape],
        [pltpu.VMEM((SLAB, BLOCK), F32)],
        place,
        [near(table), near(values_two)],
        micros=0.1,
    )
    mine, other = sum_fields(place, add_halves(keep, send))
    result_shape = shape_of((CHANNELS + 16, BLOCK), BF16)
    result_spec = whole((CHANNELS + 16, BLOCK))
    values, theta, charge = call_whole(
        first_gradient_kernel,
        [
            shape_of((2 * BLOCK, atoms_here), BF16),
            shape_of((SLAB, atoms_here), F32),
            shape_of((CHANNELS, atoms_here), F32),
        ],
        [
            pltpu.VMEM(half, F32),
            pltpu.VMEM(half, BF16),
            pltpu.VMEM(half, BF16),
            pltpu.SemaphoreType.DMA((2,)),
        ],
        place,
        [weights, mine, near(table), far(fields_mine), far(values_two)],
        spaces=[pltpu.VMEM] * 3 + [pltpu.HBM] * 2,
    )
    pairs, flipped, o2, o1, o3 = call_whole(
        gradient_kernel,
        [shape_of((SLAB, 2 * BLOCK), BF16), shape_of((CHANNELS, SLAB), BF16)] + [result_shape] * 3,
        [pltpu.VMEM(half, F32)],
        place,
        [weights, other, near(table), fields_other, values, theta, charge],
    )
    (o0,) = call_whole(
        own_gradient_kernel,
        [result_shape],
        [],
        place,
        [near(table), pairs, flipped, values, theta, charge],
        micros=0.1,
    )
    results = (o0, o1, o2, o3)
    arrived = spread_out(lambda shift: shifted(results[shift], shift), results[0], (2, 1, 3))
    return tuple(
        call_whole(
            final_kernel,
            [shape_of(own_block, BF16), shape_of((3, BLOCK), F32)],
            [],
            place,
            [*arrived, gains_one, hidden_grad, inward_flipped],
        )
    )


def solution(mesh):
    fine = Mesh(mesh.devices.reshape(SLABS, 2, 2, -1, 2), ("x", "yh", "yl", "z", "core"))
    atom, group = ("yl", "z", "core"), ("x", "yh")
    in_specs = (
        P(atom, None),
        P(None, atom),
        P(atom),
        P(None, group),
        P(),
        P(),
        P(),
        P(atom, None),
    )
    out_specs = (P(atom + group, None), P(None, atom + group))
    return jax.shard_map(
        per_device, mesh=fine, in_specs=in_specs, out_specs=out_specs, check_vma=False
    )
```
